32 devices in a mesh: chan: 4 (over x, core), filt: 8 (over z, y).
Axes of the slice: x: 2, y: 2, z: 4, core: 2. Of those that a mesh axis runs over, the one named last changes fastest.
Arguments:
- inputs: bfloat16 [1, 64, 128, 1024], P(None, 'filt', None, 'chan'), may hold values from -6 to 6
- weights: bfloat16 [3, 3, 1024, 1024], P(None, None, 'filt', 'chan'), may hold values from -0.0625 to 0.0625
- cotangent: bfloat16 [1, 64, 1024, 128], P(None, 'chan', 'filt'), may hold values from -6 to 6
Outputs:
- outputs: bfloat16 [1, 64, 1024, 128], P(None, 'chan', 'filt')
- input_grad: bfloat16 [1, 64, 128, 1024], P(None, 'filt', None, 'chan')
- weight_grad: float32 [3, 3, 1024, 1024], P(None, None, 'filt', 'chan')
The draws below stay inside these ranges and needn't reach their ends.
All inputs are finite; a program needn't handle non-finite values.
Results may differ from the reference program's by a relative error of at most 0.001.
Values may be sent and summed in bfloat16 or wider, within the bound.
No kernel may reach another device: no remote copies, remote signals or barrier semaphores. Data moves between devices by JAX's collectives and lax.ppermute only.
A program may use at most 128 MiB of HBM per device.

```python
import math
import jax
import jax.numpy as jnp

CIN = 1024
COUT = 1024
BATCH = 1
HEIGHT = 64
WIDTH = 128


def block_scale(rng, dims, pieces, smallest, high):
    loudness = 1.0
    for dim, blocks in pieces:
        steps = jax.random.uniform(jax.random.fold_in(jax.random.fold_in(rng, 6), dim), (blocks,), jnp.float32, smallest / len(pieces), high / len(pieces))
        loudness = loudness * jnp.repeat(jnp.exp(steps), dims[dim] // blocks).reshape((-1,) + (1,) * (len(dims) - 1 - dim))
    return loudness


def gaussian(stream_key, shape, scale, reach, cuts=(), dtype=jnp.bfloat16):
    values = jax.random.normal(stream_key, shape, jnp.float32) * scale
    if len(cuts) > 0:
        values = block_scale(stream_key, shape, cuts, -0.22, 0.18) * values
    return jnp.clip(values, min=-reach, max=reach).astype(dtype)


def setup_inputs(seed: int = 0) -> dict:
    key_of = jax.random.split(jax.random.key(seed), 4)
    return {
        "inputs": gaussian(key_of[0], (BATCH, HEIGHT, WIDTH, CIN), 1.0, 6.0, ((1, 8), (3, 4))),
        "weights": gaussian(key_of[1], (3, 3, COUT, CIN), (9 * CIN) ** -0.5, 0.0625, ((2, 8), (3, 4))),
        "cotangent": gaussian(key_of[2], (BATCH, HEIGHT, COUT, WIDTH), 1.0, 6.0, ((1, 4), (2, 8))),
    }


def window(padded, tap_row, tap_col):
    return padded[:, tap_row:tap_row + HEIGHT, tap_col:tap_col + WIDTH, :].reshape(-1, padded.shape[3])

def reference(inputs, weights, cotangent):
    cot_last = jnp.transpose(cotangent, (0, 1, 3, 2))
    padded_in = jnp.pad(inputs, ((0, 0), (1, 1), (1, 1), (0, 0))).astype(jnp.float32)
    padded_cot = jnp.pad(cot_last, ((0, 0), (1, 1), (1, 1), (0, 0))).astype(jnp.float32)
    kernel = weights.astype(jnp.float32)
    cot_flat = cot_last.astype(jnp.float32).reshape(-1, COUT)
    summed_out = jnp.zeros((BATCH * HEIGHT * WIDTH, COUT), jnp.float32)
    summed_grad = jnp.zeros((BATCH * HEIGHT * WIDTH, CIN), jnp.float32)
    grad_taps = []
    norm_factor = 1.0 / math.sqrt(BATCH * HEIGHT * WIDTH)
    for tap_row in range(3):
        for tap_col in range(3):
            source = window(padded_in, tap_row, tap_col)
            summed_out = summed_out + jnp.dot(source, kernel[tap_row, tap_col].T, preferred_element_type=jnp.float32)
            back = window(padded_cot, 2 - tap_row, 2 - tap_col)
            summed_grad = summed_grad + jnp.dot(back, kernel[tap_row, tap_col], preferred_element_type=jnp.float32)
            grad_taps.append(jnp.dot(cot_flat.T, source, preferred_element_type=jnp.float32) * norm_factor)
    outputs = jnp.transpose(summed_out.reshape(BATCH, HEIGHT, WIDTH, COUT), (0, 1, 3, 2)).astype(jnp.bfloat16)
    input_grad = summed_grad.reshape(BATCH, HEIGHT, WIDTH, CIN).astype(jnp.bfloat16)
    weight_grad = jnp.stack(grad_taps).reshape(3, 3, COUT, CIN)
    return (outputs, input_grad, weight_grad)
```

```python
import functools
import math

import jax
import jax.numpy as jnp
from jax import lax
from jax.experimental import pallas as pl
from jax.experimental.pallas import tpu as pltpu
from jax.sharding import PartitionSpec as P

F32 = jnp.float32
BF16 = jnp.bfloat16
NT = (((1,), (1,)), ((), ()))
ANY = pl.BlockSpec(memory_space=pl.ANY)
VMEM = pl.BlockSpec(memory_space=pltpu.VMEM)
SMEM = pl.BlockSpec(memory_space=pltpu.SMEM)
PAIR = 2


def params(mib):
    return pltpu.CompilerParams(vmem_limit_bytes=mib << 20)


def cost(flops, moved):
    return pl.CostEstimate(flops=int(flops), bytes_accessed=int(moved), transcendentals=0)


def lane_shift(value, by):
    size = value.shape[1]
    lane = lax.broadcasted_iota(jnp.int32, value.shape, 1)
    keep = lane >= by if by > 0 else lane < size + by
    return jnp.where(keep, pltpu.roll(value, by % size, 1), 0.0)


def row_shift(value, by):
    size = value.shape[0]
    row = lax.broadcasted_iota(jnp.int32, value.shape, 0)
    keep = row >= by if by > 0 else row < size + by
    return jnp.where(keep, pltpu.roll(value, by % size, 0), 0.0)


def load_rows(depth, mine, parts, rows, sems):
    height = parts[0][0].shape[0]
    line, side = mine
    rows[0] = jnp.zeros(rows.shape[1:], rows.dtype)
    rows[rows.shape[0] - 1] = jnp.zeros(rows.shape[1:], rows.dtype)

    def each(act):
        for half in range(PAIR):
            of_side = lax.rem(side + half, PAIR)
            for step in range(depth):
                for way in (-1, 1) if step else (0,):
                    source = parts[half][0 if step == 0 else 2 * step - (way < 0)]
                    block = line + way * step
                    copy = pltpu.make_async_copy(
                        source,
                        rows.at[pl.ds(1 + (block * PAIR + of_side) * height, height)],
                        sems.at[half, 0 if step == 0 else 2 * step - (way < 0)],
                    )
                    pl.when(jnp.logical_and(block >= 0, block < depth))(functools.partial(act, copy))

    each(lambda copy: copy.start())
    each(lambda copy: copy.wait())


def forward_kernel(depth, chans, at, weights, *refs):
    count = 2 * depth - 1
    parts = (refs[:count], refs[count : 2 * count])
    keep, send, rows, taps, sems = refs[2 * count :]
    load_rows(depth, (at[0], at[1]), parts, rows, sems)
    filters, chans_in = weights.shape[2], weights.shape[3]
    for tap_row in range(3):
        for tap_col in range(3):
            taps[pl.ds(tap_col * filters, filters), pl.ds(tap_row * chans_in, chans_in)] = weights[tap_row, tap_col]
    width = rows.shape[1]
    block = keep.shape[1]
    group = min(4, block)
    per_block = block // group
    far, core = at[2], at[3]

    def run(target, of_core, step):
        which, group_at = step // per_block, step % per_block
        first = ((lax.rem(far + which, chans // 2)) * 2 + of_core) * block + group_at * group
        window = jnp.concatenate(
            [rows[pl.ds(first + i, group)].reshape(group * width, chans_in) for i in range(3)], axis=1
        )
        product = lax.dot_general(taps[...], window, NT, preferred_element_type=F32)
        for row in range(group):
            part = [
                product[j * filters : (j + 1) * filters, row * width : (row + 1) * width] for j in range(3)
            ]
            target[which, group_at * group + row] = part[1] + lane_shift(part[0], 1) + lane_shift(part[2], -1)

    @pl.loop(0, (chans // 2) * per_block)
    def _(step):
        run(send, 1 - core, step)
        run(keep, core, step)


def forward_partial(depth, chans, at, weights, own, other):
    height, width, chans_in = own[0].shape
    filters = weights.shape[2]
    rows = height * depth * PAIR
    half = jax.ShapeDtypeStruct((chans // 2, rows // chans, filters, width), F32)
    return pl.pallas_call(
        functools.partial(forward_kernel, depth, chans),
        out_shape=(half, half),
        in_specs=[SMEM, VMEM] + [ANY] * (len(own) + len(other)),
        out_specs=(VMEM, VMEM),
        scratch_shapes=[
            pltpu.VMEM((rows + 2, width, chans_in), BF16),
            pltpu.VMEM((3 * filters, 3 * chans_in), BF16),
            pltpu.SemaphoreType.DMA((PAIR, len(own))),
        ],
        compiler_params=params(40),
        cost_estimate=cost(18 * rows * width * chans_in * filters, 4 * rows * width * filters + 2 * rows * width * chans_in),
        name="forward",
    )(at, weights, *own, *other)


def weight_kernel(depth, scale, at, cot, *refs):
    count = 2 * depth - 1
    parts = (refs[:count], refs[count : 2 * count])
    out, rows, moved, sems = refs[2 * count :]
    load_rows(depth, (at[0], at[1]), parts, rows, sems)
    filters, width = cot.shape[1], cot.shape[2]
    total = cot.shape[0]
    chans_in = rows.shape[2]
    chunk = min(8, total)
    out[...] = jnp.zeros(out.shape, F32)

    @pl.loop(0, total // chunk)
    def _(step):
        first = step * chunk
        for row in range(chunk):
            value = cot[first + row]
            wide = value.astype(F32)
            lanes = pl.ds(row * width, width)
            moved[0:filters, lanes] = lane_shift(wide, -1).astype(BF16)
            moved[filters : 2 * filters, lanes] = value
            moved[2 * filters :, lanes] = lane_shift(wide, 1).astype(BF16)
        for tap_row in range(3):
            window = rows[pl.ds(first + tap_row, chunk)].reshape(chunk * width, chans_in)
            out[tap_row] += jnp.dot(moved[...], window, preferred_element_type=F32)

    out[...] = out[...] * scale


def weight_gradient(depth, at, scale, cot, own, other):
    height, width, chans_in = own[0].shape
    rows, filters = cot.shape[0], cot.shape[1]
    return pl.pallas_call(
        functools.partial(weight_kernel, depth, scale),
        out_shape=jax.ShapeDtypeStruct((3, 3 * filters, chans_in), F32),
        in_specs=[SMEM, VMEM] + [ANY] * (len(own) + len(other)),
        out_specs=VMEM,
        scratch_shapes=[
            pltpu.VMEM((rows + 2, width, chans_in), BF16),
            pltpu.VMEM((3 * filters, min(8, rows) * width), BF16),
            pltpu.SemaphoreType.DMA((PAIR, len(own))),
        ],
        compiler_params=params(40),
        cost_estimate=cost(18 * rows * width * chans_in * filters, 2 * rows * width * (filters + chans_in) + 36 * filters * chans_in),
        name="weight_gradient",
    )(at, cot, *own, *other)


def turn_kernel(pieces, out):
    rows = pieces.shape[2]

    @pl.loop(0, rows)
    def _(row):
        value = jnp.concatenate([pieces[c, 0, row].astype(F32) for c in range(pieces.shape[0])], axis=0)
        turned = value.T
        out[0, 0, row] = row_shift(turned, -1).astype(BF16)
        out[0, 1, row] = turned.astype(BF16)
        out[0, 2, row] = row_shift(turned, 1).astype(BF16)


def turned(pieces):
    chans, depth, rows, part, width = pieces.shape
    return pl.pallas_call(
        turn_kernel,
        grid=(depth,),
        out_shape=jax.ShapeDtypeStruct((depth, 3, rows, width, chans * part), BF16),
        in_specs=[pl.BlockSpec((chans, 1, rows, part, width), lambda d: (0, d, 0, 0, 0))],
        out_specs=pl.BlockSpec((1, 3, rows, width, chans * part), lambda d: (d, 0, 0, 0, 0)),
        compiler_params=params(32),
        cost_estimate=cost(1e9, 8 * depth * rows * width * chans * part),
        name="turned",
    )(pieces)


def input_kernel(depth, steps, final, at, cot, *refs):
    count = len(steps)
    kernels = refs[:count]
    refs = refs[count:]
    before = None
    if steps[0] != 0:
        before, refs = refs[0], refs[1:]
    outs, refs = refs[: 2 if final else 1], refs[2 if final else 1 :]
    total, source, taps, sems = refs
    line, side = at[0], at[1]
    rows, width, chans_in = total.shape
    filters = taps.shape[2]
    wanted = [jnp.logical_and(line + step >= 0, line + step < depth) for step in steps]

    def copies(n):
        return (
            pltpu.make_async_copy(cot.at[(-steps[n]) % depth], source.at[n], sems.at[n, 0]),
            pltpu.make_async_copy(kernels[n], taps.at[n], sems.at[n, 1]),
        )

    for n in range(count):

        @pl.when(wanted[n])
        def _():
            for copy in copies(n):
                copy.start()

    if before is None:
        total[...] = jnp.zeros(total.shape, F32)
    else:
        total[...] = before[...]
    chunk = min(8, rows)
    for n in range(count):

        @pl.when(wanted[n])
        def _():
            for copy in copies(n):
                copy.wait()

            @pl.loop(0, rows // chunk)
            def _(step):
                first = step * chunk

                def window(i, j):
                    return source[n, j, pl.ds(first + 2 - i, chunk)].reshape(chunk * width, filters)

                here = pl.ds(first, chunk)
                if filters % 128 == 0:
                    value = jnp.concatenate([window(i, j) for i in range(3) for j in range(3)], axis=1)
                    product = jnp.dot(
                        value, taps[n].reshape(9 * filters, chans_in), preferred_element_type=F32
                    )
                else:
                    product = sum(
                        jnp.dot(window(i, j), taps[n, 3 * i + j], preferred_element_type=F32)
                        for i in range(3)
                        for j in range(3)
                    )
                total[here] += product.reshape(chunk, width, chans_in)

    if final:
        half = rows // PAIR
        outs[0][...] = total[pl.ds(side * half, half)]
        outs[1][...] = total[pl.ds((1 - side) * half, half)]
    else:
        outs[0][...] = total[...]


def input_partial(depth, steps, final, at, cot, kernels, before):
    rows, width, filters = cot.shape[2] - 2, cot.shape[3], cot.shape[4]
    chans_in = kernels[0].shape[2]
    count = len(steps)
    if final:
        half = jax.ShapeDtypeStruct((rows // PAIR, width, chans_in), F32)
        out_shape, out_specs = (half, half), (VMEM, VMEM)
    else:
        out_shape, out_specs = jax.ShapeDtypeStruct((rows, width, chans_in), F32), VMEM
    extra = [] if before is None else [before]
    return pl.pallas_call(
        functools.partial(input_kernel, depth, steps, final),
        out_shape=out_shape,
        in_specs=[SMEM, ANY] + [ANY] * count + [VMEM] * len(extra),
        out_specs=out_specs,
        scratch_shapes=[
            pltpu.VMEM((rows, width, chans_in), F32),
            pltpu.VMEM((count,) + cot.shape[1:], BF16),
            pltpu.VMEM((count,) + kernels[0].shape, BF16),
            pltpu.SemaphoreType.DMA((count, 2)),
        ],
        compiler_params=params(48),
        cost_estimate=cost(18 * rows * width * chans_in * filters * 2, count * 2 * 3 * (rows + 2) * width * filters),
        name="input_gradient",
    )(at, cot, *kernels, *extra)


def line_gather(value, depth, each=None):
    got = [value]
    below = above = value
    for step in range(1, depth):
        up = [(z * PAIR + y, (z + 1) * PAIR + y) for z in range(step - 1, depth - 1) for y in range(PAIR)]
        down = [(z * PAIR + y, (z - 1) * PAIR + y) for z in range(1, depth - step + 1) for y in range(PAIR)]
        below = lax.ppermute(below, "filt", up)
        above = lax.ppermute(above, "filt", down)
        got += [below, above]
    return got


def pair_swap(value, depth, valid=None):
    return lax.ppermute(
        value,
        "filt",
        [(z * PAIR + y, z * PAIR + 1 - y) for z in range(depth) if valid is None or valid(z) for y in range(PAIR)],
    )


def body(inputs, weights, cotangent):
    chans, filts = lax.axis_size("chan"), lax.axis_size("filt")
    depth = filts // PAIR
    chan, filt = lax.axis_index("chan"), lax.axis_index("filt")
    line, side = filt // PAIR, filt % PAIR
    far, core = chan // 2, chan % 2
    at = jnp.stack([line, side, far, core]).astype(jnp.int32)
    own_rows, width, chans_in = inputs.shape[1:]
    block, filters = cotangent.shape[1], cotangent.shape[2]
    height = own_rows * filts
    scale = 1.0 / math.sqrt(inputs.shape[0] * height * width)

    cot_all = lax.all_gather(cotangent[0], "chan", axis=0, tiled=True)

    mine = line_gather(inputs[0], depth)
    theirs = [pair_swap(mine[0], depth)]
    for step in range(1, depth):
        theirs.append(pair_swap(mine[2 * step - 1], depth, lambda z: z >= step))
        theirs.append(pair_swap(mine[2 * step], depth, lambda z: z + step < depth))

    padded = jnp.pad(cot_all, ((1, 1), (0, 0), (0, 0)))
    part = filters // chans
    line_rows = own_rows * PAIR
    pieces = []
    for step in range(depth):
        target = lax.rem(line + step, depth)
        piece = lax.dynamic_slice(padded, (target * line_rows, chan * part, 0), (line_rows + 2, part, width))
        if step:
            piece = lax.ppermute(
                piece,
                "filt",
                [(z * PAIR + y, (z + step) % depth * PAIR + y) for z in range(depth) for y in range(PAIR)],
            )
        pieces.append(piece)
    sources = turned(lax.all_gather(jnp.stack(pieces), "chan", axis=0))

    kernels = line_gather(weights.reshape((9,) + weights.shape[2:]), depth)

    keep, send = forward_partial(depth, chans, at, weights, mine, theirs)
    from_core = lax.ppermute(send, "chan", [(c, c ^ 1) for c in range(chans)])
    outputs = None
    for step in range(1, chans // 2):
        moving = keep[step] + from_core[step]
        came = lax.ppermute(moving, "chan", [(c, (c + 2 * step) % chans) for c in range(chans)])
        outputs = came if outputs is None else outputs + came
    outputs = keep[0] + from_core[0] + outputs if outputs is not None else keep[0] + from_core[0]
    outputs = outputs.astype(BF16)[None]

    weight_grad = weight_gradient(depth, at, scale, cot_all, mine, theirs)
    weight_grad = weight_grad.reshape((3, 3, filters, chans_in))

    total = None
    for step in range(1, depth):
        steps = ((0,) if step == 1 else ()) + (-step, step)
        arrived = ([kernels[0]] if step == 1 else []) + kernels[2 * step - 1 : 2 * step + 1]
        total = input_partial(depth, steps, step == depth - 1, at, sources, arrived, total)
    kept, sent = total
    input_grad = (kept + pair_swap(sent, depth)).astype(BF16)[None]
    return (outputs, input_grad, weight_grad)


def solution(mesh):
    return jax.shard_map(
        body,
        mesh=mesh,
        in_specs=(
            P(None, "filt", None, "chan"),
            P(None, None, "filt", "chan"),
            P(None, "chan", "filt", None),
        ),
        out_specs=(
            P(None, "chan", "filt", None),
            P(None, "filt", None, "chan"),
            P(None, None, "filt", "chan"),
        ),
        check_vma=False,
    )
```

```python
import functools
import math

import jax
import jax.numpy as jnp
from jax import lax
from jax.experimental import pallas as pl
from jax.experimental.pallas import tpu as pltpu
from jax.sharding import PartitionSpec as P

F32 = jnp.float32
BF16 = jnp.bfloat16
NT = (((1,), (1,)), ((), ()))
HBM = pl.BlockSpec(memory_space=pltpu.HBM)
VMEM = pl.BlockSpec(memory_space=pltpu.VMEM)
SMEM = pl.BlockSpec(memory_space=pltpu.SMEM)
PAIR = 2


def params(mib):
    return pltpu.CompilerParams(vmem_limit_bytes=mib << 20)


def cost(flops, moved):
    return pl.CostEstimate(flops=int(flops), bytes_accessed=int(moved), transcendentals=0)


def lane_shift(value, by):
    size = value.shape[1]
    lane = lax.broadcasted_iota(jnp.int32, value.shape, 1)
    keep = lane >= by if by > 0 else lane < size + by
    return jnp.where(keep, pltpu.roll(value, by % size, 1), 0.0)


def row_shift(value, by):
    size = value.shape[0]
    row = lax.broadcasted_iota(jnp.int32, value.shape, 0)
    keep = row >= by if by > 0 else row < size + by
    return jnp.where(keep, pltpu.roll(value, by % size, 0), 0.0)


def load_rows(depth, side, parts, rows, sems):
    height = sum(part.shape[1] for part in parts[0])
    rows[0] = jnp.zeros(rows.shape[1:], rows.dtype)
    rows[rows.shape[0] - 1] = jnp.zeros(rows.shape[1:], rows.dtype)
    copies = []
    for half in range(PAIR):
        of_side = lax.rem(side + half, PAIR)
        first = 1 + of_side * height
        for index, part in enumerate(parts[half]):
            size = part.shape[1]
            for block in range(depth):
                copies.append(
                    pltpu.make_async_copy(
                        part.at[block],
                        rows.at[pl.ds(first + block * PAIR * height, size)],
                        sems.at[half, index, block],
                    )
                )
            first = first + size
    for copy in copies:
        copy.start()
    for copy in copies:
        copy.wait()


def forward_kernel(depth, chans, at, weights, *refs):
    count = (len(refs) - 5) // 2
    parts = (refs[:count], refs[count : 2 * count])
    keep, send, rows, taps, sems = refs[2 * count :]
    load_rows(depth, at[1], parts, rows, sems)
    filters, chans_in = weights.shape[2], weights.shape[3]
    for tap_row in range(3):
        for tap_col in range(3):
            taps[pl.ds(tap_col * filters, filters), pl.ds(tap_row * chans_in, chans_in)] = weights[tap_row, tap_col]
    width = rows.shape[1]
    block = keep.shape[1]
    group = min(4, block)
    per_block = block // group
    far, core = at[2], at[3]

    def run(target, of_core, step):
        which, group_at = step // per_block, step % per_block
        first = ((lax.rem(far + which, chans // 2)) * 2 + of_core) * block + group_at * group
        window = jnp.concatenate(
            [rows[pl.ds(first + i, group)].reshape(group * width, chans_in) for i in range(3)], axis=1
        )
        product = lax.dot_general(taps[...], window, NT, preferred_element_type=F32)
        for row in range(group):
            part = [
                product[j * filters : (j + 1) * filters, row * width : (row + 1) * width] for j in range(3)
            ]
            target[which, group_at * group + row] = part[1] + lane_shift(part[0], 1) + lane_shift(part[2], -1)

    @pl.loop(0, (chans // 2) * per_block)
    def _(step):
        run(send, 1 - core, step)
        run(keep, core, step)


def forward_partial(depth, chans, at, weights, own, other):
    width, chans_in = own[0].shape[2:]
    filters = weights.shape[2]
    rows = sum(part.shape[1] for part in own) * depth * PAIR
    half = jax.ShapeDtypeStruct((chans // 2, rows // chans, filters, width), F32)
    return pl.pallas_call(
        functools.partial(forward_kernel, depth, chans),
        out_shape=(half, half),
        in_specs=[SMEM, VMEM] + [HBM] * (len(own) + len(other)),
        out_specs=(VMEM, VMEM),
        scratch_shapes=[
            pltpu.VMEM((rows + 2, width, chans_in), BF16),
            pltpu.VMEM((3 * filters, 3 * chans_in), BF16),
            pltpu.SemaphoreType.DMA((PAIR, len(own), depth)),
        ],
        compiler_params=params(40),
        cost_estimate=cost(18 * rows * width * chans_in * filters, 4 * rows * width * filters + 2 * rows * width * chans_in),
        name="forward",
    )(at, weights, *own, *other)


def weight_kernel(depth, scale, at, cot, *refs):
    count = (len(refs) - 4) // 2
    parts = (refs[:count], refs[count : 2 * count])
    out, rows, moved, sems = refs[2 * count :]
    load_rows(depth, at[1], parts, rows, sems)
    filters, width = cot.shape[1], cot.shape[2]
    total = cot.shape[0] - 2
    chans_in = rows.shape[2]
    chunk = min(8, total)
    out[...] = jnp.zeros(out.shape, F32)

    @pl.loop(0, total // chunk)
    def _(step):
        first = step * chunk
        for row in range(chunk):
            value = cot[1 + first + row]
            wide = value.astype(F32)
            lanes = pl.ds(row * width, width)
            moved[0:filters, lanes] = lane_shift(wide, -1).astype(BF16)
            moved[filters : 2 * filters, lanes] = value
            moved[2 * filters :, lanes] = lane_shift(wide, 1).astype(BF16)
        for tap_row in range(3):
            window = rows[pl.ds(first + tap_row, chunk)].reshape(chunk * width, chans_in)
            out[tap_row] += jnp.dot(moved[...], window, preferred_element_type=F32)

    out[...] = out[...] * scale


def weight_gradient(depth, at, scale, cot, own, other):
    width, chans_in = own[0].shape[2:]
    rows, filters = cot.shape[0] - 2, cot.shape[1]
    return pl.pallas_call(
        functools.partial(weight_kernel, depth, scale),
        out_shape=jax.ShapeDtypeStruct((3, 3 * filters, chans_in), F32),
        in_specs=[SMEM, VMEM] + [HBM] * (len(own) + len(other)),
        out_specs=VMEM,
        scratch_shapes=[
            pltpu.VMEM((rows + 2, width, chans_in), BF16),
            pltpu.VMEM((3 * filters, min(8, rows) * width), BF16),
            pltpu.SemaphoreType.DMA((PAIR, len(own), depth)),
        ],
        compiler_params=params(40),
        cost_estimate=cost(18 * rows * width * chans_in * filters, 2 * rows * width * (filters + chans_in) + 36 * filters * chans_in),
        name="weight_gradient",
    )(at, cot, *own, *other)


def turn_kernel(at, same, cross, out):
    fars, _, rows, _, _ = same.shape
    far, core = at[2], at[3]

    @pl.loop(0, rows)
    def _(row):
        parts = []
        for c in range(2 * fars):
            from_far = lax.rem(far - c // 2 + fars, fars)
            parts.append(jnp.where(core == c % 2, same[from_far, 0, row].astype(F32), cross[from_far, 0, row].astype(F32)))
        turned = jnp.concatenate(parts, axis=0).T
        out[0, 0, row] = row_shift(turned, -1).astype(BF16)
        out[0, 1, row] = turned.astype(BF16)
        out[0, 2, row] = row_shift(turned, 1).astype(BF16)


def turned(at, same, cross):
    fars, depth, rows, part, width = same.shape
    filters = 2 * fars * part
    spec = pl.BlockSpec((fars, 1, rows, part, width), lambda d: (0, d, 0, 0, 0))
    return pl.pallas_call(
        turn_kernel,
        grid=(depth,),
        out_shape=jax.ShapeDtypeStruct((depth, 3, rows, width, filters), BF16),
        in_specs=[SMEM, spec, spec],
        out_specs=pl.BlockSpec((1, 3, rows, width, filters), lambda d: (d, 0, 0, 0, 0)),
        compiler_params=params(32),
        cost_estimate=cost(4e9, 8 * depth * rows * width * filters),
        name="turned",
    )(at, same, cross)


def input_kernel(at, cot, kernels, keep, send, total, source, taps, sems):
    line, side = at[0], at[1]
    depth = kernels.shape[0]
    rows, width, chans_in = total.shape
    filters = taps.shape[2]
    copies = []
    for n in range(depth):
        copies.append(
            (
                pltpu.make_async_copy(cot.at[n], source.at[n], sems.at[n, 0]),
                pltpu.make_async_copy(kernels.at[lax.rem(line - n + depth, depth)], taps.at[n], sems.at[n, 1]),
            )
        )
        for copy in copies[n]:
            copy.start()
    total[...] = jnp.zeros(total.shape, F32)
    chunk = min(8, rows)
    for n in range(depth):
        for copy in copies[n]:
            copy.wait()

        @pl.loop(0, rows // chunk)
        def _(step):
            first = step * chunk

            def window(i, j):
                return source[n, j, pl.ds(first + 2 - i, chunk)].reshape(chunk * width, filters)

            if filters % 128 == 0:
                value = jnp.concatenate([window(i, j) for i in range(3) for j in range(3)], axis=1)
                product = jnp.dot(value, taps[n].reshape(9 * filters, chans_in), preferred_element_type=F32)
            else:
                product = sum(
                    jnp.dot(window(i, j), taps[n, 3 * i + j], preferred_element_type=F32)
                    for i in range(3)
                    for j in range(3)
                )
            total[pl.ds(first, chunk)] += product.reshape(chunk, width, chans_in)

    half = rows // PAIR
    keep[...] = total[pl.ds(side * half, half)]
    send[...] = total[pl.ds((1 - side) * half, half)]


def input_partial(at, cot, kernels):
    depth, _, rows, width, filters = cot.shape
    rows = rows - 2
    chans_in = kernels.shape[3]
    half = jax.ShapeDtypeStruct((rows // PAIR, width, chans_in), F32)
    return pl.pallas_call(
        input_kernel,
        out_shape=(half, half),
        in_specs=[SMEM, HBM, HBM],
        out_specs=(VMEM, VMEM),
        scratch_shapes=[
            pltpu.VMEM((rows, width, chans_in), F32),
            pltpu.VMEM(cot.shape, BF16),
            pltpu.VMEM(kernels.shape, BF16),
            pltpu.SemaphoreType.DMA((depth, 2)),
        ],
        compiler_params=params(40),
        cost_estimate=cost(18 * rows * width * chans_in * filters * depth * 2, depth * 6 * (rows + 2) * width * filters),
        name="input_gradient",
    )(at, cot, kernels)


def line_gather(value, depth):
    groups = [[z * PAIR + y for z in range(depth)] for y in range(PAIR)]
    return lax.all_gather(value, "filt", axis=0, axis_index_groups=groups)


def fars_gather(value, chans):
    got = [value]
    for step in range(1, chans // 2):
        got.append(lax.ppermute(value, "chan", [(c, (c + 2 * step) % chans) for c in range(chans)]))
    return jnp.stack(got)


def core_swap(value, chans):
    return lax.ppermute(value, "chan", [(c, c ^ 1) for c in range(chans)])


def pair_swap(value, depth):
    return lax.ppermute(
        value, "filt", [(z * PAIR + y, z * PAIR + 1 - y) for z in range(depth) for y in range(PAIR)]
    )


def cuts(rows):
    if rows < 8:
        return [rows // 2, rows - rows // 2] if rows > 1 else [rows]
    return [rows // 4, 3 * rows // 8, rows - rows // 4 - 3 * rows // 8]


def body(inputs, weights, cotangent):
    chans, filts = lax.axis_size("chan"), lax.axis_size("filt")
    depth = filts // PAIR
    chan, filt = lax.axis_index("chan"), lax.axis_index("filt")
    line, side = filt // PAIR, filt % PAIR
    far, core = chan // 2, chan % 2
    at = jnp.stack([line, side, far, core]).astype(jnp.int32)
    own_rows, width, chans_in = inputs.shape[1:]
    block, filters = cotangent.shape[1], cotangent.shape[2]
    height = own_rows * filts
    scale = 1.0 / math.sqrt(inputs.shape[0] * height * width)

    mine, theirs, first = [], [], 0
    for size in cuts(own_rows):
        mine.append(line_gather(inputs[0, first : first + size], depth))
        first += size
    kernels = [line_gather(part.reshape((9,) + part.shape[2:]), depth) for part in jnp.split(weights, 2, axis=3)]

    same = fars_gather(cotangent[0], chans)
    cross = core_swap(same, chans)
    padded = jnp.zeros((height + 2, filters, width), BF16)
    for step in range(chans // 2):
        at_far = lax.rem(far - step + chans // 2, chans // 2) * 2
        padded = lax.dynamic_update_slice(padded, same[step], (1 + (at_far + core) * block, 0, 0))
        padded = lax.dynamic_update_slice(padded, cross[step], (1 + (at_far + 1 - core) * block, 0, 0))

    part = filters // chans
    line_rows = own_rows * PAIR
    pieces = []
    for step in range(depth):
        target = lax.rem(line + step, depth)
        piece = lax.dynamic_slice(padded, (target * line_rows, chan * part, 0), (line_rows + 2, part, width))
        if step:
            piece = lax.ppermute(
                piece,
                "filt",
                [(z * PAIR + y, (z + step) % depth * PAIR + y) for z in range(depth) for y in range(PAIR)],
            )
        pieces.append(piece)
    same = fars_gather(jnp.stack(pieces), chans)
    sources = turned(at, same, core_swap(same, chans))

    theirs = [pair_swap(part, depth) for part in mine]
    keep, send = forward_partial(depth, chans, at, weights, mine, theirs)
    from_core = core_swap(send, chans)
    outputs = keep[0] + from_core[0]
    for step in range(1, chans // 2):
        moving = keep[step] + from_core[step]
        outputs += lax.ppermute(moving, "chan", [(c, (c + 2 * step) % chans) for c in range(chans)])
    outputs = outputs.astype(BF16)[None]

    weight_grad = weight_gradient(depth, at, scale, padded, mine, theirs)
    weight_grad = weight_grad.reshape((3, 3, filters, chans_in))

    input_grad = []
    for part in kernels:
        kept, sent = input_partial(at, sources, part)
        input_grad.append((kept + pair_swap(sent, depth)).astype(BF16))
    input_grad = jnp.concatenate(input_grad, axis=2)[None]
    return (outputs, input_grad, weight_grad)


def solution(mesh):
    return jax.shard_map(
        body,
        mesh=mesh,
        in_specs=(
            P(None, "filt", None, "chan"),
            P(None, None, "filt", "chan"),
            P(None, "chan", "filt", None),
        ),
        out_specs=(
            P(None, "chan", "filt", None),
            P(None, "filt", None, "chan"),
            P(None, None, "filt", "chan"),
        ),
        check_vma=False,
    )
```

```python
import functools
import math

import jax
import jax.numpy as jnp
from jax import lax
from jax.experimental import pallas as pl
from jax.experimental.pallas import tpu as pltpu
from jax.sharding import PartitionSpec as P

F32 = jnp.float32
BF16 = jnp.bfloat16
NT = (((1,), (1,)), ((), ()))
HBM = pl.BlockSpec(memory_space=pltpu.HBM)
VMEM = pl.BlockSpec(memory_space=pltpu.VMEM)
SMEM = pl.BlockSpec(memory_space=pltpu.SMEM)
PAIR = 2


def params(mib):
    return pltpu.CompilerParams(vmem_limit_bytes=mib << 20)


def cost(flops, moved):
    return pl.CostEstimate(flops=int(flops), bytes_accessed=int(moved), transcendentals=0)


def lane_shift(value, by):
    size = value.shape[1]
    lane = lax.broadcasted_iota(jnp.int32, value.shape, 1)
    keep = lane >= by if by > 0 else lane < size + by
    return jnp.where(keep, pltpu.roll(value, by % size, 1), 0.0)


def after(value, *others):
    return lax.optimization_barrier((value,) + others)[0]


def offsets(depth):
    apart = [(0,)]
    for step in range(1, depth):
        apart += [(-step,), (step,)] if 2 * step < depth else [(-step, step)]
    return apart


def singles(depth):
    return [0] + [way for step in range(1, depth) for way in (-step, step)]


def load_rows(depth, mine, parts, rows, sems):
    height = parts[0][0].shape[0]
    line, side = mine
    rows[0] = jnp.zeros(rows.shape[1:], rows.dtype)
    rows[rows.shape[0] - 1] = jnp.zeros(rows.shape[1:], rows.dtype)

    def each(act):
        for half in range(PAIR):
            of_side = lax.rem(side + half, PAIR)
            for index, ways in enumerate(offsets(depth)):
                for way in ways:
                    block = line + way
                    copy = pltpu.make_async_copy(
                        parts[half][index],
                        rows.at[pl.ds(1 + (block * PAIR + of_side) * height, height)],
                        sems.at[half, index],
                    )
                    pl.when(jnp.logical_and(block >= 0, block < depth))(functools.partial(act, copy))

    each(lambda copy: copy.start())
    each(lambda copy: copy.wait())


def forward_kernel(depth, chans, at, weights, *refs):
    count = (len(refs) - 4) // 2
    parts = (refs[:count], refs[count : 2 * count])
    target, rows, taps, sems = refs[2 * count :]
    load_rows(depth, (at[0], at[1]), parts, rows, sems)
    filters, chans_in = weights.shape[2], weights.shape[3]
    for tap_row in range(3):
        for tap_col in range(3):
            taps[pl.ds(tap_col * filters, filters), pl.ds(tap_row * chans_in, chans_in)] = weights[tap_row, tap_col]
    width = rows.shape[1]
    block = target.shape[1]
    group = min(4, block)
    per_block = block // group
    far, of_core = at[2], at[4]

    @pl.loop(0, (chans // 2) * per_block)
    def _(step):
        which, group_at = step // per_block, step % per_block
        first = ((lax.rem(far + which, chans // 2)) * 2 + of_core) * block + group_at * group
        window = jnp.concatenate(
            [rows[pl.ds(first + i, group)].reshape(group * width, chans_in) for i in range(3)], axis=1
        )
        product = lax.dot_general(taps[...], window, NT, preferred_element_type=F32)
        for row in range(group):
            part = [
                product[j * filters : (j + 1) * filters, row * width : (row + 1) * width] for j in range(3)
            ]
            target[which, group_at * group + row] = part[1] + lane_shift(part[0], 1) + lane_shift(part[2], -1)


def forward_partial(depth, chans, at, weights, own, other):
    height, width, chans_in = own[0].shape
    filters = weights.shape[2]
    rows = height * depth * PAIR
    half = jax.ShapeDtypeStruct((chans // 2, rows // chans, filters, width), F32)
    return pl.pallas_call(
        functools.partial(forward_kernel, depth, chans),
        out_shape=half,
        in_specs=[SMEM, VMEM] + [HBM] * (len(own) + len(other)),
        out_specs=VMEM,
        scratch_shapes=[
            pltpu.VMEM((rows + 2, width, chans_in), BF16),
            pltpu.VMEM((3 * filters, 3 * chans_in), BF16),
            pltpu.SemaphoreType.DMA((PAIR, len(own))),
        ],
        compiler_params=params(40),
        cost_estimate=cost(9 * rows * width * chans_in * filters, 2 * rows * width * (filters + chans_in)),
        name="forward",
    )(at, weights, *own, *other)


def weight_kernel(depth, scale, at, cot, *refs):
    count = (len(refs) - 4) // 2
    parts = (refs[:count], refs[count : 2 * count])
    out, rows, moved, sems = refs[2 * count :]
    load_rows(depth, (at[0], at[1]), parts, rows, sems)
    filters, width = cot.shape[1], cot.shape[2]
    total = cot.shape[0] - 2
    chans_in = rows.shape[2]
    chunk = min(8, total)
    out[...] = jnp.zeros(out.shape, F32)

    @pl.loop(0, total // chunk)
    def _(step):
        first = step * chunk
        for row in range(chunk):
            value = cot[1 + first + row]
            wide = value.astype(F32)
            lanes = pl.ds(row * width, width)
            moved[0:filters, lanes] = lane_shift(wide, -1).astype(BF16)
            moved[filters : 2 * filters, lanes] = value
            moved[2 * filters :, lanes] = lane_shift(wide, 1).astype(BF16)
        for tap_row in range(3):
            window = rows[pl.ds(first + tap_row, chunk)].reshape(chunk * width, chans_in)
            out[tap_row] += jnp.dot(moved[...], window, preferred_element_type=F32)

    out[...] = out[...] * scale


def weight_gradient(depth, at, scale, cot, own, other):
    width, chans_in = own[0].shape[1:]
    rows, filters = cot.shape[0] - 2, cot.shape[1]
    return pl.pallas_call(
        functools.partial(weight_kernel, depth, scale),
        out_shape=jax.ShapeDtypeStruct((3, 3 * filters, chans_in), F32),
        in_specs=[SMEM, VMEM] + [HBM] * (len(own) + len(other)),
        out_specs=VMEM,
        scratch_shapes=[
            pltpu.VMEM((rows + 2, width, chans_in), BF16),
            pltpu.VMEM((3 * filters, min(8, rows) * width), BF16),
            pltpu.SemaphoreType.DMA((PAIR, len(own))),
        ],
        compiler_params=params(40),
        cost_estimate=cost(18 * rows * width * chans_in * filters, 2 * rows * width * (filters + chans_in) + 36 * filters * chans_in),
        name="weight_gradient",
    )(at, cot, *own, *other)


def turn_kernel(pieces, out):
    @pl.loop(0, pieces.shape[2])
    def _(row):
        value = jnp.concatenate([pieces[c, 0, row].astype(F32) for c in range(pieces.shape[0])], axis=0)
        out[0, row] = value.T.astype(BF16)


def turned(pieces):
    chans, depth, rows, part, width = pieces.shape
    return pl.pallas_call(
        turn_kernel,
        grid=(depth,),
        out_shape=jax.ShapeDtypeStruct((depth, rows, width, chans * part), BF16),
        in_specs=[pl.BlockSpec((chans, 1, rows, part, width), lambda d: (0, d, 0, 0, 0))],
        out_specs=pl.BlockSpec((1, rows, width, chans * part), lambda d: (d, 0, 0, 0)),
        compiler_params=params(32),
        cost_estimate=cost(4e9, 4 * depth * rows * width * chans * part),
        name="turned",
    )(pieces)


def input_kernel(depth, first, last, at, cot, *refs):
    ways = singles(depth)[first:last]
    count = len(ways)
    kernels, refs = refs[:count], refs[count:]
    before = None
    if first:
        before, refs = refs[0], refs[1:]
    final = last == len(singles(depth))
    outs, refs = refs[: 2 if final else 1], refs[2 if final else 1 :]
    total, source, taps, stacked, sems = refs
    line, side = at[0], at[1]
    rows, width, chans_in = total.shape
    filters = taps.shape[2]
    cases = list(enumerate(ways))

    def when(way):
        return pl.when(jnp.logical_and(line + way >= 0, line + way < depth))

    def copies(n, way):
        return (
            pltpu.make_async_copy(cot.at[line + way], source.at[n], sems.at[n, 0]),
            pltpu.make_async_copy(kernels[n], taps.at[n], sems.at[n, 1]),
        )

    for n, way in cases:

        @when(way)
        def _():
            for copy in copies(n, way):
                copy.start()

    if before is None:
        total[...] = jnp.zeros(total.shape, F32)
    else:
        total[...] = before[...]
    chunk = min(4, rows)
    lanes = lax.broadcasted_iota(jnp.int32, (width, chans_in), 0)
    for n, way in cases:

        @when(way)
        def _():
            for copy in copies(n, way):
                copy.wait()
            for i in range(3):
                for j in range(3):
                    stacked[pl.ds(i * filters, filters), pl.ds(j * chans_in, chans_in)] = taps[n, 3 * i + j]

            @pl.loop(0, rows // chunk)
            def _(step):
                at_row = step * chunk
                window = [
                    source[n, pl.ds(at_row + 2 - i, chunk)].reshape(chunk * width, filters) for i in range(3)
                ]
                if filters % 128 == 0:
                    product = jnp.dot(jnp.concatenate(window, axis=1), stacked[...], preferred_element_type=F32)
                else:
                    product = sum(
                        jnp.dot(window[i], stacked[i * filters : (i + 1) * filters], preferred_element_type=F32)
                        for i in range(3)
                    )
                for row in range(chunk):
                    here = [
                        product[row * width : (row + 1) * width, j * chans_in : (j + 1) * chans_in] for j in range(3)
                    ]
                    before_it = jnp.where(lanes < width - 1, pltpu.roll(here[0], width - 1, 0), 0.0)
                    behind_it = jnp.where(lanes >= 1, pltpu.roll(here[2], 1, 0), 0.0)
                    total[at_row + row] += here[1] + before_it + behind_it

    if final:
        half = rows // PAIR
        outs[0][...] = total[pl.ds(side * half, half)]
        outs[1][...] = total[pl.ds((1 - side) * half, half)]
    else:
        outs[0][...] = total[...]


def input_partial(depth, first, last, at, cot, kernels, before):
    rows, width, filters = cot.shape[1] - 2, cot.shape[2], cot.shape[3]
    chans_in = kernels[0].shape[2]
    count = last - first
    if last == len(singles(depth)):
        half = jax.ShapeDtypeStruct((rows // PAIR, width, chans_in), F32)
        out_shape, out_specs = (half, half), (VMEM, VMEM)
    else:
        out_shape, out_specs = jax.ShapeDtypeStruct((rows, width, chans_in), F32), VMEM
    extra = [] if before is None else [before]
    return pl.pallas_call(
        functools.partial(input_kernel, depth, first, last),
        out_shape=out_shape,
        in_specs=[SMEM, HBM] + [HBM] * count + [VMEM] * len(extra),
        out_specs=out_specs,
        scratch_shapes=[
            pltpu.VMEM((rows, width, chans_in), F32),
            pltpu.VMEM((count,) + cot.shape[1:], BF16),
            pltpu.VMEM((count,) + kernels[0].shape, BF16),
            pltpu.VMEM((3 * filters, 3 * chans_in), BF16),
            pltpu.SemaphoreType.DMA((count, 2)),
        ],
        compiler_params=params(40),
        cost_estimate=cost(18 * rows * width * chans_in * filters * count, 2 * count * (rows + 2) * width * filters),
        name="input_gradient",
    )(at, cot, *kernels, *extra)


def lines(depth):
    return [[z * PAIR + y for z in range(depth)] for y in range(PAIR)]


def line_steps(step, depth):
    up = [(z * PAIR + y, (z + 1) * PAIR + y) for z in range(step - 1, depth - 1) for y in range(PAIR)]
    down = [(z * PAIR + y, (z - 1) * PAIR + y) for z in range(1, depth - step + 1) for y in range(PAIR)]
    return up, down


def line_gather(value, depth, gates):
    got = [value]
    below = above = value
    for step in range(1, depth):
        up, down = line_steps(step, depth)
        wait = gates(step)
        if wait:
            below, above = after(below, *wait), after(above, *wait)
        below, above = lax.ppermute(below, "filt", up), lax.ppermute(above, "filt", down)
        got += [below, above]
    return got


def merged(got, depth, line):
    kept = [got[0]]
    for step in range(1, depth):
        below, above = got[2 * step - 1 : 2 * step + 1]
        kept += [below, above] if 2 * step < depth else [jnp.where(line >= step, below, above)]
    return kept


def core_swap(value, chans):
    return lax.ppermute(value, "chan", [(c, c ^ 1) for c in range(chans)])


def pair_swap(value, depth, ways=(0,)):
    pairs = [
        (z * PAIR + y, z * PAIR + 1 - y)
        for z in range(depth)
        if any(0 <= z + way < depth for way in ways)
        for y in range(PAIR)
    ]
    return lax.ppermute(value, "filt", pairs)


def body(inputs, weights, cotangent):
    chans, filts = lax.axis_size("chan"), lax.axis_size("filt")
    depth = filts // PAIR
    chan, filt = lax.axis_index("chan"), lax.axis_index("filt")
    line, side = filt // PAIR, filt % PAIR
    far, core = chan // 2, chan % 2
    at = jnp.stack([line, side, far, core, core]).astype(jnp.int32)
    at_send = jnp.stack([line, side, far, core, 1 - core]).astype(jnp.int32)
    own_rows, width, chans_in = inputs.shape[1:]
    block, filters = cotangent.shape[1], cotangent.shape[2]
    height = own_rows * filts
    scale = 1.0 / math.sqrt(inputs.shape[0] * height * width)
    ways = offsets(depth)

    cot_all = lax.all_gather(cotangent[0], "chan", axis=0, tiled=True)

    first_swap = pair_swap(inputs[0], depth)
    along = line_gather(inputs[0], depth, lambda step: [first_swap] if step == 2 else [])
    mine = merged(along, depth, line)
    theirs = [first_swap] + [pair_swap(value, depth, way) for value, way in zip(mine[1:], ways[1:])]

    padded = jnp.pad(cot_all, ((1, 1), (0, 0), (0, 0)))
    part = filters // chans
    line_rows = own_rows * PAIR
    own_part = lax.dynamic_slice_in_dim(padded, chan * part, part, axis=1)
    pieces = jnp.stack([own_part[z * line_rows : (z + 1) * line_rows + 2] for z in range(depth)])
    pieces = lax.all_to_all(after(pieces, *along[3:5]), "filt", 0, 0, axis_index_groups=lines(depth), tiled=True)
    sources = turned(lax.all_gather(pieces, "chan", axis=0))

    def gates(step):
        if step == 1:
            return along[-2:] + theirs[:3] + [pieces]
        if step == 2:
            return theirs[:-1]
        return theirs

    kernels = line_gather(weights.reshape((9,) + weights.shape[2:]), depth, gates)

    send = forward_partial(depth, chans, after(at_send, *kernels[1:3]), weights, mine, theirs)
    from_core = core_swap(send, chans)
    keep = forward_partial(depth, chans, after(at, send, *kernels[3:5]), weights, mine, theirs)
    outputs = keep[0] + from_core[0]
    for step in range(1, chans // 2):
        moving = keep[step] + from_core[step]
        at = after(at, moving)
        outputs += lax.ppermute(moving, "chan", [(c, (c + 2 * step) % chans) for c in range(chans)])
    outputs = outputs.astype(BF16)[None]

    near = min(3, 2 * depth - 1)
    total = input_partial(depth, 0, near, at, sources, kernels[:near], None)
    kept, sent = input_partial(depth, near, 2 * depth - 1, at, sources, kernels[near:], total)
    input_grad = (kept + pair_swap(sent, depth)).astype(BF16)[None]

    weight_grad = weight_gradient(depth, after(at, sent), scale, padded, mine, theirs)
    weight_grad = weight_grad.reshape((3, 3, filters, chans_in))
    return (outputs, input_grad, weight_grad)


def solution(mesh):
    return jax.shard_map(
        body,
        mesh=mesh,
        in_specs=(
            P(None, "filt", None, "chan"),
            P(None, None, "filt", "chan"),
            P(None, "chan", "filt", None),
        ),
        out_specs=(
            P(None, "chan", "filt", None),
            P(None, "filt", None, "chan"),
            P(None, None, "filt", "chan"),
        ),
        check_vma=False,
    )
```

```python
import functools
import math

import jax
import jax.numpy as jnp
from jax import lax
from jax.experimental import pallas as pl
from jax.experimental.pallas import tpu as pltpu
from jax.sharding import PartitionSpec as P

F32 = jnp.float32
BF16 = jnp.bfloat16
NT = (((1,), (1,)), ((), ()))
HBM = pl.BlockSpec(memory_space=pltpu.HBM)
VMEM = pl.BlockSpec(memory_space=pltpu.VMEM)
SMEM = pl.BlockSpec(memory_space=pltpu.SMEM)
PAIR = 2


def params(mib):
    return pltpu.CompilerParams(vmem_limit_bytes=mib << 20)


def lane_shift(value, by):
    size = value.shape[1]
    lane = lax.broadcasted_iota(jnp.int32, value.shape, 1)
    keep = lane >= by if by > 0 else lane < size + by
    return jnp.where(keep, pltpu.roll(value, by % size, 1), 0.0)


def after(value, *others):
    return lax.optimization_barrier((value,) + others)[0]


def offsets(depth):
    apart = [(0,)]
    for step in range(1, depth):
        apart += [(-step,), (step,)] if 2 * step < depth else [(-step, step)]
    return apart


def singles(depth):
    return [0] + [way for step in range(1, depth) for way in (-step, step)]


def start_rows(depth, mine, parts, rows, sems):
    height = parts[0][0].shape[0]
    line, side = mine

    def place(spot):
        return rows.at[pl.ds(1 + spot * height, height)]

    for half in range(PAIR):
        of_side = lax.rem(side + half, PAIR)
        for index, ways in enumerate(offsets(depth)):
            for way in ways:
                spot = (line + way) * PAIR + of_side

                @pl.when(jnp.logical_and(line + way >= 0, line + way < depth))
                def _():
                    pltpu.make_async_copy(parts[half][index], place(spot), sems.at[spot]).start()

    rows[0] = jnp.zeros(rows.shape[1:], rows.dtype)
    rows[rows.shape[0] - 1] = jnp.zeros(rows.shape[1:], rows.dtype)
    return lambda spot: pltpu.make_async_copy(parts[0][0], place(spot), sems.at[spot]).wait()


def forward_kernel(depth, chans, at, weights, *refs):
    count = (len(refs) - 5) // 2
    parts = (refs[:count], refs[count : 2 * count])
    keep, send, rows, taps, sems = refs[2 * count :]
    wait = start_rows(depth, (at[0], at[1]), parts, rows, sems)
    filters, chans_in = weights.shape[2], weights.shape[3]
    for tap_row in range(3):
        for tap_col in range(3):
            taps[pl.ds(tap_col * filters, filters), pl.ds(tap_row * chans_in, chans_in)] = weights[tap_row, tap_col]
    width = rows.shape[1]
    block = keep.shape[1]
    height = parts[0][0].shape[0]
    group = min(4, height)
    far, core = at[2], at[3]
    spots = depth * PAIR
    wait(0)
    for spot in range(spots):
        if spot + 1 < spots:
            wait(spot + 1)

        @pl.loop(0, height // group)
        def _(step):
            first = spot * height + step * group
            window = jnp.concatenate(
                [rows[pl.ds(first + i, group)].reshape(group * width, chans_in) for i in range(3)], axis=1
            )
            product = lax.dot_general(taps[...], window, NT, preferred_element_type=F32)
            owner = spot * height // block
            which = lax.rem(owner // 2 - far + chans // 2, chans // 2)
            for row in range(group):
                part = [
                    product[j * filters : (j + 1) * filters, row * width : (row + 1) * width] for j in range(3)
                ]
                value = part[1] + lane_shift(part[0], 1) + lane_shift(part[2], -1)
                inside = spot * height % block + step * group + row

                @pl.when(core == owner % 2)
                def _():
                    keep[which, inside] = value

                @pl.when(core != owner % 2)
                def _():
                    send[which, inside] = value


def forward_partial(depth, chans, at, weights, own, other):
    height, width, chans_in = own[0].shape
    filters = weights.shape[2]
    rows = height * depth * PAIR
    half = jax.ShapeDtypeStruct((chans // 2, rows // chans, filters, width), F32)
    return pl.pallas_call(
        functools.partial(forward_kernel, depth, chans),
        out_shape=(half, half),
        in_specs=[SMEM, VMEM] + [HBM] * (len(own) + len(other)),
        out_specs=(VMEM, VMEM),
        scratch_shapes=[
            pltpu.VMEM((rows + 2, width, chans_in), BF16),
            pltpu.VMEM((3 * filters, 3 * chans_in), BF16),
            pltpu.SemaphoreType.DMA((depth * PAIR,)),
        ],
        compiler_params=params(58),
        name="forward",
    )(at, weights, *own, *other)


def weight_kernel(depth, scale, at, cot, *refs):
    count = (len(refs) - 4) // 2
    parts = (refs[:count], refs[count : 2 * count])
    out, rows, moved, sems = refs[2 * count :]
    wait = start_rows(depth, (at[0], at[1]), parts, rows, sems)
    for spot in range(depth * PAIR):
        wait(spot)
    filters, width = cot.shape[1], cot.shape[2]
    total = cot.shape[0] - 2
    chans_in = rows.shape[2]
    chunk = min(8, total)
    out[...] = jnp.zeros(out.shape, F32)

    @pl.loop(0, total // chunk)
    def _(step):
        first = step * chunk
        for row in range(chunk):
            value = cot[1 + first + row]
            wide = value.astype(F32)
            lanes = pl.ds(row * width, width)
            moved[0:filters, lanes] = lane_shift(wide, -1).astype(BF16)
            moved[filters : 2 * filters, lanes] = value
            moved[2 * filters :, lanes] = lane_shift(wide, 1).astype(BF16)
        for tap_row in range(3):
            window = rows[pl.ds(first + tap_row, chunk)].reshape(chunk * width, chans_in)
            out[tap_row] += jnp.dot(moved[...], window, preferred_element_type=F32)

    out[...] = out[...] * scale


def weight_gradient(depth, at, scale, cot, own, other):
    width, chans_in = own[0].shape[1:]
    rows, filters = cot.shape[0] - 2, cot.shape[1]
    return pl.pallas_call(
        functools.partial(weight_kernel, depth, scale),
        out_shape=jax.ShapeDtypeStruct((3, 3 * filters, chans_in), F32),
        in_specs=[SMEM, VMEM] + [HBM] * (len(own) + len(other)),
        out_specs=VMEM,
        scratch_shapes=[
            pltpu.VMEM((rows + 2, width, chans_in), BF16),
            pltpu.VMEM((3 * filters, min(8, rows) * width), BF16),
            pltpu.SemaphoreType.DMA((depth * PAIR,)),
        ],
        compiler_params=params(58),
        name="weight_gradient",
    )(at, cot, *own, *other)


def turn_kernel(at, same, cross, out):
    fars, _, rows, _, _ = same.shape
    far, core = at[2], at[3]

    @pl.loop(0, rows)
    def _(row):
        parts = []
        for c in range(2 * fars):
            from_far = lax.rem(far - c // 2 + fars, fars)
            parts.append(jnp.where(core == c % 2, same[from_far, 0, row].astype(F32), cross[from_far, 0, row].astype(F32)))
        out[0, row] = jnp.concatenate(parts, axis=0).T.astype(BF16)


def turned(at, same, cross):
    fars, depth, rows, part, width = same.shape
    filters = 2 * fars * part
    spec = pl.BlockSpec((fars, 1, rows, part, width), lambda d: (0, d, 0, 0, 0))
    return pl.pallas_call(
        turn_kernel,
        grid=(depth,),
        out_shape=jax.ShapeDtypeStruct((depth, rows, width, filters), BF16),
        in_specs=[SMEM, spec, spec],
        out_specs=pl.BlockSpec((1, rows, width, filters), lambda d: (d, 0, 0, 0)),
        compiler_params=params(58),
        name="turned",
    )(at, same, cross)


def input_kernel(depth, first, last, at, cot, *refs):
    ways = singles(depth)[first:last]
    count = len(ways)
    kernels, refs = refs[:count], refs[count:]
    before = None
    if first:
        before, refs = refs[0], refs[1:]
    final = last == len(singles(depth))
    outs, refs = refs[: 2 if final else 1], refs[2 if final else 1 :]
    total, source, taps, stacked, sems = refs
    line, side = at[0], at[1]
    rows, width, chans_in = total.shape
    filters = taps.shape[2]
    cases = list(enumerate(ways))

    def when(way):
        return pl.when(jnp.logical_and(line + way >= 0, line + way < depth))

    def copies(n, way):
        return (
            pltpu.make_async_copy(cot.at[line + way], source.at[n], sems.at[n, 0]),
            pltpu.make_async_copy(kernels[n], taps.at[n], sems.at[n, 1]),
        )

    for n, way in cases:

        @when(way)
        def _():
            for copy in copies(n, way):
                copy.start()

    if before is None:
        total[...] = jnp.zeros(total.shape, F32)
    else:
        total[...] = before[...]
    chunk = min(4, rows)
    lanes = lax.broadcasted_iota(jnp.int32, (width, chans_in), 0)
    for n, way in cases:

        @when(way)
        def _():
            for copy in copies(n, way):
                copy.wait()
            for i in range(3):
                for j in range(3):
                    stacked[pl.ds(i * filters, filters), pl.ds(j * chans_in, chans_in)] = taps[n, 3 * i + j]

            @pl.loop(0, rows // chunk)
            def _(step):
                at_row = step * chunk
                window = [
                    source[n, pl.ds(at_row + 2 - i, chunk)].reshape(chunk * width, filters) for i in range(3)
                ]
                if filters % 128 == 0:
                    product = jnp.dot(jnp.concatenate(window, axis=1), stacked[...], preferred_element_type=F32)
                else:
                    product = sum(
                        jnp.dot(window[i], stacked[i * filters : (i + 1) * filters], preferred_element_type=F32)
                        for i in range(3)
                    )
                for row in range(chunk):
                    here = [
                        product[row * width : (row + 1) * width, j * chans_in : (j + 1) * chans_in] for j in range(3)
                    ]
                    before_it = jnp.where(lanes < width - 1, pltpu.roll(here[0], width - 1, 0), 0.0)
                    behind_it = jnp.where(lanes >= 1, pltpu.roll(here[2], 1, 0), 0.0)
                    total[at_row + row] += here[1] + before_it + behind_it

    if final:
        half = rows // PAIR
        outs[0][...] = total[pl.ds(side * half, half)]
        outs[1][...] = total[pl.ds((1 - side) * half, half)]
    else:
        outs[0][...] = total[...]


def input_partial(depth, first, last, at, cot, kernels, before):
    rows, width, filters = cot.shape[1] - 2, cot.shape[2], cot.shape[3]
    chans_in = kernels[0].shape[2]
    count = last - first
    if last == len(singles(depth)):
        half = jax.ShapeDtypeStruct((rows // PAIR, width, chans_in), F32)
        out_shape, out_specs = (half, half), (VMEM, VMEM)
    else:
        out_shape, out_specs = jax.ShapeDtypeStruct((rows, width, chans_in), F32), VMEM
    extra = [] if before is None else [before]
    return pl.pallas_call(
        functools.partial(input_kernel, depth, first, last),
        out_shape=out_shape,
        in_specs=[SMEM, HBM] + [HBM] * count + [VMEM] * len(extra),
        out_specs=out_specs,
        scratch_shapes=[
            pltpu.VMEM((rows, width, chans_in), F32),
            pltpu.VMEM((count,) + cot.shape[1:], BF16),
            pltpu.VMEM((count,) + kernels[0].shape, BF16),
            pltpu.VMEM((3 * filters, 3 * chans_in), BF16),
            pltpu.SemaphoreType.DMA((count, 2)),
        ],
        compiler_params=params(58),
        name="input_gradient",
    )(at, cot, *kernels, *extra)


def fars_gather(value, chans):
    got = [value]
    for step in range(1, chans // 2):
        got.append(lax.ppermute(value, "chan", [(c, (c + 2 * step) % chans) for c in range(chans)]))
    return jnp.stack(got)


def lines(depth):
    return [[z * PAIR + y for z in range(depth)] for y in range(PAIR)]


def line_steps(step, depth):
    up = [(z * PAIR + y, (z + 1) * PAIR + y) for z in range(step - 1, depth - 1) for y in range(PAIR)]
    down = [(z * PAIR + y, (z - 1) * PAIR + y) for z in range(1, depth - step + 1) for y in range(PAIR)]
    return up, down


def line_step(along, step, depth, first):
    up, down = line_steps(step, depth)
    below, above = along[0 if step == 1 else -2], along[0 if step == 1 else -1]
    if first:
        below, above = after(below, *first), after(above, *first)
    return [lax.ppermute(below, "filt", up), lax.ppermute(above, "filt", down)]


def merged(got, depth, line):
    kept = [got[0]]
    for step in range(1, depth):
        below, above = got[2 * step - 1 : 2 * step + 1]
        kept += [below, above] if 2 * step < depth else [jnp.where(line >= step, below, above)]
    return kept


def core_swap(value, chans):
    return lax.ppermute(value, "chan", [(c, c ^ 1) for c in range(chans)])


def pair_swap(value, depth, ways=(0,)):
    pairs = [
        (z * PAIR + y, z * PAIR + 1 - y)
        for z in range(depth)
        if any(0 <= z + way < depth for way in ways)
        for y in range(PAIR)
    ]
    return lax.ppermute(value, "filt", pairs)


def body(inputs, weights, cotangent):
    chans, filts = lax.axis_size("chan"), lax.axis_size("filt")
    depth = filts // PAIR
    chan, filt = lax.axis_index("chan"), lax.axis_index("filt")
    line, side = filt // PAIR, filt % PAIR
    far, core = chan // 2, chan % 2
    at = jnp.stack([line, side, far, core]).astype(jnp.int32)
    own_rows, width, chans_in = inputs.shape[1:]
    block, filters = cotangent.shape[1], cotangent.shape[2]
    height = own_rows * filts
    scale = 1.0 / math.sqrt(inputs.shape[0] * height * width)
    ways = offsets(depth)

    swapped = [pair_swap(inputs[0], depth)]
    along = [inputs[0]]
    kernels = [weights.reshape((9,) + weights.shape[2:])]
    for step in range(1, depth):
        along += line_step(along, step, depth, ([], swapped, swapped + kernels[1:])[min(step - 1, 2)])
        if step == 1 or 2 * step < depth:
            swapped += [pair_swap(along[2 * step - 1], depth, (-step,)), pair_swap(along[2 * step], depth, (step,))]
        if step > 1:
            kernels += line_step(kernels, step - 1, depth, along[-2:])
    kernels += line_step(kernels, depth - 1, depth, along[-2:])
    mine = merged(along, depth, line)
    theirs = swapped + [
        pair_swap(value, depth, way) for value, way in zip(mine[len(swapped) :], ways[len(swapped) :])
    ]

    same = fars_gather(cotangent[0], chans)
    cross = core_swap(same, chans)
    padded = jnp.zeros((height + 2, filters, width), BF16)
    for step in range(chans // 2):
        at_far = lax.rem(far - step + chans // 2, chans // 2) * 2
        padded = lax.dynamic_update_slice(padded, same[step], (1 + (at_far + core) * block, 0, 0))
        padded = lax.dynamic_update_slice(padded, cross[step], (1 + (at_far + 1 - core) * block, 0, 0))

    part = filters // chans
    line_rows = own_rows * PAIR
    own_part = lax.dynamic_slice_in_dim(padded, chan * part, part, axis=1)
    pieces = jnp.stack([own_part[z * line_rows : (z + 1) * line_rows + 2] for z in range(depth)])
    pieces = lax.all_to_all(after(pieces, *along[3:5]), "filt", 0, 0, axis_index_groups=lines(depth), tiled=True)
    same = fars_gather(pieces, chans)
    sources = turned(at, same, core_swap(same, chans))

    keep, send = forward_partial(depth, chans, after(at, same, *kernels[3:5]), weights, mine, theirs)
    from_core = core_swap(send, chans)
    outputs = keep[0] + from_core[0]
    at_next = after(at, send)
    for step in range(1, chans // 2):
        moving = after(keep[step] + from_core[step], sources)
        at_next = after(at_next, moving)
        outputs += lax.ppermute(moving, "chan", [(c, (c + 2 * step) % chans) for c in range(chans)])
    outputs = outputs.astype(BF16)[None]

    near = min(3, 2 * depth - 1)
    total = input_partial(depth, 0, near, at_next, sources, kernels[:near], None)
    kept, sent = input_partial(depth, near, 2 * depth - 1, at, sources, kernels[near:], total)
    input_grad = (kept + pair_swap(sent, depth)).astype(BF16)[None]

    weight_grad = weight_gradient(depth, after(at, sent), scale, padded, mine, theirs)
    weight_grad = weight_grad.reshape((3, 3, filters, chans_in))
    return (outputs, input_grad, weight_grad)


def solution(mesh):
    return jax.shard_map(
        body,
        mesh=mesh,
        in_specs=(
            P(None, "filt", None, "chan"),
            P(None, None, "filt", "chan"),
            P(None, "chan", "filt", None),
        ),
        out_specs=(
            P(None, "chan", "filt", None),
            P(None, "filt", None, "chan"),
            P(None, None, "filt", "chan"),
        ),
        check_vma=False,
    )
```

```python
import functools
import math

import jax
import jax.numpy as jnp
from jax import lax
from jax.experimental import pallas as pl
from jax.experimental.pallas import tpu as pltpu
from jax.sharding import PartitionSpec as P

F32 = jnp.float32
BF16 = jnp.bfloat16
NT = (((1,), (1,)), ((), ()))
HBM = pl.BlockSpec(memory_space=pltpu.HBM)
VMEM = pl.BlockSpec(memory_space=pltpu.VMEM)
SMEM = pl.BlockSpec(memory_space=pltpu.SMEM)
PAIR = 2


def params(mib):
    return pltpu.CompilerParams(vmem_limit_bytes=mib << 20)


def lane_shift(value, by):
    size = value.shape[1]
    lane = lax.broadcasted_iota(jnp.int32, value.shape, 1)
    keep = lane >= by if by > 0 else lane < size + by
    return jnp.where(keep, pltpu.roll(value, by % size, 1), 0.0)


def after(value, *others):
    return lax.optimization_barrier((value,) + others)[0]


def arrivals(depth, line):
    steps = [way for step in range(1, depth) for way in (-step, step)]
    return [way for way in steps if 0 <= line + way < depth]


def arrival(along, depth, line, place):
    picked = None
    for z in range(depth):
        way = arrivals(depth, z)[place]
        value = along[2 * abs(way) - (way < 0)]
        picked = value if picked is None or value is picked else jnp.where(line == z, value, picked)
    return picked


def start_rows(at, parts, rows, sems):
    height = parts[0][0].shape[0]

    def place(spot):
        return rows.at[pl.ds(1 + spot * height, height)]

    for half in range(PAIR):
        of_side = lax.rem(at[1] + half, PAIR)
        for index, part in enumerate(parts[half]):
            spot = at[4 + index] * PAIR + of_side
            pltpu.make_async_copy(part, place(spot), sems.at[spot]).start()

    rows[0] = jnp.zeros(rows.shape[1:], rows.dtype)
    rows[rows.shape[0] - 1] = jnp.zeros(rows.shape[1:], rows.dtype)
    return lambda spot: pltpu.make_async_copy(parts[0][0], place(spot), sems.at[spot]).wait()


def forward_kernel(depth, chans, at, weights, *refs):
    count = (len(refs) - 5) // 2
    parts = (refs[:count], refs[count : 2 * count])
    keep, send, rows, taps, sems = refs[2 * count :]
    wait = start_rows(at, parts, rows, sems)
    filters, chans_in = weights.shape[2], weights.shape[3]
    for tap_row in range(3):
        for tap_col in range(3):
            taps[pl.ds(tap_col * filters, filters), pl.ds(tap_row * chans_in, chans_in)] = weights[tap_row, tap_col]
    width = rows.shape[1]
    block = keep.shape[1]
    height = parts[0][0].shape[0]
    group = min(4, block)
    far, core = at[2], at[3]
    spots = depth * PAIR
    arrived = 0
    for owner in range(chans):
        while arrived < spots and arrived * height <= (owner + 1) * block:
            wait(arrived)
            arrived += 1
        which = lax.rem(owner // 2 - far + chans // 2, chans // 2)

        def run(target):
            @pl.loop(0, block // group)
            def _(step):
                first = owner * block + step * group
                window = jnp.concatenate(
                    [rows[pl.ds(first + i, group)].reshape(group * width, chans_in) for i in range(3)], axis=1
                )
                product = lax.dot_general(taps[...], window, NT, preferred_element_type=F32)
                for row in range(group):
                    part = [
                        product[j * filters : (j + 1) * filters, row * width : (row + 1) * width] for j in range(3)
                    ]
                    target[which, step * group + row] = part[1] + lane_shift(part[0], 1) + lane_shift(part[2], -1)

        pl.when(core == owner % 2)(functools.partial(run, keep))
        pl.when(core != owner % 2)(functools.partial(run, send))


def forward_partial(depth, chans, at, weights, own, other):
    height, width, chans_in = own[0].shape
    filters = weights.shape[2]
    rows = height * depth * PAIR
    half = jax.ShapeDtypeStruct((chans // 2, rows // chans, filters, width), F32)
    return pl.pallas_call(
        functools.partial(forward_kernel, depth, chans),
        out_shape=(half, half),
        in_specs=[SMEM, VMEM] + [HBM] * (len(own) + len(other)),
        out_specs=(VMEM, VMEM),
        scratch_shapes=[
            pltpu.VMEM((rows + 2, width, chans_in), BF16),
            pltpu.VMEM((3 * filters, 3 * chans_in), BF16),
            pltpu.SemaphoreType.DMA((depth * PAIR,)),
        ],
        compiler_params=params(58),
        name="forward",
    )(at, weights, *own, *other)


def weight_kernel(depth, scale, at, cot, *refs):
    count = (len(refs) - 4) // 2
    parts = (refs[:count], refs[count : 2 * count])
    out, rows, moved, sems = refs[2 * count :]
    wait = start_rows(at, parts, rows, sems)
    filters, width = cot.shape[1], cot.shape[2]
    total = cot.shape[0] - 2
    chans_in = rows.shape[2]
    height = parts[0][0].shape[0]
    chunk = min(8, total)
    arrived = 0
    for step in range(total // chunk):
        first = step * chunk
        while arrived < depth * PAIR and arrived * height <= first + chunk:
            wait(arrived)
            arrived += 1

        @pl.loop(0, chunk)
        def _(row):
            value = cot[1 + first + row]
            wide = value.astype(F32)
            lanes = pl.ds(pl.multiple_of(row * width, width), width)
            moved[0:filters, lanes] = lane_shift(wide, -1).astype(BF16)
            moved[filters : 2 * filters, lanes] = value
            moved[2 * filters :, lanes] = lane_shift(wide, 1).astype(BF16)

        @pl.loop(0, 3)
        def _(tap_row):
            window = rows[pl.ds(first + tap_row, chunk)].reshape(chunk * width, chans_in)
            product = jnp.dot(moved[...], window, preferred_element_type=F32)
            if step == 0:
                out[tap_row] = product
            elif step == total // chunk - 1:
                out[tap_row] = (out[tap_row] + product) * scale
            else:
                out[tap_row] += product


def weight_gradient(depth, at, scale, cot, own, other):
    width, chans_in = own[0].shape[1:]
    rows, filters = cot.shape[0] - 2, cot.shape[1]
    return pl.pallas_call(
        functools.partial(weight_kernel, depth, scale),
        out_shape=jax.ShapeDtypeStruct((3, 3 * filters, chans_in), F32),
        in_specs=[SMEM, VMEM] + [HBM] * (len(own) + len(other)),
        out_specs=VMEM,
        scratch_shapes=[
            pltpu.VMEM((rows + 2, width, chans_in), BF16),
            pltpu.VMEM((3 * filters, min(8, rows) * width), BF16),
            pltpu.SemaphoreType.DMA((depth * PAIR,)),
        ],
        compiler_params=params(58),
        name="weight_gradient",
    )(at, cot, *own, *other)


def turn_kernel(same, cross, out):
    @pl.loop(0, same.shape[2])
    def _(row):
        parts = [part[far, 0, row] for far in range(same.shape[0]) for part in (same, cross)]
        out[0, row] = jnp.concatenate(parts, axis=0).T


def turned(same, cross):
    fars, depth, rows, part, width = same.shape
    filters = 2 * fars * part
    spec = pl.BlockSpec((fars, 1, rows, part, width), lambda d: (0, d, 0, 0, 0))
    return pl.pallas_call(
        turn_kernel,
        grid=(depth,),
        out_shape=jax.ShapeDtypeStruct((depth, rows, width, filters), BF16),
        in_specs=[spec, spec],
        out_specs=pl.BlockSpec((1, rows, width, filters), lambda d: (d, 0, 0, 0)),
        compiler_params=params(58),
        name="turned",
    )(same, cross)


def input_kernel(chans, index, at, cot, kernels, keep, send, source, taps, stacked, sems):
    side, far, core = at[1], at[2], at[3]
    depth, rows, width, filters = source.shape
    rows = rows - 2
    chans_in = taps.shape[3]
    copies = []
    for n in range(depth):
        copies.append(
            (
                pltpu.make_async_copy(
                    kernels.at[n, :, :, pl.ds(index * chans_in, chans_in)], taps.at[n], sems.at[n, 0]
                ),
                pltpu.make_async_copy(cot.at[n], source.at[n], sems.at[n, 1]),
            )
        )
        for copy in copies[n]:
            copy.start()
    part = filters // chans
    for n in range(depth):
        copies[n][0].wait()
        places = chans if part % 16 == 0 else 1
        for place in range(places):
            size = filters // places
            chan = 0 if places == 1 else lax.rem(far - place // 2 + chans // 2, chans // 2) * 2 + lax.rem(core + place, 2)
            of_chan = pl.ds(pl.multiple_of(chan * size, size), size)
            for i in range(3):
                for j in range(3):
                    stacked[
                        pl.ds((n * 3 + i) * filters + place * size, size), pl.ds(j * chans_in, chans_in)
                    ] = taps[n, 3 * i + j, of_chan]
    for n in range(depth):
        copies[n][1].wait()
    half = rows // PAIR
    chunk = min(4, half)
    lanes = lax.broadcasted_iota(jnp.int32, (width, chans_in), 0)

    for out, of_side in ((send, 1 - side), (keep, side)):

        @pl.loop(0, half // chunk)
        def _(step):
            first = of_side * half + step * chunk
            window = [
                source[n, pl.ds(first + 2 - i, chunk)].reshape(chunk * width, filters)
                for n in range(depth)
                for i in range(3)
            ]
            if filters % 128 == 0:
                product = jnp.dot(jnp.concatenate(window, axis=1), stacked[...], preferred_element_type=F32)
            else:
                product = sum(
                    jnp.dot(value, stacked[n * filters : (n + 1) * filters], preferred_element_type=F32)
                    for n, value in enumerate(window)
                )
            for row in range(chunk):
                here = [
                    product[row * width : (row + 1) * width, j * chans_in : (j + 1) * chans_in] for j in range(3)
                ]
                before_it = jnp.where(lanes < width - 1, pltpu.roll(here[0], width - 1, 0), 0.0)
                behind_it = jnp.where(lanes >= 1, pltpu.roll(here[2], 1, 0), 0.0)
                out[step * chunk + row] = here[1] + before_it + behind_it


def input_partial(chans, at, cot, kernels, index, parts):
    depth, rows, width, filters = cot.shape
    rows = rows - 2
    chans_in = kernels.shape[3] // parts
    half = jax.ShapeDtypeStruct((rows // PAIR, width, chans_in), F32)
    return pl.pallas_call(
        functools.partial(input_kernel, chans, index),
        out_shape=(half, half),
        in_specs=[SMEM, HBM, HBM],
        out_specs=(VMEM, VMEM),
        scratch_shapes=[
            pltpu.VMEM(cot.shape, BF16),
            pltpu.VMEM(kernels.shape[:3] + (chans_in,), BF16),
            pltpu.VMEM((depth * 3 * filters, 3 * chans_in), BF16),
            pltpu.SemaphoreType.DMA((depth, 2)),
        ],
        compiler_params=params(58),
        name="input_gradient",
    )(at, cot, kernels)


def fars_gather(value, chans):
    got = [value]
    for step in range(1, chans // 2):
        got.append(lax.ppermute(value, "chan", [(c, (c + 2 * step) % chans) for c in range(chans)]))
    return jnp.stack(got)


def lines(depth):
    return [[z * PAIR + y for z in range(depth)] for y in range(PAIR)]


def line_steps(step, depth):
    up = [(z * PAIR + y, (z + 1) * PAIR + y) for z in range(step - 1, depth - 1) for y in range(PAIR)]
    down = [(z * PAIR + y, (z - 1) * PAIR + y) for z in range(1, depth - step + 1) for y in range(PAIR)]
    return up, down


def line_step(along, step, depth):
    up, down = line_steps(step, depth)
    below, above = along[0 if step == 1 else -2], along[0 if step == 1 else -1]
    return [lax.ppermute(below, "filt", up), lax.ppermute(above, "filt", down)]


def core_swap(value, chans):
    return lax.ppermute(value, "chan", [(c, c ^ 1) for c in range(chans)])


def pair_swap(value, depth):
    pairs = [(z * PAIR + y, z * PAIR + 1 - y) for z in range(depth) for y in range(PAIR)]
    return lax.ppermute(value, "filt", pairs)


def body(inputs, weights, cotangent):
    chans, filts = lax.axis_size("chan"), lax.axis_size("filt")
    depth = filts // PAIR
    chan, filt = lax.axis_index("chan"), lax.axis_index("filt")
    line, side = filt // PAIR, filt % PAIR
    far, core = chan // 2, chan % 2
    spots = jnp.asarray([[z] + [z + way for way in arrivals(depth, z)] for z in range(depth)], jnp.int32)
    at = jnp.concatenate([jnp.stack([line, side, far, core]).astype(jnp.int32), spots[line]])
    own_rows, width, chans_in = inputs.shape[1:]
    block, filters = cotangent.shape[1], cotangent.shape[2]
    height = own_rows * filts
    scale = 1.0 / math.sqrt(inputs.shape[0] * height * width)

    kernels = lax.all_gather(weights, "filt", axis=0, axis_index_groups=lines(depth))
    kernels = kernels.reshape((depth, 9) + weights.shape[2:])

    along, mine, theirs = [inputs[0]], [inputs[0]], [pair_swap(inputs[0], depth)]
    same, gate = fars_gather(cotangent[0], chans), []
    for step in range(1, depth + 1):
        along = list(lax.optimization_barrier(tuple(along + gate)))[: len(along)]
        if step < depth:
            along += line_step(along, step, depth)
        if step == 1:
            gate = along[1:] + theirs + [same]
            continue
        mine.append(arrival(along, depth, line, step - 2))
        theirs.append(pair_swap(mine[-1], depth))
        if step == 2:
            cross = core_swap(after(same, *gate), chans)
        gate = along[-2:] + theirs[-1:] + [cross]

    padded = jnp.zeros((height + 2, filters, width), BF16)
    for step in range(chans // 2):
        at_far = lax.rem(far - step + chans // 2, chans // 2) * 2
        padded = lax.dynamic_update_slice(padded, same[step], (1 + (at_far + core) * block, 0, 0))
        padded = lax.dynamic_update_slice(padded, cross[step], (1 + (at_far + 1 - core) * block, 0, 0))

    part = filters // chans
    line_rows = own_rows * PAIR
    own_part = lax.dynamic_slice_in_dim(padded, chan * part, part, axis=1)
    pieces = jnp.stack([own_part[z * line_rows : (z + 1) * line_rows + 2] for z in range(depth)])
    pieces = lax.all_to_all(after(pieces, *along[-2:]), "filt", 0, 0, axis_index_groups=lines(depth), tiled=True)
    same = fars_gather(pieces, chans)
    sources = turned(same, core_swap(same, chans))

    if part % 16:
        order = [(far - c // 2 + chans // 2) % (chans // 2) * 2 + (core + c) % 2 for c in range(chans)]
        split = kernels.reshape((depth, 9, chans, part, chans_in))
        kernels = jnp.take(split, jnp.stack(order), axis=2).reshape(kernels.shape)

    keep, send = forward_partial(depth, chans, after(at, pieces), weights, mine, theirs)
    from_core = core_swap(send, chans)
    outputs = keep[0] + from_core[0]
    at_next = after(at, send)
    for step in range(1, chans // 2):
        moving = keep[step] + from_core[step]
        at_next = after(at_next, moving)
        outputs += lax.ppermute(moving, "chan", [(c, (c + 2 * step) % chans) for c in range(chans)])
    outputs = outputs.astype(BF16)[None]

    weight_grad = weight_gradient(depth, at_next, scale, padded, mine, theirs)
    weight_grad = weight_grad.reshape((3, 3, filters, chans_in))

    at_next = after(at_next, weight_grad)
    parts = 1
    input_grad = []
    for index in range(parts):
        kept, sent = input_partial(chans, at_next, sources, kernels, index, parts)
        at_next = after(at_next, sent)
        input_grad.append((kept + pair_swap(sent, depth)).astype(BF16))
    input_grad = jnp.concatenate(input_grad, axis=2)[None]
    return (outputs, input_grad, weight_grad)


def solution(mesh):
    return jax.shard_map(
        body,
        mesh=mesh,
        in_specs=(
            P(None, "filt", None, "chan"),
            P(None, None, "filt", "chan"),
            P(None, "chan", "filt", None),
        ),
        out_specs=(
            P(None, "chan", "filt", None),
            P(None, "filt", None, "chan"),
            P(None, None, "filt", "chan"),
        ),
        check_vma=False,
    )
```

```python
import functools
import math

import jax
import jax.numpy as jnp
from jax import lax
from jax.experimental import pallas as pl
from jax.experimental.pallas import tpu as pltpu
from jax.sharding import PartitionSpec as P

F32 = jnp.float32
BF16 = jnp.bfloat16
NT = (((1,), (1,)), ((), ()))
HBM = pl.BlockSpec(memory_space=pltpu.HBM)
VMEM = pl.BlockSpec(memory_space=pltpu.VMEM)
SMEM = pl.BlockSpec(memory_space=pltpu.SMEM)
PAIR = 2


def params(mib):
    return pltpu.CompilerParams(vmem_limit_bytes=mib << 20)


def cost(flops, moved):
    return pl.CostEstimate(flops=int(flops), bytes_accessed=int(moved), transcendentals=0)


def lane_shift(value, by):
    size = value.shape[1]
    lane = lax.broadcasted_iota(jnp.int32, value.shape, 1)
    keep = lane >= by if by > 0 else lane < size + by
    return jnp.where(keep, pltpu.roll(value, by % size, 1), 0.0)


def after(value, *others):
    return lax.optimization_barrier((value,) + others)[0]


def arrivals(depth, line):
    steps = [way for step in range(1, depth) for way in (-step, step)]
    return [way for way in steps if 0 <= line + way < depth]


def arrival(along, depth, line, place):
    picked = None
    for z in range(depth):
        way = arrivals(depth, z)[place]
        value = along[2 * abs(way) - (way < 0)]
        picked = value if picked is None or value is picked else jnp.where(line == z, value, picked)
    return picked


def start_rows(at, parts, rows, sems):
    height = parts[0][0].shape[0]

    def place(spot):
        return rows.at[pl.ds(1 + spot * height, height)]

    for half in range(PAIR):
        of_side = lax.rem(at[1] + half, PAIR)
        for index, part in enumerate(parts[half]):
            spot = at[4 + index] * PAIR + of_side
            pltpu.make_async_copy(part, place(spot), sems.at[spot]).start()

    rows[0] = jnp.zeros(rows.shape[1:], rows.dtype)
    rows[rows.shape[0] - 1] = jnp.zeros(rows.shape[1:], rows.dtype)
    return lambda spot: pltpu.make_async_copy(parts[0][0], place(spot), sems.at[spot]).wait()


def forward_kernel(depth, chans, at, weights, *refs):
    count = (len(refs) - 5) // 2
    parts = (refs[:count], refs[count : 2 * count])
    keep, send, rows, taps, sems = refs[2 * count :]
    wait = start_rows(at, parts, rows, sems)
    filters, chans_in = weights.shape[2], weights.shape[3]
    for tap_row in range(3):
        for tap_col in range(3):
            taps[pl.ds(tap_col * filters, filters), pl.ds(tap_row * chans_in, chans_in)] = weights[tap_row, tap_col]
    width = rows.shape[1]
    block = keep.shape[1]
    height = parts[0][0].shape[0]
    group = min(4, block)
    per_block = block // group
    far, core = at[2], at[3]
    for spot in range(depth * PAIR):
        wait(spot)

    @pl.loop(0, (chans // 2) * per_block)
    def _(step):
        which, group_at = step // per_block, step % per_block
        for target, of_core in ((send, 1 - core), (keep, core)):
            first = (lax.rem(far + which, chans // 2) * 2 + of_core) * block + group_at * group
            window = jnp.concatenate(
                [rows[pl.ds(first + i, group)].reshape(group * width, chans_in) for i in range(3)], axis=1
            )
            product = lax.dot_general(taps[...], window, NT, preferred_element_type=F32)
            for row in range(group):
                part = [
                    product[j * filters : (j + 1) * filters, row * width : (row + 1) * width] for j in range(3)
                ]
                target[which, group_at * group + row] = part[1] + lane_shift(part[0], 1) + lane_shift(part[2], -1)


def forward_partial(depth, chans, at, weights, own, other):
    height, width, chans_in = own[0].shape
    filters = weights.shape[2]
    rows = height * depth * PAIR
    half = jax.ShapeDtypeStruct((chans // 2, rows // chans, filters, width), F32)
    return pl.pallas_call(
        functools.partial(forward_kernel, depth, chans),
        out_shape=(half, half),
        in_specs=[SMEM, VMEM] + [HBM] * (len(own) + len(other)),
        out_specs=(VMEM, VMEM),
        scratch_shapes=[
            pltpu.VMEM((rows + 2, width, chans_in), BF16),
            pltpu.VMEM((3 * filters, 3 * chans_in), BF16),
            pltpu.SemaphoreType.DMA((depth * PAIR,)),
        ],
        compiler_params=params(58),
        cost_estimate=cost(18 * rows * width * chans_in * filters, 4 * rows * width * filters + 2 * rows * width * chans_in),
        name="forward",
    )(at, weights, *own, *other)


def weight_kernel(depth, scale, at, cot, *refs):
    count = (len(refs) - 4) // 2
    parts = (refs[:count], refs[count : 2 * count])
    out, rows, moved, sems = refs[2 * count :]
    wait = start_rows(at, parts, rows, sems)
    filters, width = cot.shape[1], cot.shape[2]
    total = cot.shape[0] - 2
    chans_in = rows.shape[2]
    chunk = min(8, total)
    for spot in range(depth * PAIR):
        wait(spot)
    out[...] = jnp.zeros(out.shape, F32)

    @pl.loop(0, total // chunk)
    def _(step):
        first = step * chunk
        for row in range(chunk):
            value = cot[1 + first + row]
            wide = value.astype(F32)
            lanes = pl.ds(row * width, width)
            moved[0:filters, lanes] = lane_shift(wide, -1).astype(BF16)
            moved[filters : 2 * filters, lanes] = value
            moved[2 * filters :, lanes] = lane_shift(wide, 1).astype(BF16)
        for tap_row in range(3):
            window = rows[pl.ds(first + tap_row, chunk)].reshape(chunk * width, chans_in)
            out[tap_row] += jnp.dot(moved[...], window, preferred_element_type=F32)

    out[...] = out[...] * scale


def weight_gradient(depth, at, scale, cot, own, other):
    width, chans_in = own[0].shape[1:]
    rows, filters = cot.shape[0] - 2, cot.shape[1]
    return pl.pallas_call(
        functools.partial(weight_kernel, depth, scale),
        out_shape=jax.ShapeDtypeStruct((3, 3 * filters, chans_in), F32),
        in_specs=[SMEM, VMEM] + [HBM] * (len(own) + len(other)),
        out_specs=VMEM,
        scratch_shapes=[
            pltpu.VMEM((rows + 2, width, chans_in), BF16),
            pltpu.VMEM((3 * filters, min(8, rows) * width), BF16),
            pltpu.SemaphoreType.DMA((depth * PAIR,)),
        ],
        compiler_params=params(58),
        cost_estimate=cost(18 * rows * width * chans_in * filters, 2 * rows * width * (filters + chans_in)),
        name="weight_gradient",
    )(at, cot, *own, *other)


def turn_kernel(same, cross, out):
    rows = same.shape[1]
    unroll = max(n for n in (1, 2, 3, 6) if rows % n == 0)

    @pl.loop(0, rows // unroll)
    def _(step):
        for n in range(unroll):
            row = step * unroll + n
            out[0, row] = jnp.concatenate([same[0, row], cross[0, row]], axis=0).T


def turned(same, cross):
    depth, rows, part, width = same.shape
    spec = pl.BlockSpec((1, rows, part, width), lambda d: (d, 0, 0, 0))
    return pl.pallas_call(
        turn_kernel,
        grid=(depth,),
        out_shape=jax.ShapeDtypeStruct((depth, rows, width, 2 * part), BF16),
        in_specs=[spec, spec],
        out_specs=pl.BlockSpec((1, rows, width, 2 * part), lambda d: (d, 0, 0, 0)),
        compiler_params=params(58),
        cost_estimate=cost(0, 8 * depth * rows * width * part),
        name="turned",
    )(same, cross)


def input_kernel(index, at, cot, kernels, keep, send, source, taps, stacked, sems):
    side, core = at[1], at[3]
    depth, rows, width, filters = source.shape
    rows = rows - 2
    chans_in = taps.shape[3]
    copies = []
    for n in range(depth):
        copies.append(
            (
                pltpu.make_async_copy(
                    kernels.at[n, :, :, pl.ds(index * chans_in, chans_in)], taps.at[n], sems.at[n, 0]
                ),
                pltpu.make_async_copy(cot.at[n], source.at[n], sems.at[n, 1]),
            )
        )
        for copy in copies[n]:
            copy.start()
    size = filters // 2
    for n in range(depth):
        copies[n][0].wait()
        for place in range(2):
            of_core = pl.ds(pl.multiple_of(lax.rem(core + place, 2) * size, size), size)
            for i in range(3):
                for j in range(3):
                    stacked[
                        pl.ds((n * 3 + i) * filters + place * size, size), pl.ds(j * chans_in, chans_in)
                    ] = taps[n, 3 * i + j, of_core]
    for n in range(depth):
        copies[n][1].wait()
    half = rows // PAIR
    chunk = min(8, half)
    lanes = lax.broadcasted_iota(jnp.int32, (width, chans_in), 0)

    for out, of_side in ((send, 1 - side), (keep, side)):

        @pl.loop(0, half // chunk)
        def _(step):
            first = of_side * half + step * chunk
            window = [
                source[n, pl.ds(first + 2 - i, chunk)].reshape(chunk * width, filters)
                for n in range(depth)
                for i in range(3)
            ]
            if filters % 128 == 0:
                product = jnp.dot(jnp.concatenate(window, axis=1), stacked[...], preferred_element_type=F32)
            else:
                product = sum(
                    jnp.dot(value, stacked[n * filters : (n + 1) * filters], preferred_element_type=F32)
                    for n, value in enumerate(window)
                )
            for row in range(chunk):
                here = [
                    product[row * width : (row + 1) * width, j * chans_in : (j + 1) * chans_in] for j in range(3)
                ]
                before_it = jnp.where(lanes < width - 1, pltpu.roll(here[0], width - 1, 0), 0.0)
                behind_it = jnp.where(lanes >= 1, pltpu.roll(here[2], 1, 0), 0.0)
                out[step * chunk + row] = here[1] + before_it + behind_it


def input_partial(at, cot, kernels, index, parts):
    depth, rows, width, filters = cot.shape
    rows = rows - 2
    chans_in = kernels.shape[3] // parts
    half = jax.ShapeDtypeStruct((rows // PAIR, width, chans_in), F32)
    return pl.pallas_call(
        functools.partial(input_kernel, index),
        out_shape=(half, half),
        in_specs=[SMEM, HBM, HBM],
        out_specs=(VMEM, VMEM),
        scratch_shapes=[
            pltpu.VMEM(cot.shape, BF16),
            pltpu.VMEM(kernels.shape[:3] + (chans_in,), BF16),
            pltpu.VMEM((depth * 3 * filters, 3 * chans_in), BF16),
            pltpu.SemaphoreType.DMA((depth, 2)),
        ],
        compiler_params=params(58),
        cost_estimate=cost(
            18 * rows * width * chans_in * filters * depth, 2 * depth * filters * ((rows + 2) * width + 9 * chans_in)
        ),
        name="input_gradient",
    )(at, cot, kernels)


def fars_gather(value, chans):
    got = [value]
    for step in range(1, chans // 2):
        got.append(lax.ppermute(value, "chan", [(c, (c + 2 * step) % chans) for c in range(chans)]))
    return jnp.stack(got)


def lines(depth):
    return [[z * PAIR + y for z in range(depth)] for y in range(PAIR)]


def line_steps(step, depth):
    up = [(z * PAIR + y, (z + 1) * PAIR + y) for z in range(step - 1, depth - 1) for y in range(PAIR)]
    down = [(z * PAIR + y, (z - 1) * PAIR + y) for z in range(1, depth - step + 1) for y in range(PAIR)]
    return up, down


def line_step(along, step, depth):
    up, down = line_steps(step, depth)
    below, above = along[0 if step == 1 else -2], along[0 if step == 1 else -1]
    return [lax.ppermute(below, "filt", up), lax.ppermute(above, "filt", down)]


def core_swap(value, chans):
    return lax.ppermute(value, "chan", [(c, c ^ 1) for c in range(chans)])


def pair_swap(value, depth):
    pairs = [(z * PAIR + y, z * PAIR + 1 - y) for z in range(depth) for y in range(PAIR)]
    return lax.ppermute(value, "filt", pairs)


def body(inputs, weights, cotangent):
    chans, filts = lax.axis_size("chan"), lax.axis_size("filt")
    depth = filts // PAIR
    chan, filt = lax.axis_index("chan"), lax.axis_index("filt")
    line, side = filt // PAIR, filt % PAIR
    far, core = chan // 2, chan % 2
    spots = jnp.asarray([[z] + [z + way for way in arrivals(depth, z)] for z in range(depth)], jnp.int32)
    at = jnp.concatenate([jnp.stack([line, side, far, core]).astype(jnp.int32), spots[line]])
    own_rows, width, chans_in = inputs.shape[1:]
    block, filters = cotangent.shape[1], cotangent.shape[2]
    height = own_rows * filts
    scale = 1.0 / math.sqrt(inputs.shape[0] * height * width)

    kernels = lax.all_gather(weights, "filt", axis=0, axis_index_groups=lines(depth))
    kernels = kernels.reshape((depth, 9) + weights.shape[2:])

    along, mine, theirs = [inputs[0]], [inputs[0]], [pair_swap(inputs[0], depth)]
    same, gate = fars_gather(cotangent[0], chans), []
    for step in range(1, depth + 1):
        along = list(lax.optimization_barrier(tuple(along + gate)))[: len(along)]
        if step < depth:
            along += line_step(along, step, depth)
        if step == 1:
            gate = along[1:] + theirs + [same]
            gates = [gate]
            continue
        mine.append(arrival(along, depth, line, step - 2))
        theirs.append(pair_swap(mine[-1], depth))
        if step == 2:
            cross = core_swap(after(same, *gate), chans)
        gate = along[-2:] + theirs[-1:] + [cross]
        gates.append(gate)

    padded = jnp.zeros((height + 2, filters, width), BF16)
    for step in range(chans // 2):
        at_far = lax.rem(far - step + chans // 2, chans // 2) * 2
        padded = lax.dynamic_update_slice(padded, same[step], (1 + (at_far + core) * block, 0, 0))
        padded = lax.dynamic_update_slice(padded, cross[step], (1 + (at_far + 1 - core) * block, 0, 0))

    part = filters // 2
    line_rows = own_rows * PAIR
    own_part = lax.dynamic_slice_in_dim(padded, core * part, part, axis=1)
    pieces = jnp.stack([own_part[z * line_rows : (z + 1) * line_rows + 2] for z in range(depth)])
    pieces = lax.all_to_all(after(pieces, *gates[1]), "filt", 0, 0, axis_index_groups=lines(depth), tiled=True)
    sources = turned(pieces, core_swap(pieces, chans))

    keep, send = forward_partial(depth, chans, after(at, pieces), weights, mine, theirs)
    from_core = core_swap(send, chans)
    outputs = keep[0] + from_core[0]
    at_next = after(at, send)
    for step in range(1, chans // 2):
        moving = keep[step] + from_core[step]
        at_next = after(at_next, moving)
        outputs += lax.ppermute(moving, "chan", [(c, (c + 2 * step) % chans) for c in range(chans)])
    outputs = outputs.astype(BF16)[None]

    parts = 1
    input_grad = []
    for index in range(parts):
        kept, sent = input_partial(at_next, sources, kernels, index, parts)
        at_next = after(at_next, sent)
        input_grad.append((kept + pair_swap(sent, depth)).astype(BF16))
    input_grad = jnp.concatenate(input_grad, axis=2)[None]

    weight_grad = weight_gradient(depth, after(at_next, outputs), scale, padded, mine, theirs)
    weight_grad = weight_grad.reshape((3, 3, filters, chans_in))
    return (outputs, input_grad, weight_grad)


def solution(mesh):
    return jax.shard_map(
        body,
        mesh=mesh,
        in_specs=(
            P(None, "filt", None, "chan"),
            P(None, None, "filt", "chan"),
            P(None, "chan", "filt", None),
        ),
        out_specs=(
            P(None, "chan", "filt", None),
            P(None, "filt", None, "chan"),
            P(None, None, "filt", "chan"),
        ),
        check_vma=False,
    )
```

```python
import functools
import math

import jax
import jax.numpy as jnp
from jax import lax
from jax.experimental import pallas as pl
from jax.experimental.pallas import tpu as pltpu
from jax.sharding import PartitionSpec as P

F32 = jnp.float32
BF16 = jnp.bfloat16
NT = (((1,), (1,)), ((), ()))
HBM = pl.BlockSpec(memory_space=pltpu.HBM)
VMEM = pl.BlockSpec(memory_space=pltpu.VMEM)
SMEM = pl.BlockSpec(memory_space=pltpu.SMEM)
PAIR = 2


def params(mib):
    return pltpu.CompilerParams(vmem_limit_bytes=mib << 20)


def cost(flops, moved):
    return pl.CostEstimate(flops=int(flops), bytes_accessed=int(moved), transcendentals=0)


def lane_shift(value, by):
    size = value.shape[1]
    lane = lax.broadcasted_iota(jnp.int32, value.shape, 1)
    keep = lane >= by if by > 0 else lane < size + by
    return jnp.where(keep, pltpu.roll(value, by % size, 1), 0.0)


def after(value, *others):
    return lax.optimization_barrier((value,) + others)[0]


def start_rows(at, along, swapped, rows, sems):
    depth, height = along.shape[:2]
    line, side = at[0], at[1]

    def copy(source, block, of_side):
        spot = block * PAIR + of_side
        return pltpu.make_async_copy(source, rows.at[pl.ds(1 + spot * height, height)], sems.at[spot])

    for block in range(depth):
        copy(along.at[block], block, side).start()
        copy(swapped[block], lax.rem(line + block, depth), 1 - side).start()

    rows[0] = jnp.zeros(rows.shape[1:], rows.dtype)
    rows[rows.shape[0] - 1] = jnp.zeros(rows.shape[1:], rows.dtype)
    return lambda spot: copy(along.at[0], spot // PAIR, spot % PAIR).wait()


def forward_kernel(depth, chans, at, weights, *refs):
    along, swapped = refs[0], refs[1 : depth + 1]
    keep, send, rows, taps, sems = refs[depth + 1 :]
    wait = start_rows(at, along, swapped, rows, sems)
    filters, chans_in = weights.shape[2], weights.shape[3]
    for tap_row in range(3):
        for tap_col in range(3):
            taps[pl.ds(tap_col * filters, filters), pl.ds(tap_row * chans_in, chans_in)] = weights[tap_row, tap_col]
    width = rows.shape[1]
    block = keep.shape[1]
    group = min(4, block)
    per_block = block // group
    far, core = at[2], at[3]
    for spot in range(depth * PAIR):
        wait(spot)

    @pl.loop(0, (chans // 2) * per_block)
    def _(step):
        which, group_at = step // per_block, step % per_block
        for target, of_core in ((send, 1 - core), (keep, core)):
            first = (lax.rem(far + which, chans // 2) * 2 + of_core) * block + group_at * group
            window = jnp.concatenate(
                [rows[pl.ds(first + i, group)].reshape(group * width, chans_in) for i in range(3)], axis=1
            )
            product = lax.dot_general(taps[...], window, NT, preferred_element_type=F32)
            for row in range(group):
                part = [
                    product[j * filters : (j + 1) * filters, row * width : (row + 1) * width] for j in range(3)
                ]
                target[which, group_at * group + row] = part[1] + lane_shift(part[0], 1) + lane_shift(part[2], -1)


def forward_partial(chans, at, weights, along, swapped):
    depth, height, width, chans_in = along.shape
    filters = weights.shape[2]
    rows = height * depth * PAIR
    half = jax.ShapeDtypeStruct((chans // 2, rows // chans, filters, width), F32)
    return pl.pallas_call(
        functools.partial(forward_kernel, depth, chans),
        out_shape=(half, half),
        in_specs=[SMEM, VMEM] + [HBM] * (depth + 1),
        out_specs=(VMEM, VMEM),
        scratch_shapes=[
            pltpu.VMEM((rows + 2, width, chans_in), BF16),
            pltpu.VMEM((3 * filters, 3 * chans_in), BF16),
            pltpu.SemaphoreType.DMA((depth * PAIR,)),
        ],
        compiler_params=params(58),
        cost_estimate=cost(18 * rows * width * chans_in * filters, 4 * rows * width * filters + 2 * rows * width * chans_in),
        name="forward",
    )(at, weights, along, *swapped)


def weight_kernel(depth, scale, at, cot, *refs):
    along, swapped = refs[0], refs[1 : depth + 1]
    out, rows, moved, sems = refs[depth + 1 :]
    wait = start_rows(at, along, swapped, rows, sems)
    filters, width = cot.shape[1], cot.shape[2]
    total = cot.shape[0] - 2
    chans_in = rows.shape[2]
    chunk = min(8, total)
    for spot in range(depth * PAIR):
        wait(spot)
    out[...] = jnp.zeros(out.shape, F32)

    @pl.loop(0, total // chunk)
    def _(step):
        first = step * chunk
        for row in range(chunk):
            value = cot[1 + first + row]
            wide = value.astype(F32)
            lanes = pl.ds(row * width, width)
            moved[0:filters, lanes] = lane_shift(wide, -1).astype(BF16)
            moved[filters : 2 * filters, lanes] = value
            moved[2 * filters :, lanes] = lane_shift(wide, 1).astype(BF16)
        for tap_row in range(3):
            window = rows[pl.ds(first + tap_row, chunk)].reshape(chunk * width, chans_in)
            out[tap_row] += jnp.dot(moved[...], window, preferred_element_type=F32)

    out[...] = out[...] * scale


def weight_gradient(at, scale, cot, along, swapped):
    depth, _, width, chans_in = along.shape
    rows, filters = cot.shape[0] - 2, cot.shape[1]
    return pl.pallas_call(
        functools.partial(weight_kernel, depth, scale),
        out_shape=jax.ShapeDtypeStruct((3, 3 * filters, chans_in), F32),
        in_specs=[SMEM, VMEM] + [HBM] * (depth + 1),
        out_specs=VMEM,
        scratch_shapes=[
            pltpu.VMEM((rows + 2, width, chans_in), BF16),
            pltpu.VMEM((3 * filters, min(8, rows) * width), BF16),
            pltpu.SemaphoreType.DMA((depth * PAIR,)),
        ],
        compiler_params=params(58),
        cost_estimate=cost(18 * rows * width * chans_in * filters, 2 * rows * width * (filters + chans_in)),
        name="weight_gradient",
    )(at, cot, along, *swapped)


def turn_kernel(same, cross, out):
    fars, _, rows = same.shape[:3]
    unroll = max(n for n in (1, 2, 3, 6) if rows % n == 0)

    @pl.loop(0, rows // unroll)
    def _(step):
        for n in range(unroll):
            row = step * unroll + n
            out[0, row] = jnp.concatenate([part[far, 0, row] for far in range(fars) for part in (same, cross)], axis=0).T


def turned(same, cross):
    fars, depth, rows, part, width = same.shape
    filters = 2 * fars * part
    spec = pl.BlockSpec((fars, 1, rows, part, width), lambda d: (0, d, 0, 0, 0))
    return pl.pallas_call(
        turn_kernel,
        grid=(depth,),
        out_shape=jax.ShapeDtypeStruct((depth, rows, width, filters), BF16),
        in_specs=[spec, spec],
        out_specs=pl.BlockSpec((1, rows, width, filters), lambda d: (d, 0, 0, 0)),
        compiler_params=params(58),
        cost_estimate=cost(0, 4 * depth * rows * width * filters),
        name="turned",
    )(same, cross)


def input_kernel(chans, at, cot, *refs):
    line, side, far, core = at[0], at[1], at[2], at[3]
    kernels = refs[:-6]
    keep, send, source, taps, stacked, sems = refs[-6:]
    depth, rows, width, filters = source.shape
    rows = rows - 2
    chans_in = taps.shape[3]
    ways = [0] + [way for step in range(1, depth) for way in (-step, step)]
    for kernel, way in zip(kernels, ways):

        @pl.when(jnp.logical_and(line + way >= 0, line + way < depth))
        def _():
            pltpu.make_async_copy(kernel, taps.at[line + way], sems.at[line + way, 0]).start()

    copies = []
    for n in range(depth):
        copies.append(
            (
                pltpu.make_async_copy(kernels[0], taps.at[n], sems.at[n, 0]),
                pltpu.make_async_copy(cot.at[n], source.at[n], sems.at[n, 1]),
            )
        )
        copies[n][1].start()
    part = filters // chans
    places = chans if part % 16 == 0 else 1
    size = filters // places
    for n in range(depth):
        copies[n][0].wait()
        for place in range(places):
            chan = lax.rem(far - place // 2 + chans // 2, chans // 2) * 2 + lax.rem(core + place, 2)
            of_chan = pl.ds(0 if places == 1 else pl.multiple_of(chan * size, size), size)
            for i in range(3):
                for j in range(3):
                    stacked[
                        pl.ds((n * 3 + i) * filters + place * size, size), pl.ds(j * chans_in, chans_in)
                    ] = taps[n, 3 * i + j, of_chan]
    for n in range(depth):
        copies[n][1].wait()
    half = rows // PAIR
    chunk = min(8, half)
    lanes = lax.broadcasted_iota(jnp.int32, (width, chans_in), 0)

    for out, of_side in ((send, 1 - side), (keep, side)):

        @pl.loop(0, half // chunk)
        def _(step):
            first = of_side * half + step * chunk
            window = [
                source[n, pl.ds(first + 2 - i, chunk)].reshape(chunk * width, filters)
                for n in range(depth)
                for i in range(3)
            ]
            if filters % 128 == 0:
                product = jnp.dot(jnp.concatenate(window, axis=1), stacked[...], preferred_element_type=F32)
            else:
                product = sum(
                    jnp.dot(value, stacked[n * filters : (n + 1) * filters], preferred_element_type=F32)
                    for n, value in enumerate(window)
                )
            for row in range(chunk):
                here = [
                    product[row * width : (row + 1) * width, j * chans_in : (j + 1) * chans_in] for j in range(3)
                ]
                before_it = jnp.where(lanes < width - 1, pltpu.roll(here[0], width - 1, 0), 0.0)
                behind_it = jnp.where(lanes >= 1, pltpu.roll(here[2], 1, 0), 0.0)
                out[step * chunk + row] = here[1] + before_it + behind_it


def input_partial(chans, at, cot, kernels):
    depth, rows, width, filters = cot.shape
    rows = rows - 2
    chans_in = kernels[0].shape[2]
    half = jax.ShapeDtypeStruct((rows // PAIR, width, chans_in), F32)
    return pl.pallas_call(
        functools.partial(input_kernel, chans),
        out_shape=(half, half),
        in_specs=[SMEM, HBM] + [HBM] * len(kernels),
        out_specs=(VMEM, VMEM),
        scratch_shapes=[
            pltpu.VMEM(cot.shape, BF16),
            pltpu.VMEM((depth,) + kernels[0].shape, BF16),
            pltpu.VMEM((depth * 3 * filters, 3 * chans_in), BF16),
            pltpu.SemaphoreType.DMA((depth, 2)),
        ],
        compiler_params=params(58),
        cost_estimate=cost(
            18 * rows * width * chans_in * filters * depth, 2 * depth * filters * ((rows + 2) * width + 9 * chans_in)
        ),
        name="input_gradient",
    )(at, cot, *kernels)


def fars_gather(value, chans):
    got = [value]
    for step in range(1, chans // 2):
        got.append(lax.ppermute(value, "chan", [(c, (c + 2 * step) % chans) for c in range(chans)]))
    return jnp.stack(got)


def lines(depth):
    return [[z * PAIR + y for z in range(depth)] for y in range(PAIR)]


def line_step(shards, step, depth):
    up = [(z * PAIR + y, (z + 1) * PAIR + y) for z in range(step - 1, depth - 1) for y in range(PAIR)]
    down = [(z * PAIR + y, (z - 1) * PAIR + y) for z in range(1, depth - step + 1) for y in range(PAIR)]
    below, above = shards[0 if step == 1 else -2], shards[0 if step == 1 else -1]
    return [lax.ppermute(below, "filt", up), lax.ppermute(above, "filt", down)]


def core_swap(value, chans):
    return lax.ppermute(value, "chan", [(c, c ^ 1) for c in range(chans)])


def pair_swap(value, depth):
    pairs = [(z * PAIR + y, z * PAIR + 1 - y) for z in range(depth) for y in range(PAIR)]
    return lax.ppermute(value, "filt", pairs)


def body(inputs, weights, cotangent):
    chans, filts = lax.axis_size("chan"), lax.axis_size("filt")
    depth = filts // PAIR
    chan, filt = lax.axis_index("chan"), lax.axis_index("filt")
    line, side = filt // PAIR, filt % PAIR
    far, core = chan // 2, chan % 2
    at = jnp.stack([line, side, far, core]).astype(jnp.int32)
    own_rows, width, chans_in = inputs.shape[1:]
    block, filters = cotangent.shape[1], cotangent.shape[2]
    height = own_rows * filts
    scale = 1.0 / math.sqrt(inputs.shape[0] * height * width)

    along = lax.all_gather(inputs[0], "filt", axis=0, axis_index_groups=lines(depth))
    same = fars_gather(cotangent[0], chans)
    cross = core_swap(same, chans)
    padded = jnp.zeros((height + 2, filters, width), BF16)
    for step in range(chans // 2):
        at_far = lax.rem(far - step + chans // 2, chans // 2) * 2
        padded = lax.dynamic_update_slice(padded, same[step], (1 + (at_far + core) * block, 0, 0))
        padded = lax.dynamic_update_slice(padded, cross[step], (1 + (at_far + 1 - core) * block, 0, 0))

    part = filters // chans
    line_rows = own_rows * PAIR
    own_part = lax.dynamic_slice_in_dim(padded, chan * part, part, axis=1)
    pieces = jnp.stack([own_part[z * line_rows : (z + 1) * line_rows + 2] for z in range(depth)])
    pieces = lax.all_to_all(pieces, "filt", 0, 0, axis_index_groups=lines(depth), tiled=True)

    kernels = [weights.reshape((9,) + weights.shape[2:])]
    if part % 16:
        order = [(far - c // 2 + chans // 2) % (chans // 2) * 2 + (core + c) % 2 for c in range(chans)]
        split = kernels[0].reshape((9, chans, part, chans_in))
        kernels = [jnp.take(split, jnp.stack(order), axis=1).reshape(kernels[0].shape)]
    kernels += line_step(kernels, 1, depth)

    swapped = [pair_swap(inputs[0], depth)]
    same, gate = None, [pieces, swapped[0]]
    for step in range(1, depth):
        if step + 1 < depth:
            along, below, above, *gate = lax.optimization_barrier([along] + kernels[-2:] + gate)
            if same is None:
                same = fars_gather(gate[0], chans)
                gate = [same]
            kernels = kernels[:-2] + [below, above]
            kernels += line_step(kernels, step + 1, depth)
            gate = gate[:1]
        swapped.append(pair_swap(along[lax.rem(line + step, depth)], depth))
        gate.append(swapped[-1])
    same = fars_gather(pieces, chans) if same is None else same
    sources = turned(same, core_swap(same, chans))

    keep, send = forward_partial(chans, after(at, sources, *kernels[-2:]), weights, along, swapped)
    from_core = core_swap(send, chans)
    outputs = keep[0] + from_core[0]
    at_next = after(at, send)
    for step in range(1, chans // 2):
        moving = keep[step] + from_core[step]
        outputs += lax.ppermute(moving, "chan", [(c, (c + 2 * step) % chans) for c in range(chans)])
    outputs = outputs.astype(BF16)[None]

    kept, sent = input_partial(chans, at_next, sources, kernels)
    input_grad = (kept + pair_swap(sent, depth)).astype(BF16)[None]

    weight_grad = weight_gradient(after(at_next, sent), scale, padded, along, swapped)
    weight_grad = weight_grad.reshape((3, 3, filters, chans_in))
    return (outputs, input_grad, weight_grad)


def solution(mesh):
    return jax.shard_map(
        body,
        mesh=mesh,
        in_specs=(
            P(None, "filt", None, "chan"),
            P(None, None, "filt", "chan"),
            P(None, "chan", "filt", None),
        ),
        out_specs=(
            P(None, "chan", "filt", None),
            P(None, "filt", None, "chan"),
            P(None, None, "filt", "chan"),
        ),
        check_vma=False,
    )
```

```python
import functools
import math

import jax
import jax.numpy as jnp
from jax import lax
from jax.experimental import pallas as pl
from jax.experimental.pallas import tpu as pltpu
from jax.sharding import PartitionSpec as P

F32 = jnp.float32
BF16 = jnp.bfloat16
NT = (((1,), (1,)), ((), ()))
HBM = pl.BlockSpec(memory_space=pltpu.HBM)
VMEM = pl.BlockSpec(memory_space=pltpu.VMEM)
SMEM = pl.BlockSpec(memory_space=pltpu.SMEM)
PAIR = 2


def params(mib):
    return pltpu.CompilerParams(vmem_limit_bytes=mib << 20)


def cost(flops, moved):
    return pl.CostEstimate(flops=int(flops), bytes_accessed=int(moved), transcendentals=0)


def lane_shift(value, by):
    size = value.shape[1]
    lane = lax.broadcasted_iota(jnp.int32, value.shape, 1)
    keep = lane >= by if by > 0 else lane < size + by
    return jnp.where(keep, pltpu.roll(value, by % size, 1), 0.0)


def after(value, *others):
    return lax.optimization_barrier((value,) + others)[0]


def arrivals(depth, line):
    steps = [way for step in range(1, depth) for way in (-step, step)]
    return [way for way in steps if 0 <= line + way < depth]


def arrival(along, depth, line, place):
    picked = None
    for z in range(depth):
        way = arrivals(depth, z)[place]
        value = along[2 * abs(way) - (way < 0)]
        picked = value if picked is None or value is picked else jnp.where(line == z, value, picked)
    return picked


def start_rows(at, parts, rows, sems):
    height = parts[0][0].shape[0]

    def place(spot):
        return rows.at[pl.ds(1 + spot * height, height)]

    for half in range(PAIR):
        of_side = lax.rem(at[1] + half, PAIR)
        for index, part in enumerate(parts[half]):
            spot = at[4 + index] * PAIR + of_side
            pltpu.make_async_copy(part, place(spot), sems.at[spot]).start()

    rows[0] = jnp.zeros(rows.shape[1:], rows.dtype)
    rows[rows.shape[0] - 1] = jnp.zeros(rows.shape[1:], rows.dtype)
    return lambda spot: pltpu.make_async_copy(parts[0][0], place(spot), sems.at[spot]).wait()


def forward_kernel(depth, chans, at, weights, *refs):
    count = (len(refs) - 5) // 2
    parts = (refs[:count], refs[count : 2 * count])
    keep, send, rows, taps, sems = refs[2 * count :]
    wait = start_rows(at, parts, rows, sems)
    filters, chans_in = weights.shape[2], weights.shape[3]
    for tap_row in range(3):
        for tap_col in range(3):
            taps[pl.ds(tap_col * filters, filters), pl.ds(tap_row * chans_in, chans_in)] = weights[tap_row, tap_col]
    width = rows.shape[1]
    block = keep.shape[1]
    height = parts[0][0].shape[0]
    group = min(4, block)
    per_block = block // group
    far, core = at[2], at[3]
    for spot in range(depth * PAIR):
        wait(spot)

    @pl.loop(0, (chans // 2) * per_block)
    def _(step):
        which, group_at = step // per_block, step % per_block
        for target, of_core in ((send, 1 - core), (keep, core)):
            first = (lax.rem(far + which, chans // 2) * 2 + of_core) * block + group_at * group
            window = jnp.concatenate(
                [rows[pl.ds(first + i, group)].reshape(group * width, chans_in) for i in range(3)], axis=1
            )
            product = lax.dot_general(taps[...], window, NT, preferred_element_type=F32)
            for row in range(group):
                part = [
                    product[j * filters : (j + 1) * filters, row * width : (row + 1) * width] for j in range(3)
                ]
                target[which, group_at * group + row] = part[1] + lane_shift(part[0], 1) + lane_shift(part[2], -1)


def forward_partial(depth, chans, at, weights, own, other):
    height, width, chans_in = own[0].shape
    filters = weights.shape[2]
    rows = height * depth * PAIR
    half = jax.ShapeDtypeStruct((chans // 2, rows // chans, filters, width), F32)
    return pl.pallas_call(
        functools.partial(forward_kernel, depth, chans),
        out_shape=(half, half),
        in_specs=[SMEM, VMEM] + [HBM] * (len(own) + len(other)),
        out_specs=(VMEM, VMEM),
        scratch_shapes=[
            pltpu.VMEM((rows + 2, width, chans_in), BF16),
            pltpu.VMEM((3 * filters, 3 * chans_in), BF16),
            pltpu.SemaphoreType.DMA((depth * PAIR,)),
        ],
        compiler_params=params(58),
        cost_estimate=cost(18 * rows * width * chans_in * filters, 4 * rows * width * filters + 2 * rows * width * chans_in),
        name="forward",
    )(at, weights, *own, *other)


def weight_kernel(depth, scale, at, cot, *refs):
    count = (len(refs) - 4) // 2
    parts = (refs[:count], refs[count : 2 * count])
    out, rows, moved, sems = refs[2 * count :]
    wait = start_rows(at, parts, rows, sems)
    filters, width = cot.shape[1], cot.shape[2]
    total = cot.shape[0] - 2
    chans_in = rows.shape[2]
    chunk = min(8, total)
    for spot in range(depth * PAIR):
        wait(spot)
    out[...] = jnp.zeros(out.shape, F32)

    @pl.loop(0, total // chunk)
    def _(step):
        first = step * chunk
        for row in range(chunk):
            value = cot[1 + first + row]
            wide = value.astype(F32)
            lanes = pl.ds(row * width, width)
            moved[0:filters, lanes] = lane_shift(wide, -1).astype(BF16)
            moved[filters : 2 * filters, lanes] = value
            moved[2 * filters :, lanes] = lane_shift(wide, 1).astype(BF16)
        for tap_row in range(3):
            window = rows[pl.ds(first + tap_row, chunk)].reshape(chunk * width, chans_in)
            out[tap_row] += jnp.dot(moved[...], window, preferred_element_type=F32)

    out[...] = out[...] * scale


def weight_gradient(depth, at, scale, cot, own, other):
    width, chans_in = own[0].shape[1:]
    rows, filters = cot.shape[0] - 2, cot.shape[1]
    return pl.pallas_call(
        functools.partial(weight_kernel, depth, scale),
        out_shape=jax.ShapeDtypeStruct((3, 3 * filters, chans_in), F32),
        in_specs=[SMEM, VMEM] + [HBM] * (len(own) + len(other)),
        out_specs=VMEM,
        scratch_shapes=[
            pltpu.VMEM((rows + 2, width, chans_in), BF16),
            pltpu.VMEM((3 * filters, min(8, rows) * width), BF16),
            pltpu.SemaphoreType.DMA((depth * PAIR,)),
        ],
        compiler_params=params(58),
        cost_estimate=cost(18 * rows * width * chans_in * filters, 2 * rows * width * (filters + chans_in)),
        name="weight_gradient",
    )(at, cot, *own, *other)


def turn_kernel(same, cross, out):
    fars, _, rows = same.shape[:3]
    unroll = max(n for n in (1, 2, 3, 6) if rows % n == 0)

    @pl.loop(0, rows // unroll)
    def _(step):
        for n in range(unroll):
            row = step * unroll + n
            out[0, row] = jnp.concatenate([part[far, 0, row] for far in range(fars) for part in (same, cross)], axis=0).T


def turned(same, cross):
    fars, depth, rows, part, width = same.shape
    filters = 2 * fars * part
    spec = pl.BlockSpec((fars, 1, rows, part, width), lambda d: (0, d, 0, 0, 0))
    return pl.pallas_call(
        turn_kernel,
        grid=(depth,),
        out_shape=jax.ShapeDtypeStruct((depth, rows, width, filters), BF16),
        in_specs=[spec, spec],
        out_specs=pl.BlockSpec((1, rows, width, filters), lambda d: (d, 0, 0, 0)),
        compiler_params=params(58),
        cost_estimate=cost(0, 4 * depth * rows * width * filters),
        name="turned",
    )(same, cross)


def input_kernel(chans, index, at, cot, kernels, keep, send, source, taps, stacked, sems):
    side, far, core = at[1], at[2], at[3]
    depth, rows, width, filters = source.shape
    rows = rows - 2
    chans_in = taps.shape[3]
    copies = []
    for n in range(depth):
        copies.append(
            (
                pltpu.make_async_copy(
                    kernels.at[n, :, :, pl.ds(index * chans_in, chans_in)], taps.at[n], sems.at[n, 0]
                ),
                pltpu.make_async_copy(cot.at[n], source.at[n], sems.at[n, 1]),
            )
        )
        for copy in copies[n]:
            copy.start()
    part = filters // chans
    places = chans if part % 16 == 0 else 1
    size = filters // places
    for n in range(depth):
        copies[n][0].wait()
        for place in range(places):
            chan = lax.rem(far - place // 2 + chans // 2, chans // 2) * 2 + lax.rem(core + place, 2)
            of_chan = pl.ds(0 if places == 1 else pl.multiple_of(chan * size, size), size)
            for i in range(3):
                for j in range(3):
                    stacked[
                        pl.ds((n * 3 + i) * filters + place * size, size), pl.ds(j * chans_in, chans_in)
                    ] = taps[n, 3 * i + j, of_chan]
    for n in range(depth):
        copies[n][1].wait()
    half = rows // PAIR
    chunk = min(8, half)
    lanes = lax.broadcasted_iota(jnp.int32, (width, chans_in), 0)

    for out, of_side in ((send, 1 - side), (keep, side)):

        @pl.loop(0, half // chunk)
        def _(step):
            first = of_side * half + step * chunk
            window = [
                source[n, pl.ds(first + 2 - i, chunk)].reshape(chunk * width, filters)
                for n in range(depth)
                for i in range(3)
            ]
            if filters % 128 == 0:
                product = jnp.dot(jnp.concatenate(window, axis=1), stacked[...], preferred_element_type=F32)
            else:
                product = sum(
                    jnp.dot(value, stacked[n * filters : (n + 1) * filters], preferred_element_type=F32)
                    for n, value in enumerate(window)
                )
            for row in range(chunk):
                here = [
                    product[row * width : (row + 1) * width, j * chans_in : (j + 1) * chans_in] for j in range(3)
                ]
                before_it = jnp.where(lanes < width - 1, pltpu.roll(here[0], width - 1, 0), 0.0)
                behind_it = jnp.where(lanes >= 1, pltpu.roll(here[2], 1, 0), 0.0)
                out[step * chunk + row] = here[1] + before_it + behind_it


def input_partial(chans, at, cot, kernels, index, parts):
    depth, rows, width, filters = cot.shape
    rows = rows - 2
    chans_in = kernels.shape[3] // parts
    half = jax.ShapeDtypeStruct((rows // PAIR, width, chans_in), F32)
    return pl.pallas_call(
        functools.partial(input_kernel, chans, index),
        out_shape=(half, half),
        in_specs=[SMEM, HBM, HBM],
        out_specs=(VMEM, VMEM),
        scratch_shapes=[
            pltpu.VMEM(cot.shape, BF16),
            pltpu.VMEM(kernels.shape[:3] + (chans_in,), BF16),
            pltpu.VMEM((depth * 3 * filters, 3 * chans_in), BF16),
            pltpu.SemaphoreType.DMA((depth, 2)),
        ],
        compiler_params=params(58),
        cost_estimate=cost(
            18 * rows * width * chans_in * filters * depth, 2 * depth * filters * ((rows + 2) * width + 9 * chans_in)
        ),
        name="input_gradient",
    )(at, cot, kernels)


def fars_gather(value, chans):
    got = [value]
    for step in range(1, chans // 2):
        got.append(lax.ppermute(value, "chan", [(c, (c + 2 * step) % chans) for c in range(chans)]))
    return jnp.stack(got)


def lines(depth):
    return [[z * PAIR + y for z in range(depth)] for y in range(PAIR)]


def line_steps(step, depth):
    up = [(z * PAIR + y, (z + 1) * PAIR + y) for z in range(step - 1, depth - 1) for y in range(PAIR)]
    down = [(z * PAIR + y, (z - 1) * PAIR + y) for z in range(1, depth - step + 1) for y in range(PAIR)]
    return up, down


def line_step(along, step, depth):
    up, down = line_steps(step, depth)
    below, above = along[0 if step == 1 else -2], along[0 if step == 1 else -1]
    return [lax.ppermute(below, "filt", up), lax.ppermute(above, "filt", down)]


def core_swap(value, chans):
    return lax.ppermute(value, "chan", [(c, c ^ 1) for c in range(chans)])


def pair_swap(value, depth):
    pairs = [(z * PAIR + y, z * PAIR + 1 - y) for z in range(depth) for y in range(PAIR)]
    return lax.ppermute(value, "filt", pairs)


def body(inputs, weights, cotangent):
    chans, filts = lax.axis_size("chan"), lax.axis_size("filt")
    depth = filts // PAIR
    chan, filt = lax.axis_index("chan"), lax.axis_index("filt")
    line, side = filt // PAIR, filt % PAIR
    far, core = chan // 2, chan % 2
    spots = jnp.asarray([[z] + [z + way for way in arrivals(depth, z)] for z in range(depth)], jnp.int32)
    at = jnp.concatenate([jnp.stack([line, side, far, core]).astype(jnp.int32), spots[line]])
    own_rows, width, chans_in = inputs.shape[1:]
    block, filters = cotangent.shape[1], cotangent.shape[2]
    height = own_rows * filts
    scale = 1.0 / math.sqrt(inputs.shape[0] * height * width)

    kernels = lax.all_gather(weights, "filt", axis=0, axis_index_groups=lines(depth))
    kernels = kernels.reshape((depth, 9) + weights.shape[2:])

    part = filters // chans
    line_rows = own_rows * PAIR

    def all_rows(same):
        cross = core_swap(same, chans)
        padded = jnp.zeros((height + 2, filters, width), BF16)
        for step in range(chans // 2):
            at_far = lax.rem(far - step + chans // 2, chans // 2) * 2
            padded = lax.dynamic_update_slice(padded, same[step], (1 + (at_far + core) * block, 0, 0))
            padded = lax.dynamic_update_slice(padded, cross[step], (1 + (at_far + 1 - core) * block, 0, 0))
        return padded

    def line_pieces(padded):
        own_part = lax.dynamic_slice_in_dim(padded, chan * part, part, axis=1)
        return jnp.stack([own_part[z * line_rows : (z + 1) * line_rows + 2] for z in range(depth)])

    def exchange(pieces):
        return lax.all_to_all(pieces, "filt", 0, 0, axis_index_groups=lines(depth), tiled=True)

    along, mine, theirs = [inputs[0]], [inputs[0]], [pair_swap(inputs[0], depth)]
    same, gate = fars_gather(cotangent[0], chans), []
    padded = pieces = None
    for step in range(1, depth + 1):
        along = list(lax.optimization_barrier(tuple(along + gate)))[: len(along)]
        if step < depth:
            along += line_step(along, step, depth)
        if step == 1:
            gate = along[1:] + theirs + [same]
            continue
        mine.append(arrival(along, depth, line, step - 2))
        theirs.append(pair_swap(mine[-1], depth))
        before, gate = gate, along[-2:] + theirs[-1:]
        if step == 2:
            padded = all_rows(after(same, *before))
            pieces = line_pieces(padded)
            gate.append(pieces)
        elif step == 3:
            pieces = exchange(after(pieces, *before))
            gate.append(pieces)
        elif step == 4:
            same = fars_gather(after(pieces, *before), chans)
    if depth < 3:
        pieces = exchange(pieces)
    if depth < 4:
        same = fars_gather(pieces, chans)
    sources = turned(same, core_swap(same, chans))

    if part % 16:
        order = [(far - c // 2 + chans // 2) % (chans // 2) * 2 + (core + c) % 2 for c in range(chans)]
        split = kernels.reshape((depth, 9, chans, part, chans_in))
        kernels = jnp.take(split, jnp.stack(order), axis=2).reshape(kernels.shape)

    keep, send = forward_partial(depth, chans, after(at, same, kernels), weights, mine, theirs)
    from_core = core_swap(send, chans)
    outputs = keep[0] + from_core[0]
    at_next = after(at, send)
    for step in range(1, chans // 2):
        moving = keep[step] + from_core[step]
        at_next = after(at_next, moving)
        outputs += lax.ppermute(moving, "chan", [(c, (c + 2 * step) % chans) for c in range(chans)])
    outputs = outputs.astype(BF16)[None]

    parts = 1
    input_grad = []
    for index in range(parts):
        kept, sent = input_partial(chans, at_next, sources, kernels, index, parts)
        at_next = after(at_next, sent)
        input_grad.append((kept + pair_swap(sent, depth)).astype(BF16))
    input_grad = jnp.concatenate(input_grad, axis=2)[None]

    weight_grad = weight_gradient(depth, at_next, scale, padded, mine, theirs)
    weight_grad = weight_grad.reshape((3, 3, filters, chans_in))
    return (outputs, input_grad, weight_grad)


def solution(mesh):
    return jax.shard_map(
        body,
        mesh=mesh,
        in_specs=(
            P(None, "filt", None, "chan"),
            P(None, None, "filt", "chan"),
            P(None, "chan", "filt", None),
        ),
        out_specs=(
            P(None, "chan", "filt", None),
            P(None, "filt", None, "chan"),
            P(None, None, "filt", "chan"),
        ),
        check_vma=False,
    )
```

```python
import functools
import math

import jax
import jax.numpy as jnp
from jax import lax
from jax.experimental import pallas as pl
from jax.experimental.pallas import tpu as pltpu
from jax.sharding import PartitionSpec as P

F32 = jnp.float32
BF16 = jnp.bfloat16
NT = (((1,), (1,)), ((), ()))
HBM = pl.BlockSpec(memory_space=pltpu.HBM)
VMEM = pl.BlockSpec(memory_space=pltpu.VMEM)
SMEM = pl.BlockSpec(memory_space=pltpu.SMEM)
PAIR = 2


def params(mib):
    return pltpu.CompilerParams(vmem_limit_bytes=mib << 20)


def cost(flops, moved):
    return pl.CostEstimate(flops=int(flops), bytes_accessed=int(moved), transcendentals=0)


def lane_shift(value, by):
    size = value.shape[1]
    lane = lax.broadcasted_iota(jnp.int32, value.shape, 1)
    keep = lane >= by if by > 0 else lane < size + by
    return jnp.where(keep, pltpu.roll(value, by % size, 1), 0.0)


def after(value, *others):
    return lax.optimization_barrier((value,) + others)[0]


def arrivals(depth, line):
    steps = [way for step in range(1, depth) for way in (-step, step)]
    return [way for way in steps if 0 <= line + way < depth]


def arrival(along, depth, line, place):
    picked = None
    for z in range(depth):
        way = arrivals(depth, z)[place]
        value = along[2 * abs(way) - (way < 0)]
        picked = value if picked is None or value is picked else jnp.where(line == z, value, picked)
    return picked


def load_rows(at, parts, rows, sems, first, last):
    height = parts[0][0].shape[0]

    def place(spot):
        return rows.at[pl.ds(1 + spot * height, height)]

    for half in range(PAIR):
        of_side = lax.rem(at[1] + half, PAIR)
        for index, part in enumerate(parts[half]):
            spot = at[4 + index] * PAIR + of_side

            @pl.when(jnp.logical_and(spot >= first, spot <= last))
            def _():
                pltpu.make_async_copy(part, place(spot), sems.at[spot]).start()

    rows[0] = jnp.zeros(rows.shape[1:], rows.dtype)
    rows[rows.shape[0] - 1] = jnp.zeros(rows.shape[1:], rows.dtype)
    return lambda spot: pltpu.make_async_copy(parts[0][0], place(spot), sems.at[spot]).wait()


def forward_kernel(depth, chans, which, at, weights, *refs):
    count = (len(refs) - 5) // 2
    parts = (refs[:count], refs[count : 2 * count])
    keep, send, rows, taps, sems = refs[2 * count :]
    filters, chans_in = weights.shape[2], weights.shape[3]
    width = rows.shape[1]
    block = keep.shape[0]
    height = parts[0][0].shape[0]
    far, core = at[2], at[3]
    top = lax.rem(far + which, chans // 2) * 2 * block
    first, spots = top // height, max(1, 2 * block // height)
    wait = load_rows(at, parts, rows, sems, first - 1, first + spots)
    for tap_row in range(3):
        for tap_col in range(3):
            taps[pl.ds(tap_col * filters, filters), pl.ds(tap_row * chans_in, chans_in)] = weights[tap_row, tap_col]
    for spot in range(-1, spots + 1):

        @pl.when(jnp.logical_and(first + spot >= 0, first + spot < depth * PAIR))
        def _():
            wait(first + spot)

    group = min(4, block)

    @pl.loop(0, block // group)
    def _(step):
        for target, of_core in ((send, 1 - core), (keep, core)):
            start = top + of_core * block + step * group
            window = jnp.concatenate(
                [rows[pl.ds(start + i, group)].reshape(group * width, chans_in) for i in range(3)], axis=1
            )
            product = lax.dot_general(taps[...], window, NT, preferred_element_type=F32)
            for row in range(group):
                part = [
                    product[j * filters : (j + 1) * filters, row * width : (row + 1) * width] for j in range(3)
                ]
                target[step * group + row] = part[1] + lane_shift(part[0], 1) + lane_shift(part[2], -1)


def forward_partial(depth, chans, which, at, weights, own, other):
    height, width, chans_in = own[0].shape
    filters = weights.shape[2]
    rows = height * depth * PAIR
    half = jax.ShapeDtypeStruct((rows // chans, filters, width), F32)
    return pl.pallas_call(
        functools.partial(forward_kernel, depth, chans, which),
        out_shape=(half, half),
        in_specs=[SMEM, VMEM] + [HBM] * (len(own) + len(other)),
        out_specs=(VMEM, VMEM),
        scratch_shapes=[
            pltpu.VMEM((rows + 2, width, chans_in), BF16),
            pltpu.VMEM((3 * filters, 3 * chans_in), BF16),
            pltpu.SemaphoreType.DMA((depth * PAIR,)),
        ],
        compiler_params=params(58),
        cost_estimate=cost(
            36 * rows // chans * width * chans_in * filters, 8 * rows // chans * width * (filters + chans_in)
        ),
        name="forward",
    )(at, weights, *own, *other)


def weight_kernel(depth, scale, at, cot, *refs):
    count = (len(refs) - 4) // 2
    parts = (refs[:count], refs[count : 2 * count])
    out, rows, moved, sems = refs[2 * count :]
    wait = load_rows(at, parts, rows, sems, 0, depth * PAIR - 1)
    filters, width = cot.shape[1], cot.shape[2]
    total = cot.shape[0] - 2
    chans_in = rows.shape[2]
    chunk = min(8, total)
    for spot in range(depth * PAIR):
        wait(spot)
    out[...] = jnp.zeros(out.shape, F32)

    @pl.loop(0, total // chunk)
    def _(step):
        first = step * chunk
        for row in range(chunk):
            value = cot[1 + first + row]
            wide = value.astype(F32)
            lanes = pl.ds(row * width, width)
            moved[0:filters, lanes] = lane_shift(wide, -1).astype(BF16)
            moved[filters : 2 * filters, lanes] = value
            moved[2 * filters :, lanes] = lane_shift(wide, 1).astype(BF16)
        for tap_row in range(3):
            window = rows[pl.ds(first + tap_row, chunk)].reshape(chunk * width, chans_in)
            out[tap_row] += jnp.dot(moved[...], window, preferred_element_type=F32)

    out[...] = out[...] * scale


def weight_gradient(depth, at, scale, cot, own, other):
    width, chans_in = own[0].shape[1:]
    rows, filters = cot.shape[0] - 2, cot.shape[1]
    return pl.pallas_call(
        functools.partial(weight_kernel, depth, scale),
        out_shape=jax.ShapeDtypeStruct((3, 3 * filters, chans_in), F32),
        in_specs=[SMEM, VMEM] + [HBM] * (len(own) + len(other)),
        out_specs=VMEM,
        scratch_shapes=[
            pltpu.VMEM((rows + 2, width, chans_in), BF16),
            pltpu.VMEM((3 * filters, min(8, rows) * width), BF16),
            pltpu.SemaphoreType.DMA((depth * PAIR,)),
        ],
        compiler_params=params(58),
        cost_estimate=cost(18 * rows * width * chans_in * filters, 2 * rows * width * (filters + chans_in)),
        name="weight_gradient",
    )(at, cot, *own, *other)


def turn_kernel(same, cross, out):
    fars, _, rows = same.shape[:3]
    unroll = max(n for n in (1, 2, 3, 6) if rows % n == 0)

    @pl.loop(0, rows // unroll)
    def _(step):
        for n in range(unroll):
            row = step * unroll + n
            out[0, row] = jnp.concatenate([part[far, 0, row] for far in range(fars) for part in (same, cross)], axis=0).T


def turned(same, cross):
    fars, depth, rows, part, width = same.shape
    filters = 2 * fars * part
    spec = pl.BlockSpec((fars, 1, rows, part, width), lambda d: (0, d, 0, 0, 0))
    return pl.pallas_call(
        turn_kernel,
        grid=(depth,),
        out_shape=jax.ShapeDtypeStruct((depth, rows, width, filters), BF16),
        in_specs=[spec, spec],
        out_specs=pl.BlockSpec((1, rows, width, filters), lambda d: (d, 0, 0, 0)),
        compiler_params=params(58),
        cost_estimate=cost(0, 4 * depth * rows * width * filters),
        name="turned",
    )(same, cross)


def input_kernel(chans, index, at, cot, kernels, keep, send, source, taps, stacked, sems):
    side, far, core = at[1], at[2], at[3]
    depth, rows, width, filters = source.shape
    rows = rows - 2
    chans_in = taps.shape[3]
    copies = []
    for n in range(depth):
        copies.append(
            (
                pltpu.make_async_copy(
                    kernels.at[n, :, :, pl.ds(index * chans_in, chans_in)], taps.at[n], sems.at[n, 0]
                ),
                pltpu.make_async_copy(cot.at[n], source.at[n], sems.at[n, 1]),
            )
        )
        for copy in copies[n]:
            copy.start()
    part = filters // chans
    places = chans if part % 16 == 0 else 1
    size = filters // places
    for n in range(depth):
        copies[n][0].wait()
        for place in range(places):
            chan = lax.rem(far - place // 2 + chans // 2, chans // 2) * 2 + lax.rem(core + place, 2)
            of_chan = pl.ds(0 if places == 1 else pl.multiple_of(chan * size, size), size)
            for i in range(3):
                for j in range(3):
                    stacked[
                        pl.ds((n * 3 + i) * filters + place * size, size), pl.ds(j * chans_in, chans_in)
                    ] = taps[n, 3 * i + j, of_chan]
    for n in range(depth):
        copies[n][1].wait()
    half = rows // PAIR
    chunk = min(8, half)
    lanes = lax.broadcasted_iota(jnp.int32, (width, chans_in), 0)

    for out, of_side in ((send, 1 - side), (keep, side)):

        @pl.loop(0, half // chunk)
        def _(step):
            first = of_side * half + step * chunk
            window = [
                source[n, pl.ds(first + 2 - i, chunk)].reshape(chunk * width, filters)
                for n in range(depth)
                for i in range(3)
            ]
            if filters % 128 == 0:
                product = jnp.dot(jnp.concatenate(window, axis=1), stacked[...], preferred_element_type=F32)
            else:
                product = sum(
                    jnp.dot(value, stacked[n * filters : (n + 1) * filters], preferred_element_type=F32)
                    for n, value in enumerate(window)
                )
            for row in range(chunk):
                here = [
                    product[row * width : (row + 1) * width, j * chans_in : (j + 1) * chans_in] for j in range(3)
                ]
                before_it = jnp.where(lanes < width - 1, pltpu.roll(here[0], width - 1, 0), 0.0)
                behind_it = jnp.where(lanes >= 1, pltpu.roll(here[2], 1, 0), 0.0)
                out[step * chunk + row] = here[1] + before_it + behind_it


def input_partial(chans, at, cot, kernels, index, halves):
    depth, rows, width, filters = cot.shape
    rows = rows - 2
    chans_in = kernels.shape[3] // halves
    half = jax.ShapeDtypeStruct((rows // PAIR, width, chans_in), F32)
    return pl.pallas_call(
        functools.partial(input_kernel, chans, index),
        out_shape=(half, half),
        in_specs=[SMEM, HBM, HBM],
        out_specs=(VMEM, VMEM),
        scratch_shapes=[
            pltpu.VMEM(cot.shape, BF16),
            pltpu.VMEM(kernels.shape[:3] + (chans_in,), BF16),
            pltpu.VMEM((depth * 3 * filters, 3 * chans_in), BF16),
            pltpu.SemaphoreType.DMA((depth, 2)),
        ],
        compiler_params=params(58),
        cost_estimate=cost(
            18 * rows * width * chans_in * filters * depth, 2 * depth * filters * ((rows + 2) * width + 9 * chans_in)
        ),
        name="input_gradient",
    )(at, cot, kernels)


def fars_gather(value, chans):
    got = [value]
    for step in range(1, chans // 2):
        got.append(lax.ppermute(value, "chan", [(c, (c + 2 * step) % chans) for c in range(chans)]))
    return jnp.stack(got)


def lines(depth):
    return [[z * PAIR + y for z in range(depth)] for y in range(PAIR)]


def line_steps(step, depth):
    up = [(z * PAIR + y, (z + 1) * PAIR + y) for z in range(step - 1, depth - 1) for y in range(PAIR)]
    down = [(z * PAIR + y, (z - 1) * PAIR + y) for z in range(1, depth - step + 1) for y in range(PAIR)]
    return up, down


def line_step(along, step, depth):
    up, down = line_steps(step, depth)
    below, above = along[0 if step == 1 else -2], along[0 if step == 1 else -1]
    return [lax.ppermute(below, "filt", up), lax.ppermute(above, "filt", down)]


def core_swap(value, chans):
    return lax.ppermute(value, "chan", [(c, c ^ 1) for c in range(chans)])


def pair_swap(value, depth):
    pairs = [(z * PAIR + y, z * PAIR + 1 - y) for z in range(depth) for y in range(PAIR)]
    return lax.ppermute(value, "filt", pairs)


def body(inputs, weights, cotangent):
    chans, filts = lax.axis_size("chan"), lax.axis_size("filt")
    depth = filts // PAIR
    chan, filt = lax.axis_index("chan"), lax.axis_index("filt")
    line, side = filt // PAIR, filt % PAIR
    far, core = chan // 2, chan % 2
    spots = jnp.asarray([[z] + [z + way for way in arrivals(depth, z)] for z in range(depth)], jnp.int32)
    at = jnp.concatenate([jnp.stack([line, side, far, core]).astype(jnp.int32), spots[line]])
    own_rows, width, chans_in = inputs.shape[1:]
    block, filters = cotangent.shape[1], cotangent.shape[2]
    height = own_rows * filts
    scale = 1.0 / math.sqrt(inputs.shape[0] * height * width)

    part = filters // chans
    line_rows = own_rows * PAIR

    def all_rows(same):
        cross = core_swap(same, chans)
        padded = jnp.zeros((height + 2, filters, width), BF16)
        for step in range(chans // 2):
            at_far = lax.rem(far - step + chans // 2, chans // 2) * 2
            padded = lax.dynamic_update_slice(padded, same[step], (1 + (at_far + core) * block, 0, 0))
            padded = lax.dynamic_update_slice(padded, cross[step], (1 + (at_far + 1 - core) * block, 0, 0))
        return padded

    def line_pieces(padded):
        own_part = lax.dynamic_slice_in_dim(padded, chan * part, part, axis=1)
        return jnp.stack([own_part[z * line_rows : (z + 1) * line_rows + 2] for z in range(depth)])

    def exchange(pieces):
        return lax.all_to_all(pieces, "filt", 0, 0, axis_index_groups=lines(depth), tiled=True)

    along, mine, theirs = [inputs[0]], [inputs[0]], [pair_swap(inputs[0], depth)]
    same, gate = fars_gather(cotangent[0], chans), []
    padded = pieces = None
    kernels = weights
    for step in range(1, depth + 1):
        along = list(lax.optimization_barrier(tuple(along + gate)))[: len(along)]
        if step < depth:
            along += line_step(along, step, depth)
        if step == 1:
            gate = along[1:] + theirs + [same]
            continue
        mine.append(arrival(along, depth, line, step - 2))
        theirs.append(pair_swap(mine[-1], depth))
        before, gate = gate, along[-2:] + theirs[-1:]
        if step == 2:
            padded = all_rows(after(same, *before))
            pieces = exchange(line_pieces(padded))
            gate.append(pieces)
        elif step == 3:
            kernels = after(weights, *before)
            same = fars_gather(after(pieces, *before), chans)
            gate.append(same)
    kernels = lax.all_gather(kernels, "filt", axis=0, axis_index_groups=lines(depth))
    kernels = kernels.reshape((depth, 9) + weights.shape[2:])
    if depth < 3:
        same = fars_gather(pieces, chans)
    sources = turned(same, core_swap(same, chans))

    if part % 16:
        order = [(far - c // 2 + chans // 2) % (chans // 2) * 2 + (core + c) % 2 for c in range(chans)]
        split = kernels.reshape((depth, 9, chans, part, chans_in))
        kernels = jnp.take(split, jnp.stack(order), axis=2).reshape(kernels.shape)

    halves = PAIR if chans_in % (PAIR * 128) == 0 else 1
    fars = chans // 2
    at_next = after(at, sources, kernels)
    outputs, input_grad = None, []
    for n, which in enumerate([*range(1, fars), 0]):
        keep, send = forward_partial(depth, chans, which, at_next, weights, mine, theirs)
        at_next = after(at, send)
        moving = keep + core_swap(send, chans)
        if which:
            if not input_grad:
                kept, sent = input_partial(chans, at_next, sources, kernels, 0, halves)
                at_next = after(at, sent)
                input_grad.append((kept + pair_swap(sent, depth)).astype(BF16))
            at_next = after(at_next, moving)
            moving = lax.ppermute(moving, "chan", [(c, (c + 2 * which) % chans) for c in range(chans)])
        outputs = moving if outputs is None else outputs + moving
    outputs = outputs.astype(BF16)[None]
    for index in range(len(input_grad), halves):
        kept, sent = input_partial(chans, at_next, sources, kernels, index, halves)
        at_next = after(at, sent)
        input_grad.append((kept + pair_swap(sent, depth)).astype(BF16))
    input_grad = jnp.concatenate(input_grad, axis=2)[None]

    weight_grad = weight_gradient(depth, at_next, scale, padded, mine, theirs)
    weight_grad = weight_grad.reshape((3, 3, filters, chans_in))
    return (outputs, input_grad, weight_grad)


def solution(mesh):
    return jax.shard_map(
        body,
        mesh=mesh,
        in_specs=(
            P(None, "filt", None, "chan"),
            P(None, None, "filt", "chan"),
            P(None, "chan", "filt", None),
        ),
        out_specs=(
            P(None, "chan", "filt", None),
            P(None, "filt", None, "chan"),
            P(None, None, "filt", "chan"),
        ),
        check_vma=False,
    )
```

```python
import functools
import math

import jax
import jax.numpy as jnp
from jax import lax
from jax.experimental import pallas as pl
from jax.experimental.pallas import tpu as pltpu
from jax.sharding import PartitionSpec as P

F32 = jnp.float32
BF16 = jnp.bfloat16
NT = (((1,), (1,)), ((), ()))
HBM = pl.BlockSpec(memory_space=pltpu.HBM)
VMEM = pl.BlockSpec(memory_space=pltpu.VMEM)
SMEM = pl.BlockSpec(memory_space=pltpu.SMEM)
PAIR = 2


def params(mib):
    return pltpu.CompilerParams(vmem_limit_bytes=mib << 20)


def cost(flops, moved):
    return pl.CostEstimate(flops=int(flops), bytes_accessed=int(moved), transcendentals=0)


def lane_shift(value, by):
    size = value.shape[1]
    lane = lax.broadcasted_iota(jnp.int32, value.shape, 1)
    keep = lane >= by if by > 0 else lane < size + by
    return jnp.where(keep, pltpu.roll(value, by % size, 1), 0.0)


def after(value, *others):
    return lax.optimization_barrier((value,) + others)[0]


def arrivals(depth, line):
    ways = sorted((way for way in range(-line, depth - line) if way), key=abs)
    if abs(ways[-1]) == depth - 1:
        ways.insert(1, ways.pop())
    return ways


def arrival(along, depth, line, place):
    picked = None
    for z in range(depth):
        value = along[arrivals(depth, z)[place]]
        picked = value if picked is None or value is picked else jnp.where(line == z, value, picked)
    return picked


def load_rows(at, parts, rows, sems, first, last):
    height = parts[0][0].shape[0]

    def place(spot):
        return rows.at[pl.ds(1 + spot * height, height)]

    for half in range(PAIR):
        of_side = lax.rem(at[1] + half, PAIR)
        for index, part in enumerate(parts[half]):
            spot = at[4 + index] * PAIR + of_side

            @pl.when(jnp.logical_and(spot >= first, spot <= last))
            def _():
                pltpu.make_async_copy(part, place(spot), sems.at[spot]).start()

    rows[0] = jnp.zeros(rows.shape[1:], rows.dtype)
    rows[rows.shape[0] - 1] = jnp.zeros(rows.shape[1:], rows.dtype)
    return lambda spot: pltpu.make_async_copy(parts[0][0], place(spot), sems.at[spot]).wait()


def forward_kernel(depth, chans, which, at, weights, *refs):
    count = (len(refs) - 5) // 2
    parts = (refs[:count], refs[count : 2 * count])
    keep, send, rows, taps, sems = refs[2 * count :]
    filters, chans_in = weights.shape[2], weights.shape[3]
    width = rows.shape[1]
    block = keep.shape[0]
    height = parts[0][0].shape[0]
    far, core = at[2], at[3]
    top = lax.rem(far + which, chans // 2) * 2 * block
    first, spots = top // height, max(1, 2 * block // height)
    wait = load_rows(at, parts, rows, sems, first - 1, first + spots)
    for tap_row in range(3):
        for tap_col in range(3):
            taps[pl.ds(tap_col * filters, filters), pl.ds(tap_row * chans_in, chans_in)] = weights[tap_row, tap_col]
    for spot in range(-1, spots + 1):

        @pl.when(jnp.logical_and(first + spot >= 0, first + spot < depth * PAIR))
        def _():
            wait(first + spot)

    group = min(4, block)

    @pl.loop(0, block // group)
    def _(step):
        for target, of_core in ((send, 1 - core), (keep, core)):
            start = top + of_core * block + step * group
            window = jnp.concatenate(
                [rows[pl.ds(start + i, group)].reshape(group * width, chans_in) for i in range(3)], axis=1
            )
            product = lax.dot_general(taps[...], window, NT, preferred_element_type=F32)
            for row in range(group):
                part = [
                    product[j * filters : (j + 1) * filters, row * width : (row + 1) * width] for j in range(3)
                ]
                target[step * group + row] = part[1] + lane_shift(part[0], 1) + lane_shift(part[2], -1)


def forward_partial(depth, chans, which, at, weights, own, other):
    height, width, chans_in = own[0].shape
    filters = weights.shape[2]
    rows = height * depth * PAIR
    half = jax.ShapeDtypeStruct((rows // chans, filters, width), F32)
    return pl.pallas_call(
        functools.partial(forward_kernel, depth, chans, which),
        out_shape=(half, half),
        in_specs=[SMEM, VMEM] + [HBM] * (len(own) + len(other)),
        out_specs=(VMEM, VMEM),
        scratch_shapes=[
            pltpu.VMEM((rows + 2, width, chans_in), BF16),
            pltpu.VMEM((3 * filters, 3 * chans_in), BF16),
            pltpu.SemaphoreType.DMA((depth * PAIR,)),
        ],
        compiler_params=params(58),
        cost_estimate=cost(
            36 * rows // chans * width * chans_in * filters, 8 * rows // chans * width * (filters + chans_in)
        ),
        name="forward",
    )(at, weights, *own, *other)


def weight_kernel(depth, scale, at, cot, *refs):
    count = (len(refs) - 4) // 2
    parts = (refs[:count], refs[count : 2 * count])
    out, rows, moved, sems = refs[2 * count :]
    wait = load_rows(at, parts, rows, sems, 0, depth * PAIR - 1)
    filters, width = cot.shape[1], cot.shape[2]
    total = cot.shape[0] - 2
    chans_in = rows.shape[2]
    chunk = min(8, total)
    for spot in range(depth * PAIR):
        wait(spot)
    out[...] = jnp.zeros(out.shape, F32)

    @pl.loop(0, total // chunk)
    def _(step):
        first = step * chunk
        for row in range(chunk):
            value = cot[1 + first + row]
            wide = value.astype(F32)
            lanes = pl.ds(row * width, width)
            moved[0:filters, lanes] = lane_shift(wide, -1).astype(BF16)
            moved[filters : 2 * filters, lanes] = value
            moved[2 * filters :, lanes] = lane_shift(wide, 1).astype(BF16)
        for tap_row in range(3):
            window = rows[pl.ds(first + tap_row, chunk)].reshape(chunk * width, chans_in)
            out[tap_row] += jnp.dot(moved[...], window, preferred_element_type=F32)

    out[...] = out[...] * scale


def weight_gradient(depth, at, scale, cot, own, other):
    width, chans_in = own[0].shape[1:]
    rows, filters = cot.shape[0] - 2, cot.shape[1]
    return pl.pallas_call(
        functools.partial(weight_kernel, depth, scale),
        out_shape=jax.ShapeDtypeStruct((3, 3 * filters, chans_in), F32),
        in_specs=[SMEM, VMEM] + [HBM] * (len(own) + len(other)),
        out_specs=VMEM,
        scratch_shapes=[
            pltpu.VMEM((rows + 2, width, chans_in), BF16),
            pltpu.VMEM((3 * filters, min(8, rows) * width), BF16),
            pltpu.SemaphoreType.DMA((depth * PAIR,)),
        ],
        compiler_params=params(58),
        cost_estimate=cost(18 * rows * width * chans_in * filters, 2 * rows * width * (filters + chans_in)),
        name="weight_gradient",
    )(at, cot, *own, *other)


def turn_kernel(same, cross, out):
    fars, _, rows = same.shape[:3]
    unroll = max(n for n in (1, 2, 3, 6) if rows % n == 0)

    @pl.loop(0, rows // unroll)
    def _(step):
        for n in range(unroll):
            row = step * unroll + n
            out[0, row] = jnp.concatenate([part[far, 0, row] for far in range(fars) for part in (same, cross)], axis=0).T


def turned(same, cross):
    fars, depth, rows, part, width = same.shape
    filters = 2 * fars * part
    spec = pl.BlockSpec((fars, 1, rows, part, width), lambda d: (0, d, 0, 0, 0))
    return pl.pallas_call(
        turn_kernel,
        grid=(depth,),
        out_shape=jax.ShapeDtypeStruct((depth, rows, width, filters), BF16),
        in_specs=[spec, spec],
        out_specs=pl.BlockSpec((1, rows, width, filters), lambda d: (d, 0, 0, 0)),
        compiler_params=params(58),
        cost_estimate=cost(0, 4 * depth * rows * width * filters),
        name="turned",
    )(same, cross)


def input_kernel(chans, at, cot, kernels, keep, send, source, taps, stacked, sems):
    side, far, core = at[1], at[2], at[3]
    depth, rows, width, filters = source.shape
    rows = rows - 2
    chans_in = taps.shape[3]
    copies = []
    for n in range(depth):
        copies.append(
            (
                pltpu.make_async_copy(kernels.at[n], taps.at[n], sems.at[n, 0]),
                pltpu.make_async_copy(cot.at[n], source.at[n], sems.at[n, 1]),
            )
        )
        for copy in copies[n]:
            copy.start()
    part = filters // chans
    places = chans if part % 16 == 0 else 1
    size = filters // places
    for n in range(depth):
        copies[n][0].wait()
        for place in range(places):
            chan = lax.rem(far - place // 2 + chans // 2, chans // 2) * 2 + lax.rem(core + place, 2)
            of_chan = pl.ds(0 if places == 1 else pl.multiple_of(chan * size, size), size)
            for i in range(3):
                for j in range(3):
                    stacked[
                        pl.ds((n * 3 + i) * filters + place * size, size), pl.ds(j * chans_in, chans_in)
                    ] = taps[n, 3 * i + j, of_chan]
    for n in range(depth):
        copies[n][1].wait()
    half = rows // PAIR
    chunk = min(8, half)
    lanes = lax.broadcasted_iota(jnp.int32, (width, chans_in), 0)

    for out, of_side in ((send, 1 - side), (keep, side)):

        @pl.loop(0, half // chunk)
        def _(step):
            first = of_side * half + step * chunk
            window = [
                source[n, pl.ds(first + 2 - i, chunk)].reshape(chunk * width, filters)
                for n in range(depth)
                for i in range(3)
            ]
            if filters % 128 == 0:
                product = jnp.dot(jnp.concatenate(window, axis=1), stacked[...], preferred_element_type=F32)
            else:
                product = sum(
                    jnp.dot(value, stacked[n * filters : (n + 1) * filters], preferred_element_type=F32)
                    for n, value in enumerate(window)
                )
            for row in range(chunk):
                here = [
                    product[row * width : (row + 1) * width, j * chans_in : (j + 1) * chans_in] for j in range(3)
                ]
                before_it = jnp.where(lanes < width - 1, pltpu.roll(here[0], width - 1, 0), 0.0)
                behind_it = jnp.where(lanes >= 1, pltpu.roll(here[2], 1, 0), 0.0)
                out[step * chunk + row] = here[1] + before_it + behind_it


def input_partial(chans, at, cot, kernels):
    depth, rows, width, filters = cot.shape
    rows = rows - 2
    chans_in = kernels.shape[3]
    half = jax.ShapeDtypeStruct((rows // PAIR, width, chans_in), F32)
    return pl.pallas_call(
        functools.partial(input_kernel, chans),
        out_shape=(half, half),
        in_specs=[SMEM, HBM, HBM],
        out_specs=(VMEM, VMEM),
        scratch_shapes=[
            pltpu.VMEM(cot.shape, BF16),
            pltpu.VMEM(kernels.shape, BF16),
            pltpu.VMEM((depth * 3 * filters, 3 * chans_in), BF16),
            pltpu.SemaphoreType.DMA((depth, 2)),
        ],
        compiler_params=params(58),
        cost_estimate=cost(
            18 * rows * width * chans_in * filters * depth, 2 * depth * filters * ((rows + 2) * width + 9 * chans_in)
        ),
        name="input_gradient",
    )(at, cot, kernels)


def fars_gather(value, chans):
    got = [value]
    for step in range(1, chans // 2):
        got.append(lax.ppermute(value, "chan", [(c, (c + 2 * step) % chans) for c in range(chans)]))
    return jnp.stack(got)


def lines(depth):
    return [[z * PAIR + y for z in range(depth)] for y in range(PAIR)]


def line_step(along, step, depth):
    up = [(z * PAIR + y, (z + 1) * PAIR + y) for z in range(step - 1, depth - 1) for y in range(PAIR)]
    down = [(z * PAIR + y, (z - 1) * PAIR + y) for z in range(1, depth - step + 1) for y in range(PAIR)]
    along = dict(along)
    along[-step] = lax.ppermute(along[1 - step], "filt", up)
    along[step] = lax.ppermute(along[step - 1], "filt", down)
    if step == 1 and depth > 2:
        ends = (0, depth - 1)
        across = [(z * PAIR + y, (depth - 1 - z) * PAIR + y) for z in ends for y in range(PAIR)]
        along[depth - 1] = along[1 - depth] = lax.ppermute(along[0], "filt", across)
    return along


def core_swap(value, chans):
    return lax.ppermute(value, "chan", [(c, c ^ 1) for c in range(chans)])


def pair_swap(value, depth):
    pairs = [(z * PAIR + y, z * PAIR + 1 - y) for z in range(depth) for y in range(PAIR)]
    return lax.ppermute(value, "filt", pairs)


def body(inputs, weights, cotangent):
    chans, filts = lax.axis_size("chan"), lax.axis_size("filt")
    depth = filts // PAIR
    chan, filt = lax.axis_index("chan"), lax.axis_index("filt")
    line, side = filt // PAIR, filt % PAIR
    far, core = chan // 2, chan % 2
    spots = jnp.asarray([[z] + [z + way for way in arrivals(depth, z)] for z in range(depth)], jnp.int32)
    at = jnp.concatenate([jnp.stack([line, side, far, core]).astype(jnp.int32), spots[line]])
    own_rows, width, chans_in = inputs.shape[1:]
    block, filters = cotangent.shape[1], cotangent.shape[2]
    height = own_rows * filts
    scale = 1.0 / math.sqrt(inputs.shape[0] * height * width)

    part = filters // chans
    line_rows = own_rows * PAIR

    def all_rows(same):
        cross = core_swap(same, chans)
        padded = jnp.zeros((height + 2, filters, width), BF16)
        for step in range(chans // 2):
            at_far = lax.rem(far - step + chans // 2, chans // 2) * 2
            padded = lax.dynamic_update_slice(padded, same[step], (1 + (at_far + core) * block, 0, 0))
            padded = lax.dynamic_update_slice(padded, cross[step], (1 + (at_far + 1 - core) * block, 0, 0))
        return padded

    def line_pieces(padded):
        own_part = lax.dynamic_slice_in_dim(padded, chan * part, part, axis=1)
        return jnp.stack([own_part[z * line_rows : (z + 1) * line_rows + 2] for z in range(depth)])

    def exchange(pieces):
        return lax.all_to_all(pieces, "filt", 0, 0, axis_index_groups=lines(depth), tiled=True)

    halves = PAIR if chans_in % (PAIR * 128) == 0 else 1
    kernels = []
    for half in jnp.split(weights, halves, axis=3):
        half = half.reshape((9,) + half.shape[2:])
        kernels.append(lax.all_gather(half, "filt", axis=0, axis_index_groups=lines(depth)))

    mine, theirs = [inputs[0]], [pair_swap(inputs[0], depth)]
    same = fars_gather(cotangent[0], chans)
    along = line_step({0: inputs[0]}, 1, depth)
    fresh = theirs + [same]
    stages = max(2, depth - 1)
    for stage in range(2, stages + 1):
        ways = list(along)
        ready = lax.optimization_barrier([along[way] for way in ways] + fresh)
        along = dict(zip(ways, ready))
        if stage == 2:
            padded = all_rows(ready[-1])
            pieces = line_pieces(padded)
        elif stage == 3:
            pieces = exchange(ready[-1])
        fresh = []
        if stage < stages:
            along = line_step(along, stage, depth)
        while len(theirs) < min(depth, stage + 1):
            mine.append(arrival(along, depth, line, len(theirs) - 1))
            theirs.append(pair_swap(mine[-1], depth))
            fresh.append(theirs[-1])
        fresh.append(pieces)
    if stages < 3:
        pieces = exchange(pieces)
    same = fars_gather(pieces, chans)
    sources = turned(same, core_swap(same, chans))

    if part % 16:
        order = [(far - c // 2 + chans // 2) % (chans // 2) * 2 + (core + c) % 2 for c in range(chans)]
        split = [half.reshape((depth, 9, chans, part, -1)) for half in kernels]
        kernels = [jnp.take(half, jnp.stack(order), axis=2).reshape(kernels[0].shape) for half in split]

    outputs, came, at_next = None, [], after(at, kernels[0], pieces)
    for which in [*range(1, chans // 2), 0]:
        keep, send = forward_partial(depth, chans, which, at_next, weights, mine, theirs)
        at_next = after(at, send)
        moving = keep + core_swap(send, chans)
        if which:
            at_next = after(at_next, moving)
            moving = lax.ppermute(moving, "chan", [(c, (c + 2 * which) % chans) for c in range(chans)])
            came.append(moving)
        outputs = moving if outputs is None else outputs + moving
    outputs = outputs.astype(BF16)[None]

    input_grad = []
    for half in kernels:
        kept, sent = input_partial(chans, at_next, sources, half)
        at_next = after(at_next, sent, *came)
        input_grad.append((kept + pair_swap(sent, depth)).astype(BF16))
    at_next = after(at_next, *input_grad[:-1])
    input_grad = jnp.concatenate(input_grad, axis=2)[None]
    weight_grad = weight_gradient(depth, at_next, scale, padded, mine, theirs)
    weight_grad = weight_grad.reshape((3, 3, filters, chans_in))
    return (outputs, input_grad, weight_grad)


def solution(mesh):
    return jax.shard_map(
        body,
        mesh=mesh,
        in_specs=(
            P(None, "filt", None, "chan"),
            P(None, None, "filt", "chan"),
            P(None, "chan", "filt", None),
        ),
        out_specs=(
            P(None, "chan", "filt", None),
            P(None, "filt", None, "chan"),
            P(None, None, "filt", "chan"),
        ),
        check_vma=False,
    )
```

```python
import functools
import math

import jax
import jax.numpy as jnp
from jax import lax
from jax.experimental import pallas as pl
from jax.experimental.pallas import tpu as pltpu
from jax.sharding import PartitionSpec as P

F32 = jnp.float32
BF16 = jnp.bfloat16
NT = (((1,), (1,)), ((), ()))
HBM = pl.BlockSpec(memory_space=pltpu.HBM)
VMEM = pl.BlockSpec(memory_space=pltpu.VMEM)
SMEM = pl.BlockSpec(memory_space=pltpu.SMEM)
PAIR = 2


def params(mib):
    return pltpu.CompilerParams(vmem_limit_bytes=mib << 20)


def cost(flops, moved):
    return pl.CostEstimate(flops=int(flops), bytes_accessed=int(moved), transcendentals=0)


def lane_shift(value, by):
    size = value.shape[1]
    lane = lax.broadcasted_iota(jnp.int32, value.shape, 1)
    keep = lane >= by if by > 0 else lane < size + by
    return jnp.where(keep, pltpu.roll(value, by % size, 1), 0.0)


def after(value, *others):
    return lax.optimization_barrier((value,) + others)[0]


def arrivals(depth, line):
    ways = sorted((way for way in range(-line, depth - line) if way), key=abs)
    if abs(ways[-1]) == depth - 1:
        ways.insert(1, ways.pop())
    return ways


def arrival(along, depth, line, place):
    picked = None
    for z in range(depth):
        value = along[arrivals(depth, z)[place]]
        picked = value if picked is None or value is picked else jnp.where(line == z, value, picked)
    return picked


def load_rows(at, parts, rows, sems, first, last):
    height = parts[0][0].shape[0]

    def place(spot):
        return rows.at[pl.ds(1 + spot * height, height)]

    for half in range(PAIR):
        of_side = lax.rem(at[1] + half, PAIR)
        for index, part in enumerate(parts[half]):
            spot = at[4 + index] * PAIR + of_side

            @pl.when(jnp.logical_and(spot >= first, spot <= last))
            def _():
                pltpu.make_async_copy(part, place(spot), sems.at[spot]).start()

    rows[0] = jnp.zeros(rows.shape[1:], rows.dtype)
    rows[rows.shape[0] - 1] = jnp.zeros(rows.shape[1:], rows.dtype)
    return lambda spot: pltpu.make_async_copy(parts[0][0], place(spot), sems.at[spot]).wait()


def forward_kernel(depth, chans, which, at, weights, *refs):
    count = (len(refs) - 5) // 2
    parts = (refs[:count], refs[count : 2 * count])
    keep, send, rows, taps, sems = refs[2 * count :]
    filters, chans_in = weights.shape[2], weights.shape[3]
    width = rows.shape[1]
    block = keep.shape[0]
    height = parts[0][0].shape[0]
    far, core = at[2], at[3]
    top = lax.rem(far + which, chans // 2) * 2 * block
    first, spots = top // height, max(1, 2 * block // height)
    wait = load_rows(at, parts, rows, sems, first - 1, first + spots)
    for tap_row in range(3):
        for tap_col in range(3):
            taps[pl.ds(tap_col * filters, filters), pl.ds(tap_row * chans_in, chans_in)] = weights[tap_row, tap_col]
    for spot in range(-1, spots + 1):

        @pl.when(jnp.logical_and(first + spot >= 0, first + spot < depth * PAIR))
        def _():
            wait(first + spot)

    group = min(4, block)

    @pl.loop(0, block // group)
    def _(step):
        for target, of_core in ((send, 1 - core), (keep, core)):
            start = top + of_core * block + step * group
            window = jnp.concatenate(
                [rows[pl.ds(start + i, group)].reshape(group * width, chans_in) for i in range(3)], axis=1
            )
            product = lax.dot_general(taps[...], window, NT, preferred_element_type=F32)
            for row in range(group):
                part = [
                    product[j * filters : (j + 1) * filters, row * width : (row + 1) * width] for j in range(3)
                ]
                target[step * group + row] = part[1] + lane_shift(part[0], 1) + lane_shift(part[2], -1)


def forward_partial(depth, chans, which, at, weights, own, other):
    height, width, chans_in = own[0].shape
    filters = weights.shape[2]
    rows = height * depth * PAIR
    half = jax.ShapeDtypeStruct((rows // chans, filters, width), F32)
    return pl.pallas_call(
        functools.partial(forward_kernel, depth, chans, which),
        out_shape=(half, half),
        in_specs=[SMEM, VMEM] + [HBM] * (len(own) + len(other)),
        out_specs=(VMEM, VMEM),
        scratch_shapes=[
            pltpu.VMEM((rows + 2, width, chans_in), BF16),
            pltpu.VMEM((3 * filters, 3 * chans_in), BF16),
            pltpu.SemaphoreType.DMA((depth * PAIR,)),
        ],
        compiler_params=params(58),
        cost_estimate=cost(
            36 * rows // chans * width * chans_in * filters, 8 * rows // chans * width * (filters + chans_in)
        ),
        name="forward",
    )(at, weights, *own, *other)


def weight_kernel(depth, scale, at, cot, *refs):
    count = (len(refs) - 4) // 2
    parts = (refs[:count], refs[count : 2 * count])
    out, rows, moved, sems = refs[2 * count :]
    wait = load_rows(at, parts, rows, sems, 0, depth * PAIR - 1)
    filters, width = cot.shape[1], cot.shape[2]
    total = cot.shape[0] - 2
    chans_in = rows.shape[2]
    chunk = min(8, total)
    for spot in range(depth * PAIR):
        wait(spot)
    out[...] = jnp.zeros(out.shape, F32)

    @pl.loop(0, total // chunk)
    def _(step):
        first = step * chunk
        for row in range(chunk):
            value = cot[1 + first + row]
            wide = value.astype(F32)
            lanes = pl.ds(row * width, width)
            moved[0:filters, lanes] = lane_shift(wide, -1).astype(BF16)
            moved[filters : 2 * filters, lanes] = value
            moved[2 * filters :, lanes] = lane_shift(wide, 1).astype(BF16)
        for tap_row in range(3):
            window = rows[pl.ds(first + tap_row, chunk)].reshape(chunk * width, chans_in)
            out[tap_row] += jnp.dot(moved[...], window, preferred_element_type=F32)

    out[...] = out[...] * scale


def weight_gradient(depth, at, scale, cot, own, other):
    width, chans_in = own[0].shape[1:]
    rows, filters = cot.shape[0] - 2, cot.shape[1]
    return pl.pallas_call(
        functools.partial(weight_kernel, depth, scale),
        out_shape=jax.ShapeDtypeStruct((3, 3 * filters, chans_in), F32),
        in_specs=[SMEM, VMEM] + [HBM] * (len(own) + len(other)),
        out_specs=VMEM,
        scratch_shapes=[
            pltpu.VMEM((rows + 2, width, chans_in), BF16),
            pltpu.VMEM((3 * filters, min(8, rows) * width), BF16),
            pltpu.SemaphoreType.DMA((depth * PAIR,)),
        ],
        compiler_params=params(58),
        cost_estimate=cost(18 * rows * width * chans_in * filters, 2 * rows * width * (filters + chans_in)),
        name="weight_gradient",
    )(at, cot, *own, *other)


def turn_kernel(same, cross, out):
    fars, _, rows = same.shape[:3]
    unroll = max(n for n in (1, 2, 3, 6) if rows % n == 0)

    @pl.loop(0, rows // unroll)
    def _(step):
        for n in range(unroll):
            row = step * unroll + n
            out[0, row] = jnp.concatenate([part[far, 0, row] for far in range(fars) for part in (same, cross)], axis=0).T


def turned(same, cross):
    fars, depth, rows, part, width = same.shape
    filters = 2 * fars * part
    spec = pl.BlockSpec((fars, 1, rows, part, width), lambda d: (0, d, 0, 0, 0))
    return pl.pallas_call(
        turn_kernel,
        grid=(depth,),
        out_shape=jax.ShapeDtypeStruct((depth, rows, width, filters), BF16),
        in_specs=[spec, spec],
        out_specs=pl.BlockSpec((1, rows, width, filters), lambda d: (d, 0, 0, 0)),
        compiler_params=params(58),
        cost_estimate=cost(0, 4 * depth * rows * width * filters),
        name="turned",
    )(same, cross)


def input_kernel(chans, at, cot, kernels, keep, send, source, taps, stacked, sems):
    side, far, core = at[1], at[2], at[3]
    depth, rows, width, filters = source.shape
    rows = rows - 2
    chans_in = taps.shape[3]
    copies = []
    for n in range(depth):
        copies.append(
            (
                pltpu.make_async_copy(kernels.at[n], taps.at[n], sems.at[n, 0]),
                pltpu.make_async_copy(cot.at[n], source.at[n], sems.at[n, 1]),
            )
        )
        for copy in copies[n]:
            copy.start()
    part = filters // chans
    places = chans if part % 16 == 0 else 1
    size = filters // places
    for n in range(depth):
        copies[n][0].wait()
        for place in range(places):
            chan = lax.rem(far - place // 2 + chans // 2, chans // 2) * 2 + lax.rem(core + place, 2)
            of_chan = pl.ds(0 if places == 1 else pl.multiple_of(chan * size, size), size)
            for i in range(3):
                for j in range(3):
                    stacked[
                        pl.ds((n * 3 + i) * filters + place * size, size), pl.ds(j * chans_in, chans_in)
                    ] = taps[n, 3 * i + j, of_chan]
    for n in range(depth):
        copies[n][1].wait()
    half = rows // PAIR
    chunk = min(8, half)
    lanes = lax.broadcasted_iota(jnp.int32, (width, chans_in), 0)

    for out, of_side in ((send, 1 - side), (keep, side)):

        @pl.loop(0, half // chunk)
        def _(step):
            first = of_side * half + step * chunk
            window = [
                source[n, pl.ds(first + 2 - i, chunk)].reshape(chunk * width, filters)
                for n in range(depth)
                for i in range(3)
            ]
            if filters % 128 == 0:
                product = jnp.dot(jnp.concatenate(window, axis=1), stacked[...], preferred_element_type=F32)
            else:
                product = sum(
                    jnp.dot(value, stacked[n * filters : (n + 1) * filters], preferred_element_type=F32)
                    for n, value in enumerate(window)
                )
            for row in range(chunk):
                here = [
                    product[row * width : (row + 1) * width, j * chans_in : (j + 1) * chans_in] for j in range(3)
                ]
                before_it = jnp.where(lanes < width - 1, pltpu.roll(here[0], width - 1, 0), 0.0)
                behind_it = jnp.where(lanes >= 1, pltpu.roll(here[2], 1, 0), 0.0)
                out[step * chunk + row] = here[1] + before_it + behind_it


def input_partial(chans, at, cot, kernels):
    depth, rows, width, filters = cot.shape
    rows = rows - 2
    chans_in = kernels.shape[3]
    half = jax.ShapeDtypeStruct((rows // PAIR, width, chans_in), F32)
    return pl.pallas_call(
        functools.partial(input_kernel, chans),
        out_shape=(half, half),
        in_specs=[SMEM, HBM, HBM],
        out_specs=(VMEM, VMEM),
        scratch_shapes=[
            pltpu.VMEM(cot.shape, BF16),
            pltpu.VMEM(kernels.shape, BF16),
            pltpu.VMEM((depth * 3 * filters, 3 * chans_in), BF16),
            pltpu.SemaphoreType.DMA((depth, 2)),
        ],
        compiler_params=params(58),
        cost_estimate=cost(
            18 * rows * width * chans_in * filters * depth, 2 * depth * filters * ((rows + 2) * width + 9 * chans_in)
        ),
        name="input_gradient",
    )(at, cot, kernels)


def fars_gather(value, chans):
    got = [value]
    for step in range(1, chans // 2):
        got.append(lax.ppermute(value, "chan", [(c, (c + 2 * step) % chans) for c in range(chans)]))
    return jnp.stack(got)


def lines(depth):
    return [[z * PAIR + y for z in range(depth)] for y in range(PAIR)]


def line_step(along, step, depth):
    up = [(z * PAIR + y, (z + 1) * PAIR + y) for z in range(step - 1, depth - 1) for y in range(PAIR)]
    down = [(z * PAIR + y, (z - 1) * PAIR + y) for z in range(1, depth - step + 1) for y in range(PAIR)]
    along = dict(along)
    along[-step] = lax.ppermute(along[1 - step], "filt", up)
    along[step] = lax.ppermute(along[step - 1], "filt", down)
    if step == 1 and depth > 2:
        ends = (0, depth - 1)
        across = [(z * PAIR + y, (depth - 1 - z) * PAIR + y) for z in ends for y in range(PAIR)]
        along[depth - 1] = along[1 - depth] = lax.ppermute(along[0], "filt", across)
    return along


def core_swap(value, chans):
    return lax.ppermute(value, "chan", [(c, c ^ 1) for c in range(chans)])


def pair_swap(value, depth):
    pairs = [(z * PAIR + y, z * PAIR + 1 - y) for z in range(depth) for y in range(PAIR)]
    return lax.ppermute(value, "filt", pairs)


def body(inputs, weights, cotangent):
    chans, filts = lax.axis_size("chan"), lax.axis_size("filt")
    depth = filts // PAIR
    chan, filt = lax.axis_index("chan"), lax.axis_index("filt")
    line, side = filt // PAIR, filt % PAIR
    far, core = chan // 2, chan % 2
    spots = jnp.asarray([[z] + [z + way for way in arrivals(depth, z)] for z in range(depth)], jnp.int32)
    at = jnp.concatenate([jnp.stack([line, side, far, core]).astype(jnp.int32), spots[line]])
    own_rows, width, chans_in = inputs.shape[1:]
    block, filters = cotangent.shape[1], cotangent.shape[2]
    height = own_rows * filts
    scale = 1.0 / math.sqrt(inputs.shape[0] * height * width)

    part = filters // chans
    line_rows = own_rows * PAIR

    def all_rows(same):
        cross = core_swap(same, chans)
        padded = jnp.zeros((height + 2, filters, width), BF16)
        for step in range(chans // 2):
            at_far = lax.rem(far - step + chans // 2, chans // 2) * 2
            padded = lax.dynamic_update_slice(padded, same[step], (1 + (at_far + core) * block, 0, 0))
            padded = lax.dynamic_update_slice(padded, cross[step], (1 + (at_far + 1 - core) * block, 0, 0))
        return padded

    def line_pieces(padded):
        own_part = lax.dynamic_slice_in_dim(padded, chan * part, part, axis=1)
        return jnp.stack([own_part[z * line_rows : (z + 1) * line_rows + 2] for z in range(depth)])

    def exchange(pieces):
        return lax.all_to_all(pieces, "filt", 0, 0, axis_index_groups=lines(depth), tiled=True)

    halves = PAIR if chans_in % (PAIR * 128) == 0 else 1
    kernels = []
    for half in jnp.split(weights, halves, axis=3):
        half = half.reshape((9,) + half.shape[2:])
        kernels.append(lax.all_gather(half, "filt", axis=0, axis_index_groups=lines(depth)))

    mine, theirs = [inputs[0]], [pair_swap(inputs[0], depth)]
    same = fars_gather(cotangent[0], chans)
    along = line_step({0: inputs[0]}, 1, depth)
    fresh = theirs + [same]
    stages = max(2, depth - 1)
    for stage in range(2, stages + 1):
        late = {way: along.pop(way) for way in list(along) if stage == 2 < depth - 1 == abs(way)}
        ways = list(along)
        ready = lax.optimization_barrier([along[way] for way in ways] + fresh)
        along = dict(zip(ways, ready))
        if stage == 2:
            padded = all_rows(ready[-1])
            pieces = line_pieces(padded)
        fresh, near = [], dict(along)
        if stage < stages:
            along = line_step(along, stage, depth)
        while len(theirs) < min(depth, stage + 1):
            mine.append(arrival(near, depth, line, len(theirs) - 1))
            theirs.append(pair_swap(mine[-1], depth))
            fresh.append(theirs[-1])
            if late:
                along.update(late)
                near.update(late)
                *ready, pieces, _ = lax.optimization_barrier([*near.values(), pieces, theirs[-1]])
                near, late = dict(zip(near, ready)), {}
        if stage == 2:
            pieces = exchange(pieces)
            fresh.append(pieces)
    same = fars_gather(pieces, chans)
    sources = turned(same, core_swap(same, chans))

    if part % 16:
        order = [(far - c // 2 + chans // 2) % (chans // 2) * 2 + (core + c) % 2 for c in range(chans)]
        split = [half.reshape((depth, 9, chans, part, -1)) for half in kernels]
        kernels = [jnp.take(half, jnp.stack(order), axis=2).reshape(kernels[0].shape) for half in split]

    outputs, came, input_grad, at_next = None, [], [], after(at, kernels[0])
    for which in [*range(1, chans // 2), 0]:
        keep, send = forward_partial(depth, chans, which, at_next, weights, mine, theirs)
        at_next = after(at, send)
        moving = keep + core_swap(send, chans)
        if which:
            at_next = after(at_next, moving)
            moving = lax.ppermute(moving, "chan", [(c, (c + 2 * which) % chans) for c in range(chans)])
            came.append(moving)
        outputs = moving if outputs is None else outputs + moving
    outputs = outputs.astype(BF16)[None]
    for half in kernels:
        kept, sent = input_partial(chans, at_next, sources, half)
        at_next = after(at_next, sent, *came)
        input_grad.append((kept + pair_swap(sent, depth)).astype(BF16))
    input_grad = jnp.concatenate(input_grad, axis=2)[None]

    weight_grad = weight_gradient(depth, at_next, scale, padded, mine, theirs)
    weight_grad = weight_grad.reshape((3, 3, filters, chans_in))
    return (outputs, input_grad, weight_grad)


def solution(mesh):
    return jax.shard_map(
        body,
        mesh=mesh,
        in_specs=(
            P(None, "filt", None, "chan"),
            P(None, None, "filt", "chan"),
            P(None, "chan", "filt", None),
        ),
        out_specs=(
            P(None, "chan", "filt", None),
            P(None, "filt", None, "chan"),
            P(None, None, "filt", "chan"),
        ),
        check_vma=False,
    )
```

```python
import functools
import math

import jax
import jax.numpy as jnp
from jax import lax
from jax.experimental import pallas as pl
from jax.experimental.pallas import tpu as pltpu
from jax.sharding import PartitionSpec as P

F32 = jnp.float32
BF16 = jnp.bfloat16
NT = (((1,), (1,)), ((), ()))
HBM = pl.BlockSpec(memory_space=pltpu.HBM)
VMEM = pl.BlockSpec(memory_space=pltpu.VMEM)
SMEM = pl.BlockSpec(memory_space=pltpu.SMEM)
PAIR = 2


def params(mib):
    return pltpu.CompilerParams(vmem_limit_bytes=mib << 20)


def cost(flops, moved):
    return pl.CostEstimate(flops=int(flops), bytes_accessed=int(moved), transcendentals=0)


def lane_shift(value, by):
    size = value.shape[1]
    lane = lax.broadcasted_iota(jnp.int32, value.shape, 1)
    keep = lane >= by if by > 0 else lane < size + by
    return jnp.where(keep, pltpu.roll(value, by % size, 1), 0.0)


def after(value, *others):
    return lax.optimization_barrier((value,) + others)[0]


def arrivals(depth, line):
    ways = sorted((way for way in range(-line, depth - line) if way), key=abs)
    if abs(ways[-1]) == depth - 1:
        ways.insert(1, ways.pop())
    return ways


def arrival(along, depth, line, place):
    picked = None
    for z in range(depth):
        value = along[arrivals(depth, z)[place]]
        picked = value if picked is None or value is picked else jnp.where(line == z, value, picked)
    return picked


def load_rows(at, parts, rows, sems, first, last):
    height = parts[0][0].shape[0]

    def place(spot):
        return rows.at[pl.ds(1 + spot * height, height)]

    for half in range(PAIR):
        of_side = lax.rem(at[1] + half, PAIR)
        for index, part in enumerate(parts[half]):
            spot = at[4 + index] * PAIR + of_side

            @pl.when(jnp.logical_and(spot >= first, spot <= last))
            def _():
                pltpu.make_async_copy(part, place(spot), sems.at[spot]).start()

    rows[0] = jnp.zeros(rows.shape[1:], rows.dtype)
    rows[rows.shape[0] - 1] = jnp.zeros(rows.shape[1:], rows.dtype)
    return lambda spot: pltpu.make_async_copy(parts[0][0], place(spot), sems.at[spot]).wait()


def forward_kernel(depth, chans, which, at, weights, *refs):
    count = (len(refs) - 8) // 2
    parts = (refs[:count], refs[count : 2 * count])
    keep, send, rows, taps, made, sems, tap_sems, out_sems = refs[2 * count :]
    filters, chans_in = weights.shape[2], weights.shape[3]
    width = rows.shape[1]
    block = keep.shape[0]
    height = parts[0][0].shape[0]
    far, core = at[2], at[3]
    top = lax.rem(far + which, chans // 2) * 2 * block
    first, spots = top // height, max(1, 2 * block // height)
    wait = load_rows(at, parts, rows, sems, first - 1, first + spots)
    fetches = [
        pltpu.make_async_copy(
            weights.at[tap_row, tap_col],
            taps.at[pl.ds(tap_col * filters, filters), pl.ds(tap_row * chans_in, chans_in)],
            tap_sems.at[tap_row, tap_col],
        )
        for tap_row in range(3)
        for tap_col in range(3)
    ]
    for fetch in fetches:
        fetch.start()
    for fetch in fetches:
        fetch.wait()
    for spot in range(-1, spots + 1):

        @pl.when(jnp.logical_and(first + spot >= 0, first + spot < depth * PAIR))
        def _():
            wait(first + spot)

    group = min(4, block)

    def result(step, place):
        chosen = pl.ds(step * group, group)
        return pltpu.make_async_copy(made.at[place, chosen], (send, keep)[place].at[chosen], out_sems.at[place, step])

    @pl.loop(0, block // group)
    def _(step):
        for place, of_core in enumerate((1 - core, core)):
            start = top + of_core * block + step * group
            window = jnp.concatenate(
                [rows[pl.ds(start + i, group)].reshape(group * width, chans_in) for i in range(3)], axis=1
            )
            product = lax.dot_general(taps[...], window, NT, preferred_element_type=F32)
            for row in range(group):
                part = [
                    product[j * filters : (j + 1) * filters, row * width : (row + 1) * width] for j in range(3)
                ]
                made[place, step * group + row] = part[1] + lane_shift(part[0], 1) + lane_shift(part[2], -1)
            result(step, place).start()

    for step in range(block // group):
        for place in range(2):
            result(step, place).wait()


def forward_partial(depth, chans, which, at, weights, own, other):
    height, width, chans_in = own[0].shape
    filters = weights.shape[2]
    rows = height * depth * PAIR
    half = jax.ShapeDtypeStruct((rows // chans, filters, width), F32)
    return pl.pallas_call(
        functools.partial(forward_kernel, depth, chans, which),
        out_shape=(half, half),
        in_specs=[SMEM, HBM] + [HBM] * (len(own) + len(other)),
        out_specs=(HBM, HBM),
        scratch_shapes=[
            pltpu.VMEM((rows + 2, width, chans_in), BF16),
            pltpu.VMEM((3 * filters, 3 * chans_in), BF16),
            pltpu.VMEM((2, rows // chans, filters, width), F32),
            pltpu.SemaphoreType.DMA((depth * PAIR,)),
            pltpu.SemaphoreType.DMA((3, 3)),
            pltpu.SemaphoreType.DMA((2, rows // chans // min(4, rows // chans))),
        ],
        compiler_params=params(58),
        cost_estimate=cost(
            36 * rows // chans * width * chans_in * filters, 8 * rows // chans * width * (filters + chans_in)
        ),
        name="forward",
    )(at, weights, *own, *other)


def weight_kernel(depth, scale, at, cot, *refs):
    count = (len(refs) - 7) // 2
    parts = (refs[:count], refs[count : 2 * count])
    out, rows, cots, moved, total, sems, cot_sems = refs[2 * count :]
    wait = load_rows(at, parts, rows, sems, 0, depth * PAIR - 1)
    filters, width = cot.shape[1], cot.shape[2]
    chans_in = rows.shape[2]
    height = parts[0][0].shape[0]
    steps, chunk = cots.shape[0], cots.shape[1]

    def fetch(step):
        return pltpu.make_async_copy(cot.at[pl.ds(1 + step * chunk, chunk)], cots.at[step], cot_sems.at[step])

    for step in range(steps):
        fetch(step).start()
    total[...] = jnp.zeros(total.shape, F32)
    wait(0)

    @pl.loop(0, steps)
    def _(step):
        first = step * chunk
        fetch(step).wait()
        for spot in range(max(1, chunk // height)):
            after_it = first // height + spot + 1

            @pl.when(after_it < depth * PAIR)
            def _():
                wait(after_it)

        for row in range(chunk):
            value = cots[step, row]
            wide = value.astype(F32)
            lanes = pl.ds(row * width, width)
            moved[0:filters, lanes] = lane_shift(wide, -1).astype(BF16)
            moved[filters : 2 * filters, lanes] = value
            moved[2 * filters :, lanes] = lane_shift(wide, 1).astype(BF16)
        for tap_row in range(3):
            window = rows[pl.ds(first + tap_row, chunk)].reshape(chunk * width, chans_in)
            total[tap_row] += jnp.dot(moved[...], window, preferred_element_type=F32)

    stores = []
    for tap_row in range(3):
        total[tap_row] = total[tap_row] * scale
        for tap_col in range(3):
            chosen = (tap_row, pl.ds(tap_col * filters, filters))
            stores.append(pltpu.make_async_copy(total.at[chosen], out.at[chosen], cot_sems.at[steps + 3 * tap_row + tap_col]))
            stores[-1].start()
    for store in stores:
        store.wait()


def weight_gradient(depth, at, scale, cot, own, other):
    height, width, chans_in = own[0].shape
    rows, filters = cot.shape[0] - 2, cot.shape[1]
    chunk = max(height, min(8, rows))
    return pl.pallas_call(
        functools.partial(weight_kernel, depth, scale),
        out_shape=jax.ShapeDtypeStruct((3, 3 * filters, chans_in), F32),
        in_specs=[SMEM, HBM] + [HBM] * (len(own) + len(other)),
        out_specs=HBM,
        scratch_shapes=[
            pltpu.VMEM((rows + 2, width, chans_in), BF16),
            pltpu.VMEM((rows // chunk, chunk, filters, width), BF16),
            pltpu.VMEM((3 * filters, chunk * width), BF16),
            pltpu.VMEM((3, 3 * filters, chans_in), F32),
            pltpu.SemaphoreType.DMA((depth * PAIR,)),
            pltpu.SemaphoreType.DMA((rows // chunk + 9,)),
        ],
        compiler_params=params(58),
        cost_estimate=cost(18 * rows * width * chans_in * filters, 2 * rows * width * (filters + chans_in)),
        name="weight_gradient",
    )(at, cot, *own, *other)


def turn_kernel(same, cross, out):
    fars, _, rows = same.shape[:3]
    unroll = max(n for n in (1, 2, 3, 6) if rows % n == 0)

    @pl.loop(0, rows // unroll)
    def _(step):
        for n in range(unroll):
            row = step * unroll + n
            out[0, row] = jnp.concatenate([part[far, 0, row] for far in range(fars) for part in (same, cross)], axis=0).T


def turned(same, cross):
    fars, depth, rows, part, width = same.shape
    filters = 2 * fars * part
    spec = pl.BlockSpec((fars, 1, rows, part, width), lambda d: (0, d, 0, 0, 0))
    return pl.pallas_call(
        turn_kernel,
        grid=(depth,),
        out_shape=jax.ShapeDtypeStruct((depth, rows, width, filters), BF16),
        in_specs=[spec, spec],
        out_specs=pl.BlockSpec((1, rows, width, filters), lambda d: (d, 0, 0, 0)),
        compiler_params=params(58),
        cost_estimate=cost(0, 4 * depth * rows * width * filters),
        name="turned",
    )(same, cross)


def input_kernel(chans, at, cot, kernels, keep, send, source, taps, stacked, made, sems, out_sems):
    side, far, core = at[1], at[2], at[3]
    depth, rows, width, filters = source.shape
    rows = rows - 2
    chans_in = taps.shape[3]
    copies = []
    for n in range(depth):
        copies.append(
            (
                pltpu.make_async_copy(kernels.at[n], taps.at[n], sems.at[n, 0]),
                [
                    pltpu.make_async_copy(
                        cot.at[n, pl.ds(first, (rows + 2) // 2)],
                        source.at[n, pl.ds(first, (rows + 2) // 2)],
                        sems.at[n, 1 + (first > 0)],
                    )
                    for first in (0, (rows + 2) // 2)
                ],
            )
        )
        copies[n][0].start()
    for n in range(depth):
        for copy in copies[n][1]:
            copy.start()
    part = filters // chans
    places = chans if part % 16 == 0 else 1
    size = filters // places
    for n in range(depth):
        copies[n][0].wait()
        for place in range(places):
            chan = lax.rem(far - place // 2 + chans // 2, chans // 2) * 2 + lax.rem(core + place, 2)
            of_chan = pl.ds(0 if places == 1 else pl.multiple_of(chan * size, size), size)
            for i in range(3):
                for j in range(3):
                    stacked[
                        pl.ds((n * 3 + i) * filters + place * size, size), pl.ds(j * chans_in, chans_in)
                    ] = taps[n, 3 * i + j, of_chan]
    for n in range(depth):
        for copy in copies[n][1]:
            copy.wait()
    half = rows // PAIR
    chunk = min(4, half)
    lanes = lax.broadcasted_iota(jnp.int32, (width, chans_in), 0)

    def result(place, step):
        chosen = pl.ds(step * chunk, chunk)
        return pltpu.make_async_copy(made.at[place, chosen], (send, keep)[place].at[chosen], out_sems.at[place, step])

    for place, of_side in enumerate((1 - side, side)):
        for step in range(half // chunk):
            first = of_side * half + step * chunk
            window = [
                source[n, pl.ds(first + 2 - i, chunk)].reshape(chunk * width, filters)
                for n in range(depth)
                for i in range(3)
            ]
            if filters % 128 == 0:
                product = jnp.dot(jnp.concatenate(window, axis=1), stacked[...], preferred_element_type=F32)
            else:
                product = sum(
                    jnp.dot(value, stacked[n * filters : (n + 1) * filters], preferred_element_type=F32)
                    for n, value in enumerate(window)
                )
            for row in range(chunk):
                here = [
                    product[row * width : (row + 1) * width, j * chans_in : (j + 1) * chans_in] for j in range(3)
                ]
                before_it = jnp.where(lanes < width - 1, pltpu.roll(here[0], width - 1, 0), 0.0)
                behind_it = jnp.where(lanes >= 1, pltpu.roll(here[2], 1, 0), 0.0)
                made[place, step * chunk + row] = here[1] + before_it + behind_it
            result(place, step).start()

    for place in range(2):
        for step in range(half // chunk):
            result(place, step).wait()


def input_partial(chans, at, cot, kernels):
    depth, rows, width, filters = cot.shape
    rows = rows - 2
    chans_in = kernels.shape[3]
    half = jax.ShapeDtypeStruct((rows // PAIR, width, chans_in), F32)
    return pl.pallas_call(
        functools.partial(input_kernel, chans),
        out_shape=(half, half),
        in_specs=[SMEM, HBM, HBM],
        out_specs=(HBM, HBM),
        scratch_shapes=[
            pltpu.VMEM(cot.shape, BF16),
            pltpu.VMEM(kernels.shape, BF16),
            pltpu.VMEM((depth * 3 * filters, 3 * chans_in), BF16),
            pltpu.VMEM((PAIR, rows // PAIR, width, chans_in), F32),
            pltpu.SemaphoreType.DMA((depth, 3)),
            pltpu.SemaphoreType.DMA((PAIR, rows // PAIR // min(4, rows // PAIR))),
        ],
        compiler_params=params(58),
        cost_estimate=cost(
            18 * rows * width * chans_in * filters * depth, 2 * depth * filters * ((rows + 2) * width + 9 * chans_in)
        ),
        name="input_gradient",
    )(at, cot, kernels)


def fars_gather(value, chans):
    got = [value]
    for step in range(1, chans // 2):
        got.append(lax.ppermute(value, "chan", [(c, (c + 2 * step) % chans) for c in range(chans)]))
    return jnp.stack(got)


def lines(depth):
    return [[z * PAIR + y for z in range(depth)] for y in range(PAIR)]


def line_step(along, step, depth):
    up = [(z * PAIR + y, (z + 1) * PAIR + y) for z in range(step - 1, depth - 1) for y in range(PAIR)]
    down = [(z * PAIR + y, (z - 1) * PAIR + y) for z in range(1, depth - step + 1) for y in range(PAIR)]
    along = dict(along)
    along[-step] = lax.ppermute(along[1 - step], "filt", up)
    along[step] = lax.ppermute(along[step - 1], "filt", down)
    if step == 1 and depth > 2:
        ends = (0, depth - 1)
        across = [(z * PAIR + y, (depth - 1 - z) * PAIR + y) for z in ends for y in range(PAIR)]
        along[depth - 1] = along[1 - depth] = lax.ppermute(along[0], "filt", across)
    return along


def core_swap(value, chans):
    return lax.ppermute(value, "chan", [(c, c ^ 1) for c in range(chans)])


def pair_swap(value, depth):
    pairs = [(z * PAIR + y, z * PAIR + 1 - y) for z in range(depth) for y in range(PAIR)]
    return lax.ppermute(value, "filt", pairs)


def body(inputs, weights, cotangent):
    chans, filts = lax.axis_size("chan"), lax.axis_size("filt")
    depth = filts // PAIR
    chan, filt = lax.axis_index("chan"), lax.axis_index("filt")
    line, side = filt // PAIR, filt % PAIR
    far, core = chan // 2, chan % 2
    spots = jnp.asarray([[z] + [z + way for way in arrivals(depth, z)] for z in range(depth)], jnp.int32)
    at = jnp.concatenate([jnp.stack([line, side, far, core]).astype(jnp.int32), spots[line]])
    own_rows, width, chans_in = inputs.shape[1:]
    block, filters = cotangent.shape[1], cotangent.shape[2]
    height = own_rows * filts
    scale = 1.0 / math.sqrt(inputs.shape[0] * height * width)

    part = filters // chans
    line_rows = own_rows * PAIR

    def all_rows(same):
        cross = core_swap(same, chans)
        padded = jnp.zeros((height + 2, filters, width), BF16)
        for step in range(chans // 2):
            at_far = lax.rem(far - step + chans // 2, chans // 2) * 2
            padded = lax.dynamic_update_slice(padded, same[step], (1 + (at_far + core) * block, 0, 0))
            padded = lax.dynamic_update_slice(padded, cross[step], (1 + (at_far + 1 - core) * block, 0, 0))
        return padded

    def line_pieces(padded):
        own_part = lax.dynamic_slice_in_dim(padded, chan * part, part, axis=1)
        return jnp.stack([own_part[z * line_rows : (z + 1) * line_rows + 2] for z in range(depth)])

    def exchange(pieces):
        return lax.all_to_all(pieces, "filt", 0, 0, axis_index_groups=lines(depth), tiled=True)

    halves = PAIR if chans_in % (PAIR * 128) == 0 else 1
    kernels = []
    for half in jnp.split(weights, halves, axis=3):
        half = half.reshape((9,) + half.shape[2:])
        kernels.append(lax.all_gather(half, "filt", axis=0, axis_index_groups=lines(depth)))

    mine, theirs = [inputs[0]], [pair_swap(inputs[0], depth)]
    same = fars_gather(cotangent[0], chans)
    along = line_step({0: inputs[0]}, 1, depth)
    fresh = theirs + [same]
    stages = max(2, depth - 1)
    for stage in range(2, stages + 1):
        ways = list(along)
        ready = lax.optimization_barrier([along[way] for way in ways] + fresh)
        along = dict(zip(ways, ready))
        if stage == 2:
            padded = all_rows(ready[-1])
            pieces = line_pieces(padded)
        elif stage == 3:
            pieces = exchange(ready[-1])
        fresh = []
        if stage < stages:
            along = line_step(along, stage, depth)
        while len(theirs) < min(depth, stage + 1):
            mine.append(arrival(along, depth, line, len(theirs) - 1))
            theirs.append(pair_swap(mine[-1], depth))
            fresh.append(theirs[-1])
        fresh.append(pieces)
    if stages < 3:
        pieces = exchange(pieces)
    same = fars_gather(pieces, chans)
    sources = turned(same, core_swap(same, chans))

    if part % 16:
        order = [(far - c // 2 + chans // 2) % (chans // 2) * 2 + (core + c) % 2 for c in range(chans)]
        split = [half.reshape((depth, 9, chans, part, -1)) for half in kernels]
        kernels = [jnp.take(half, jnp.stack(order), axis=2).reshape(kernels[0].shape) for half in split]

    outputs, came, at_next = None, [], after(at, kernels[0], pieces)
    for which in [*range(1, chans // 2), 0]:
        keep, send = forward_partial(depth, chans, which, at_next, weights, mine, theirs)
        at_next = after(at, send)
        moving = keep + core_swap(send, chans)
        if which:
            at_next = after(at_next, moving)
            moving = lax.ppermute(moving, "chan", [(c, (c + 2 * which) % chans) for c in range(chans)])
            came.append(moving)
        outputs = moving if outputs is None else outputs + moving
    outputs = outputs.astype(BF16)[None]

    input_grad = []
    for half in kernels:
        kept, sent = input_partial(chans, at_next, sources, half)
        at_next = after(at_next, sent, *came)
        input_grad.append((kept + pair_swap(sent, depth)).astype(BF16))
    at_next = after(at_next, *input_grad[:-1])
    input_grad = jnp.concatenate(input_grad, axis=2)[None]
    weight_grad = weight_gradient(depth, at_next, scale, padded, mine, theirs)
    weight_grad = weight_grad.reshape((3, 3, filters, chans_in))
    return (outputs, input_grad, weight_grad)


def solution(mesh):
    return jax.shard_map(
        body,
        mesh=mesh,
        in_specs=(
            P(None, "filt", None, "chan"),
            P(None, None, "filt", "chan"),
            P(None, "chan", "filt", None),
        ),
        out_specs=(
            P(None, "chan", "filt", None),
            P(None, "filt", None, "chan"),
            P(None, None, "filt", "chan"),
        ),
        check_vma=False,
    )
```

```python
import functools
import math

import jax
import jax.numpy as jnp
from jax import lax
from jax.experimental import pallas as pl
from jax.experimental.pallas import tpu as pltpu
from jax.sharding import PartitionSpec as P

F32 = jnp.float32
BF16 = jnp.bfloat16
NT = (((1,), (1,)), ((), ()))
HBM = pl.BlockSpec(memory_space=pltpu.HBM)
VMEM = pl.BlockSpec(memory_space=pltpu.VMEM)
SMEM = pl.BlockSpec(memory_space=pltpu.SMEM)
PAIR = 2


def params(mib):
    return pltpu.CompilerParams(vmem_limit_bytes=mib << 20)


def cost(flops, moved):
    return pl.CostEstimate(flops=int(flops), bytes_accessed=int(moved), transcendentals=0)


def lane_shift(value, by):
    size = value.shape[1]
    lane = lax.broadcasted_iota(jnp.int32, value.shape, 1)
    keep = lane >= by if by > 0 else lane < size + by
    return jnp.where(keep, pltpu.roll(value, by % size, 1), 0.0)


def after(value, *others):
    return lax.optimization_barrier((value,) + others)[0]


def arrivals(depth, line):
    ways = sorted((way for way in range(-line, depth - line) if way), key=abs)
    if abs(ways[-1]) == depth - 1:
        ways.insert(1, ways.pop())
    return ways


def arrival(along, depth, line, place):
    picked = None
    for z in range(depth):
        value = along[arrivals(depth, z)[place]]
        picked = value if picked is None or value is picked else jnp.where(line == z, value, picked)
    return picked


def load_rows(at, parts, rows, sems, first, last):
    height = parts[0][0].shape[0]

    def place(spot):
        return rows.at[pl.ds(1 + spot * height, height)]

    for half in range(PAIR):
        of_side = lax.rem(at[1] + half, PAIR)
        for index, part in enumerate(parts[half]):
            spot = at[4 + index] * PAIR + of_side

            @pl.when(jnp.logical_and(spot >= first, spot <= last))
            def _():
                pltpu.make_async_copy(part, place(spot), sems.at[spot]).start()

    rows[0] = jnp.zeros(rows.shape[1:], rows.dtype)
    rows[rows.shape[0] - 1] = jnp.zeros(rows.shape[1:], rows.dtype)
    return lambda spot: pltpu.make_async_copy(parts[0][0], place(spot), sems.at[spot]).wait()


def forward_kernel(depth, chans, which, at, weights, *refs):
    count = (len(refs) - 8) // 2
    parts = (refs[:count], refs[count : 2 * count])
    keep, send, rows, taps, made, sems, tap_sems, out_sems = refs[2 * count :]
    filters, chans_in = weights.shape[2], weights.shape[3]
    width = rows.shape[1]
    block = keep.shape[0]
    height = parts[0][0].shape[0]
    far, core = at[2], at[3]
    top = lax.rem(far + which, chans // 2) * 2 * block
    first, spots = top // height, max(1, 2 * block // height)
    wait = load_rows(at, parts, rows, sems, first - 1, first + spots)
    fetches = [
        pltpu.make_async_copy(
            weights.at[tap_row, tap_col],
            taps.at[pl.ds(tap_col * filters, filters), pl.ds(tap_row * chans_in, chans_in)],
            tap_sems.at[tap_row, tap_col],
        )
        for tap_row in range(3)
        for tap_col in range(3)
    ]
    for fetch in fetches:
        fetch.start()
    for fetch in fetches:
        fetch.wait()
    for spot in range(-1, spots + 1):

        @pl.when(jnp.logical_and(first + spot >= 0, first + spot < depth * PAIR))
        def _():
            wait(first + spot)

    group = min(4, block)

    def result(step, place):
        chosen = pl.ds(step * group, group)
        return pltpu.make_async_copy(made.at[place, chosen], (send, keep)[place].at[chosen], out_sems.at[place, step])

    @pl.loop(0, block // group)
    def _(step):
        for place, of_core in enumerate((1 - core, core)):
            start = top + of_core * block + step * group
            window = jnp.concatenate(
                [rows[pl.ds(start + i, group)].reshape(group * width, chans_in) for i in range(3)], axis=1
            )
            product = lax.dot_general(taps[...], window, NT, preferred_element_type=F32)
            for row in range(group):
                part = [
                    product[j * filters : (j + 1) * filters, row * width : (row + 1) * width] for j in range(3)
                ]
                made[place, step * group + row] = part[1] + lane_shift(part[0], 1) + lane_shift(part[2], -1)
            result(step, place).start()

    for step in range(block // group):
        for place in range(2):
            result(step, place).wait()


def forward_partial(depth, chans, which, at, weights, own, other):
    height, width, chans_in = own[0].shape
    filters = weights.shape[2]
    rows = height * depth * PAIR
    half = jax.ShapeDtypeStruct((rows // chans, filters, width), F32)
    return pl.pallas_call(
        functools.partial(forward_kernel, depth, chans, which),
        out_shape=(half, half),
        in_specs=[SMEM, HBM] + [HBM] * (len(own) + len(other)),
        out_specs=(HBM, HBM),
        scratch_shapes=[
            pltpu.VMEM((rows + 2, width, chans_in), BF16),
            pltpu.VMEM((3 * filters, 3 * chans_in), BF16),
            pltpu.VMEM((2, rows // chans, filters, width), F32),
            pltpu.SemaphoreType.DMA((depth * PAIR,)),
            pltpu.SemaphoreType.DMA((3, 3)),
            pltpu.SemaphoreType.DMA((2, rows // chans // min(4, rows // chans))),
        ],
        compiler_params=params(58),
        cost_estimate=cost(
            36 * rows // chans * width * chans_in * filters, 8 * rows // chans * width * (filters + chans_in)
        ),
        name="forward",
    )(at, weights, *own, *other)


def weight_kernel(depth, scale, at, cot, *refs):
    count = (len(refs) - 7) // 2
    parts = (refs[:count], refs[count : 2 * count])
    out, rows, cots, moved, total, sems, cot_sems = refs[2 * count :]
    wait = load_rows(at, parts, rows, sems, 0, depth * PAIR - 1)
    filters, width = cot.shape[1], cot.shape[2]
    chans_in = rows.shape[2]
    height = parts[0][0].shape[0]
    steps, chunk = cots.shape[0], cots.shape[1]

    def fetch(step):
        return pltpu.make_async_copy(cot.at[pl.ds(1 + step * chunk, chunk)], cots.at[step], cot_sems.at[step])

    for step in range(steps):
        fetch(step).start()
    total[...] = jnp.zeros(total.shape, F32)
    wait(0)

    @pl.loop(0, steps)
    def _(step):
        first = step * chunk
        fetch(step).wait()
        for spot in range(max(1, chunk // height)):
            after_it = first // height + spot + 1

            @pl.when(after_it < depth * PAIR)
            def _():
                wait(after_it)

        for row in range(chunk):
            value = cots[step, row]
            wide = value.astype(F32)
            lanes = pl.ds(row * width, width)
            moved[0:filters, lanes] = lane_shift(wide, -1).astype(BF16)
            moved[filters : 2 * filters, lanes] = value
            moved[2 * filters :, lanes] = lane_shift(wide, 1).astype(BF16)
        for tap_row in range(3):
            window = rows[pl.ds(first + tap_row, chunk)].reshape(chunk * width, chans_in)
            total[tap_row] += jnp.dot(moved[...], window, preferred_element_type=F32)

    stores = []
    for tap_row in range(3):
        total[tap_row] = total[tap_row] * scale
        for tap_col in range(3):
            chosen = (tap_row, pl.ds(tap_col * filters, filters))
            stores.append(pltpu.make_async_copy(total.at[chosen], out.at[chosen], cot_sems.at[steps + 3 * tap_row + tap_col]))
            stores[-1].start()
    for store in stores:
        store.wait()


def weight_gradient(depth, at, scale, cot, own, other):
    height, width, chans_in = own[0].shape
    rows, filters = cot.shape[0] - 2, cot.shape[1]
    chunk = max(height, min(8, rows))
    return pl.pallas_call(
        functools.partial(weight_kernel, depth, scale),
        out_shape=jax.ShapeDtypeStruct((3, 3 * filters, chans_in), F32),
        in_specs=[SMEM, HBM] + [HBM] * (len(own) + len(other)),
        out_specs=HBM,
        scratch_shapes=[
            pltpu.VMEM((rows + 2, width, chans_in), BF16),
            pltpu.VMEM((rows // chunk, chunk, filters, width), BF16),
            pltpu.VMEM((3 * filters, chunk * width), BF16),
            pltpu.VMEM((3, 3 * filters, chans_in), F32),
            pltpu.SemaphoreType.DMA((depth * PAIR,)),
            pltpu.SemaphoreType.DMA((rows // chunk + 9,)),
        ],
        compiler_params=params(58),
        cost_estimate=cost(18 * rows * width * chans_in * filters, 2 * rows * width * (filters + chans_in)),
        name="weight_gradient",
    )(at, cot, *own, *other)


def turn_kernel(same, cross, out):
    fars, _, rows = same.shape[:3]
    unroll = max(n for n in (1, 2, 3, 6) if rows % n == 0)

    @pl.loop(0, rows // unroll)
    def _(step):
        for n in range(unroll):
            row = step * unroll + n
            out[0, row] = jnp.concatenate([part[far, 0, row] for far in range(fars) for part in (same, cross)], axis=0).T


def turned(same, cross):
    fars, depth, rows, part, width = same.shape
    filters = 2 * fars * part
    spec = pl.BlockSpec((fars, 1, rows, part, width), lambda d: (0, d, 0, 0, 0))
    return pl.pallas_call(
        turn_kernel,
        grid=(depth,),
        out_shape=jax.ShapeDtypeStruct((depth, rows, width, filters), BF16),
        in_specs=[spec, spec],
        out_specs=pl.BlockSpec((1, rows, width, filters), lambda d: (d, 0, 0, 0)),
        compiler_params=params(58),
        cost_estimate=cost(0, 4 * depth * rows * width * filters),
        name="turned",
    )(same, cross)


def input_kernel(chans, index, at, cot, kernels, keep, send, source, taps, stacked, made, sems, out_sems):
    side, far, core = at[1], at[2], at[3]
    depth, rows, width, filters = source.shape
    rows = rows - 2
    chans_in = taps.shape[3]
    copies = []
    for n in range(depth):
        copies.append(
            (
                pltpu.make_async_copy(
                    kernels.at[n, :, :, pl.ds(index * chans_in, chans_in)], taps.at[n], sems.at[n, 0]
                ),
                [
                    pltpu.make_async_copy(
                        cot.at[n, pl.ds(first, (rows + 2) // 2)],
                        source.at[n, pl.ds(first, (rows + 2) // 2)],
                        sems.at[n, 1 + (first > 0)],
                    )
                    for first in (0, (rows + 2) // 2)
                ],
            )
        )
        copies[n][0].start()
    for n in range(depth):
        for copy in copies[n][1]:
            copy.start()
    part = filters // chans
    places = chans if part % 16 == 0 else 1
    size = filters // places
    for n in range(depth):
        copies[n][0].wait()
        for place in range(places):
            chan = lax.rem(far - place // 2 + chans // 2, chans // 2) * 2 + lax.rem(core + place, 2)
            of_chan = pl.ds(0 if places == 1 else pl.multiple_of(chan * size, size), size)
            for i in range(3):
                for j in range(3):
                    stacked[
                        pl.ds((n * 3 + i) * filters + place * size, size), pl.ds(j * chans_in, chans_in)
                    ] = taps[n, 3 * i + j, of_chan]
    for n in range(depth):
        for copy in copies[n][1]:
            copy.wait()
    half = rows // PAIR
    chunk = min(4, half)
    lanes = lax.broadcasted_iota(jnp.int32, (width, chans_in), 0)

    def result(place, step):
        chosen = pl.ds(step * chunk, chunk)
        return pltpu.make_async_copy(made.at[place, chosen], (send, keep)[place].at[chosen], out_sems.at[place, step])

    for place, of_side in enumerate((1 - side, side)):
        for step in range(half // chunk):
            first = of_side * half + step * chunk
            window = [
                source[n, pl.ds(first + 2 - i, chunk)].reshape(chunk * width, filters)
                for n in range(depth)
                for i in range(3)
            ]
            if filters % 128 == 0:
                product = jnp.dot(jnp.concatenate(window, axis=1), stacked[...], preferred_element_type=F32)
            else:
                product = sum(
                    jnp.dot(value, stacked[n * filters : (n + 1) * filters], preferred_element_type=F32)
                    for n, value in enumerate(window)
                )
            for row in range(chunk):
                here = [
                    product[row * width : (row + 1) * width, j * chans_in : (j + 1) * chans_in] for j in range(3)
                ]
                before_it = jnp.where(lanes < width - 1, pltpu.roll(here[0], width - 1, 0), 0.0)
                behind_it = jnp.where(lanes >= 1, pltpu.roll(here[2], 1, 0), 0.0)
                made[place, step * chunk + row] = here[1] + before_it + behind_it
            result(place, step).start()

    for place in range(2):
        for step in range(half // chunk):
            result(place, step).wait()


def input_partial(chans, at, cot, kernels, index, halves):
    depth, rows, width, filters = cot.shape
    rows = rows - 2
    chans_in = kernels.shape[3] // halves
    half = jax.ShapeDtypeStruct((rows // PAIR, width, chans_in), F32)
    return pl.pallas_call(
        functools.partial(input_kernel, chans, index),
        out_shape=(half, half),
        in_specs=[SMEM, HBM, HBM],
        out_specs=(HBM, HBM),
        scratch_shapes=[
            pltpu.VMEM(cot.shape, BF16),
            pltpu.VMEM(kernels.shape[:3] + (chans_in,), BF16),
            pltpu.VMEM((depth * 3 * filters, 3 * chans_in), BF16),
            pltpu.VMEM((PAIR, rows // PAIR, width, chans_in), F32),
            pltpu.SemaphoreType.DMA((depth, 3)),
            pltpu.SemaphoreType.DMA((PAIR, rows // PAIR // min(4, rows // PAIR))),
        ],
        compiler_params=params(58),
        cost_estimate=cost(
            18 * rows * width * chans_in * filters * depth, 2 * depth * filters * ((rows + 2) * width + 9 * chans_in)
        ),
        name="input_gradient",
    )(at, cot, kernels)


def fars_gather(value, chans):
    got = [value]
    for step in range(1, chans // 2):
        got.append(lax.ppermute(value, "chan", [(c, (c + 2 * step) % chans) for c in range(chans)]))
    return jnp.stack(got)


def lines(depth):
    return [[z * PAIR + y for z in range(depth)] for y in range(PAIR)]


def line_step(along, step, depth):
    up = [(z * PAIR + y, (z + 1) * PAIR + y) for z in range(step - 1, depth - 1) for y in range(PAIR)]
    down = [(z * PAIR + y, (z - 1) * PAIR + y) for z in range(1, depth - step + 1) for y in range(PAIR)]
    along = dict(along)
    along[-step] = lax.ppermute(along[1 - step], "filt", up)
    along[step] = lax.ppermute(along[step - 1], "filt", down)
    if step == 1 and depth > 2:
        ends = (0, depth - 1)
        across = [(z * PAIR + y, (depth - 1 - z) * PAIR + y) for z in ends for y in range(PAIR)]
        along[depth - 1] = along[1 - depth] = lax.ppermute(along[0], "filt", across)
    return along


def core_swap(value, chans):
    return lax.ppermute(value, "chan", [(c, c ^ 1) for c in range(chans)])


def pair_swap(value, depth):
    pairs = [(z * PAIR + y, z * PAIR + 1 - y) for z in range(depth) for y in range(PAIR)]
    return lax.ppermute(value, "filt", pairs)


def body(inputs, weights, cotangent):
    chans, filts = lax.axis_size("chan"), lax.axis_size("filt")
    depth = filts // PAIR
    chan, filt = lax.axis_index("chan"), lax.axis_index("filt")
    line, side = filt // PAIR, filt % PAIR
    far, core = chan // 2, chan % 2
    spots = jnp.asarray([[z] + [z + way for way in arrivals(depth, z)] for z in range(depth)], jnp.int32)
    at = jnp.concatenate([jnp.stack([line, side, far, core]).astype(jnp.int32), spots[line]])
    own_rows, width, chans_in = inputs.shape[1:]
    block, filters = cotangent.shape[1], cotangent.shape[2]
    height = own_rows * filts
    scale = 1.0 / math.sqrt(inputs.shape[0] * height * width)

    part = filters // chans
    line_rows = own_rows * PAIR

    def all_rows(same):
        cross = core_swap(same, chans)
        padded = jnp.zeros((height + 2, filters, width), BF16)
        for step in range(chans // 2):
            at_far = lax.rem(far - step + chans // 2, chans // 2) * 2
            padded = lax.dynamic_update_slice(padded, same[step], (1 + (at_far + core) * block, 0, 0))
            padded = lax.dynamic_update_slice(padded, cross[step], (1 + (at_far + 1 - core) * block, 0, 0))
        return padded

    def line_pieces(padded):
        own_part = lax.dynamic_slice_in_dim(padded, chan * part, part, axis=1)
        return jnp.stack([own_part[z * line_rows : (z + 1) * line_rows + 2] for z in range(depth)])

    def exchange(pieces):
        return lax.all_to_all(pieces, "filt", 0, 0, axis_index_groups=lines(depth), tiled=True)

    halves = PAIR if chans_in % (PAIR * 128) == 0 else 1
    kernels = lax.all_gather(weights, "filt", axis=0, axis_index_groups=lines(depth))
    kernels = kernels.reshape((depth, 9) + weights.shape[2:])

    mine, theirs = [inputs[0]], [pair_swap(inputs[0], depth)]
    same = fars_gather(cotangent[0], chans)
    along = line_step({0: inputs[0]}, 1, depth)
    padded = all_rows(after(same, along[-1], along[1], *theirs))
    pieces = line_pieces(padded)
    fresh = theirs + [pieces]
    stages = max(2, depth - 1)
    for stage in range(2, stages + 1):
        ways = list(along)
        ready = lax.optimization_barrier([along[way] for way in ways] + fresh)
        along = dict(zip(ways, ready))
        if stage == 2:
            pieces = exchange(ready[-1])
        fresh = []
        if stage < stages:
            along = line_step(along, stage, depth)
        while len(theirs) < min(depth, stage + 1):
            mine.append(arrival(along, depth, line, len(theirs) - 1))
            theirs.append(pair_swap(mine[-1], depth))
            fresh.append(theirs[-1])
    same = fars_gather(pieces, chans)
    sources = turned(same, core_swap(same, chans))

    if part % 16:
        order = [(far - c // 2 + chans // 2) % (chans // 2) * 2 + (core + c) % 2 for c in range(chans)]
        split = kernels.reshape((depth, 9, chans, part, chans_in))
        kernels = jnp.take(split, jnp.stack(order), axis=2).reshape(kernels.shape)

    outputs, input_grad, at_next = None, [], after(at, kernels)

    def next_half(at_next):
        kept, sent = input_partial(chans, at_next, sources, kernels, len(input_grad), halves)
        input_grad.append((kept + pair_swap(sent, depth)).astype(BF16))
        return after(at, sent)

    for which in [*range(1, chans // 2), 0]:
        keep, send = forward_partial(depth, chans, which, at_next, weights, mine, theirs)
        at_next = after(at, send)
        moving = keep + core_swap(send, chans)
        if which:
            if not input_grad:
                at_next = next_half(at_next)
            at_next = after(at_next, moving)
            moving = lax.ppermute(moving, "chan", [(c, (c + 2 * which) % chans) for c in range(chans)])
        outputs = moving if outputs is None else outputs + moving
    outputs = outputs.astype(BF16)[None]
    while len(input_grad) < halves:
        at_next = next_half(at_next)
    input_grad = jnp.concatenate(input_grad, axis=2)[None]

    weight_grad = weight_gradient(depth, at_next, scale, padded, mine, theirs)
    weight_grad = weight_grad.reshape((3, 3, filters, chans_in))
    return (outputs, input_grad, weight_grad)


def solution(mesh):
    return jax.shard_map(
        body,
        mesh=mesh,
        in_specs=(
            P(None, "filt", None, "chan"),
            P(None, None, "filt", "chan"),
            P(None, "chan", "filt", None),
        ),
        out_specs=(
            P(None, "chan", "filt", None),
            P(None, "filt", None, "chan"),
            P(None, None, "filt", "chan"),
        ),
        check_vma=False,
    )
```

```python
import functools
import math

import jax
import jax.numpy as jnp
from jax import lax
from jax.experimental import pallas as pl
from jax.experimental.pallas import tpu as pltpu
from jax.sharding import PartitionSpec as P

F32 = jnp.float32
BF16 = jnp.bfloat16
NT = (((1,), (1,)), ((), ()))
HBM = pl.BlockSpec(memory_space=pltpu.HBM)
VMEM = pl.BlockSpec(memory_space=pltpu.VMEM)
SMEM = pl.BlockSpec(memory_space=pltpu.SMEM)
PAIR = 2


def params(mib):
    return pltpu.CompilerParams(vmem_limit_bytes=mib << 20)


def cost(flops, moved):
    return pl.CostEstimate(flops=int(flops), bytes_accessed=int(moved), transcendentals=0)


def lane_shift(value, by):
    size = value.shape[1]
    lane = lax.broadcasted_iota(jnp.int32, value.shape, 1)
    keep = lane >= by if by > 0 else lane < size + by
    return jnp.where(keep, pltpu.roll(value, by % size, 1), 0.0)


def after(value, *others):
    return lax.optimization_barrier((value,) + others)[0]


def arrivals(depth, line):
    ways = sorted((way for way in range(-line, depth - line) if way), key=abs)
    if abs(ways[-1]) == depth - 1:
        ways.insert(1, ways.pop())
    return ways


def arrival(along, depth, line, place):
    picked = None
    for z in range(depth):
        value = along[arrivals(depth, z)[place]]
        picked = value if picked is None or value is picked else jnp.where(line == z, value, picked)
    return picked


def load_rows(at, parts, rows, sems, first, last):
    height = parts[0][0].shape[0]

    def place(spot):
        return rows.at[pl.ds(1 + spot * height, height)]

    for half in range(PAIR):
        of_side = lax.rem(at[1] + half, PAIR)
        for index, part in enumerate(parts[half]):
            spot = at[4 + index] * PAIR + of_side

            @pl.when(jnp.logical_and(spot >= first, spot <= last))
            def _():
                pltpu.make_async_copy(part, place(spot), sems.at[spot]).start()

    rows[0] = jnp.zeros(rows.shape[1:], rows.dtype)
    rows[rows.shape[0] - 1] = jnp.zeros(rows.shape[1:], rows.dtype)
    return lambda spot: pltpu.make_async_copy(parts[0][0], place(spot), sems.at[spot]).wait()


def forward_kernel(depth, chans, which, at, weights, *refs):
    count = (len(refs) - 8) // 2
    parts = (refs[:count], refs[count : 2 * count])
    keep, send, rows, taps, made, sems, tap_sems, out_sems = refs[2 * count :]
    filters, chans_in = weights.shape[2], weights.shape[3]
    width = rows.shape[1]
    block = keep.shape[0]
    height = parts[0][0].shape[0]
    far, core = at[2], at[3]
    top = lax.rem(far + which, chans // 2) * 2 * block
    first, spots = top // height, max(1, 2 * block // height)
    wait = load_rows(at, parts, rows, sems, first - 1, first + spots)
    fetches = [
        pltpu.make_async_copy(
            weights.at[tap_row, tap_col],
            taps.at[pl.ds(tap_col * filters, filters), pl.ds(tap_row * chans_in, chans_in)],
            tap_sems.at[tap_row, tap_col],
        )
        for tap_row in range(3)
        for tap_col in range(3)
    ]
    for fetch in fetches:
        fetch.start()
    for fetch in fetches:
        fetch.wait()
    for spot in range(-1, spots + 1):

        @pl.when(jnp.logical_and(first + spot >= 0, first + spot < depth * PAIR))
        def _():
            wait(first + spot)

    group = min(4, block)

    def result(step, place):
        chosen = pl.ds(step * group, group)
        return pltpu.make_async_copy(made.at[place, chosen], (send, keep)[place].at[chosen], out_sems.at[place, step])

    @pl.loop(0, block // group)
    def _(step):
        for place, of_core in enumerate((1 - core, core)):
            start = top + of_core * block + step * group
            window = jnp.concatenate(
                [rows[pl.ds(start + i, group)].reshape(group * width, chans_in) for i in range(3)], axis=1
            )
            product = lax.dot_general(taps[...], window, NT, preferred_element_type=F32)
            for row in range(group):
                part = [
                    product[j * filters : (j + 1) * filters, row * width : (row + 1) * width] for j in range(3)
                ]
                made[place, step * group + row] = part[1] + lane_shift(part[0], 1) + lane_shift(part[2], -1)
            result(step, place).start()

    for step in range(block // group):
        for place in range(2):
            result(step, place).wait()


def forward_partial(depth, chans, which, at, weights, own, other):
    height, width, chans_in = own[0].shape
    filters = weights.shape[2]
    rows = height * depth * PAIR
    half = jax.ShapeDtypeStruct((rows // chans, filters, width), F32)
    return pl.pallas_call(
        functools.partial(forward_kernel, depth, chans, which),
        out_shape=(half, half),
        in_specs=[SMEM, HBM] + [HBM] * (len(own) + len(other)),
        out_specs=(HBM, HBM),
        scratch_shapes=[
            pltpu.VMEM((rows + 2, width, chans_in), BF16),
            pltpu.VMEM((3 * filters, 3 * chans_in), BF16),
            pltpu.VMEM((2, rows // chans, filters, width), F32),
            pltpu.SemaphoreType.DMA((depth * PAIR,)),
            pltpu.SemaphoreType.DMA((3, 3)),
            pltpu.SemaphoreType.DMA((2, rows // chans // min(4, rows // chans))),
        ],
        compiler_params=params(58),
        cost_estimate=cost(
            36 * rows // chans * width * chans_in * filters, 8 * rows // chans * width * (filters + chans_in)
        ),
        name="forward",
    )(at, weights, *own, *other)


def weight_kernel(depth, scale, at, cot, *refs):
    count = (len(refs) - 7) // 2
    parts = (refs[:count], refs[count : 2 * count])
    out, rows, cots, moved, total, sems, cot_sems = refs[2 * count :]
    wait = load_rows(at, parts, rows, sems, 0, depth * PAIR - 1)
    filters, width = cot.shape[1], cot.shape[2]
    chans_in = rows.shape[2]
    height = parts[0][0].shape[0]
    steps, chunk = cots.shape[0], cots.shape[1]

    def fetch(step):
        return pltpu.make_async_copy(cot.at[pl.ds(1 + step * chunk, chunk)], cots.at[step], cot_sems.at[step])

    for step in range(steps):
        fetch(step).start()
    total[...] = jnp.zeros(total.shape, F32)
    wait(0)

    @pl.loop(0, steps)
    def _(step):
        first = step * chunk
        fetch(step).wait()
        for spot in range(max(1, chunk // height)):
            after_it = first // height + spot + 1

            @pl.when(after_it < depth * PAIR)
            def _():
                wait(after_it)

        for row in range(chunk):
            value = cots[step, row]
            wide = value.astype(F32)
            lanes = pl.ds(row * width, width)
            moved[0:filters, lanes] = lane_shift(wide, -1).astype(BF16)
            moved[filters : 2 * filters, lanes] = value
            moved[2 * filters :, lanes] = lane_shift(wide, 1).astype(BF16)
        for tap_row in range(3):
            window = rows[pl.ds(first + tap_row, chunk)].reshape(chunk * width, chans_in)
            total[tap_row] += jnp.dot(moved[...], window, preferred_element_type=F32)

    stores = []
    for tap_row in range(3):
        total[tap_row] = total[tap_row] * scale
        for tap_col in range(3):
            chosen = (tap_row, pl.ds(tap_col * filters, filters))
            stores.append(pltpu.make_async_copy(total.at[chosen], out.at[chosen], cot_sems.at[steps + 3 * tap_row + tap_col]))
            stores[-1].start()
    for store in stores:
        store.wait()


def weight_gradient(depth, at, scale, cot, own, other):
    height, width, chans_in = own[0].shape
    rows, filters = cot.shape[0] - 2, cot.shape[1]
    chunk = max(height, min(8, rows))
    return pl.pallas_call(
        functools.partial(weight_kernel, depth, scale),
        out_shape=jax.ShapeDtypeStruct((3, 3 * filters, chans_in), F32),
        in_specs=[SMEM, HBM] + [HBM] * (len(own) + len(other)),
        out_specs=HBM,
        scratch_shapes=[
            pltpu.VMEM((rows + 2, width, chans_in), BF16),
            pltpu.VMEM((rows // chunk, chunk, filters, width), BF16),
            pltpu.VMEM((3 * filters, chunk * width), BF16),
            pltpu.VMEM((3, 3 * filters, chans_in), F32),
            pltpu.SemaphoreType.DMA((depth * PAIR,)),
            pltpu.SemaphoreType.DMA((rows // chunk + 9,)),
        ],
        compiler_params=params(58),
        cost_estimate=cost(18 * rows * width * chans_in * filters, 2 * rows * width * (filters + chans_in)),
        name="weight_gradient",
    )(at, cot, *own, *other)


def turn_kernel(same, cross, out):
    fars, _, rows = same.shape[:3]
    unroll = max(n for n in (1, 2, 3, 6) if rows % n == 0)

    @pl.loop(0, rows // unroll)
    def _(step):
        for n in range(unroll):
            row = step * unroll + n
            out[0, row] = jnp.concatenate([part[far, 0, row] for far in range(fars) for part in (same, cross)], axis=0).T


def turned(same, cross):
    fars, depth, rows, part, width = same.shape
    filters = 2 * fars * part
    spec = pl.BlockSpec((fars, 1, rows, part, width), lambda d: (0, d, 0, 0, 0))
    return pl.pallas_call(
        turn_kernel,
        grid=(depth,),
        out_shape=jax.ShapeDtypeStruct((depth, rows, width, filters), BF16),
        in_specs=[spec, spec],
        out_specs=pl.BlockSpec((1, rows, width, filters), lambda d: (d, 0, 0, 0)),
        compiler_params=params(58),
        cost_estimate=cost(0, 4 * depth * rows * width * filters),
        name="turned",
    )(same, cross)


def input_kernel(chans, ways, at, cot, *refs):
    line, side, far, core = at[0], at[1], at[2], at[3]
    kernels = refs[:-8]
    keep, send, source, taps, stacked, made, sems, out_sems = refs[-8:]
    depth, rows, width, filters = source.shape
    rows = rows - 2
    chans_in = taps.shape[3]
    for shard, reach in zip(kernels, ways):
        for way in reach:

            @pl.when(jnp.logical_and(line + way >= 0, line + way < depth))
            def _():
                pltpu.make_async_copy(shard, taps.at[line + way], sems.at[line + way, 0]).start()

    copies = []
    for n in range(depth):
        copies.append(
            (
                pltpu.make_async_copy(kernels[0] if ways else kernels[0].at[n], taps.at[n], sems.at[n, 0]),
                [
                    pltpu.make_async_copy(
                        cot.at[n, pl.ds(first, (rows + 2) // 2)],
                        source.at[n, pl.ds(first, (rows + 2) // 2)],
                        sems.at[n, 1 + (first > 0)],
                    )
                    for first in (0, (rows + 2) // 2)
                ],
            )
        )
        if not ways:
            copies[n][0].start()
    for n in range(depth):
        for copy in copies[n][1]:
            copy.start()
    part = filters // chans
    places = chans if part % 16 == 0 else 1
    size = filters // places
    for n in range(depth):
        copies[n][0].wait()
        for place in range(places):
            chan = lax.rem(far - place // 2 + chans // 2, chans // 2) * 2 + lax.rem(core + place, 2)
            of_chan = pl.ds(0 if places == 1 else pl.multiple_of(chan * size, size), size)
            for i in range(3):
                for j in range(3):
                    stacked[
                        pl.ds((n * 3 + i) * filters + place * size, size), pl.ds(j * chans_in, chans_in)
                    ] = taps[n, 3 * i + j, of_chan]
    for n in range(depth):
        for copy in copies[n][1]:
            copy.wait()
    half = rows // PAIR
    chunk = min(4, half)
    lanes = lax.broadcasted_iota(jnp.int32, (width, chans_in), 0)

    def result(place, step):
        chosen = pl.ds(step * chunk, chunk)
        return pltpu.make_async_copy(made.at[place, chosen], (send, keep)[place].at[chosen], out_sems.at[place, step])

    for place, of_side in enumerate((1 - side, side)):
        for step in range(half // chunk):
            first = of_side * half + step * chunk
            window = [
                source[n, pl.ds(first + 2 - i, chunk)].reshape(chunk * width, filters)
                for n in range(depth)
                for i in range(3)
            ]
            if filters % 128 == 0:
                product = jnp.dot(jnp.concatenate(window, axis=1), stacked[...], preferred_element_type=F32)
            else:
                product = sum(
                    jnp.dot(value, stacked[n * filters : (n + 1) * filters], preferred_element_type=F32)
                    for n, value in enumerate(window)
                )
            for row in range(chunk):
                here = [
                    product[row * width : (row + 1) * width, j * chans_in : (j + 1) * chans_in] for j in range(3)
                ]
                before_it = jnp.where(lanes < width - 1, pltpu.roll(here[0], width - 1, 0), 0.0)
                behind_it = jnp.where(lanes >= 1, pltpu.roll(here[2], 1, 0), 0.0)
                made[place, step * chunk + row] = here[1] + before_it + behind_it
            result(place, step).start()

    for place in range(2):
        for step in range(half // chunk):
            result(place, step).wait()


def input_partial(chans, at, cot, kernels, ways=()):
    depth, rows, width, filters = cot.shape
    rows = rows - 2
    chans_in = kernels[0].shape[-1]
    half = jax.ShapeDtypeStruct((rows // PAIR, width, chans_in), F32)
    return pl.pallas_call(
        functools.partial(input_kernel, chans, ways),
        out_shape=(half, half),
        in_specs=[SMEM, HBM] + [HBM] * len(kernels),
        out_specs=(HBM, HBM),
        scratch_shapes=[
            pltpu.VMEM(cot.shape, BF16),
            pltpu.VMEM((depth, 9, filters, chans_in), BF16),
            pltpu.VMEM((depth * 3 * filters, 3 * chans_in), BF16),
            pltpu.VMEM((PAIR, rows // PAIR, width, chans_in), F32),
            pltpu.SemaphoreType.DMA((depth, 3)),
            pltpu.SemaphoreType.DMA((PAIR, rows // PAIR // min(4, rows // PAIR))),
        ],
        compiler_params=params(58),
        cost_estimate=cost(
            18 * rows * width * chans_in * filters * depth, 2 * depth * filters * ((rows + 2) * width + 9 * chans_in)
        ),
        name="input_gradient",
    )(at, cot, *kernels)


def fars_gather(value, chans):
    got = [value]
    for step in range(1, chans // 2):
        got.append(lax.ppermute(value, "chan", [(c, (c + 2 * step) % chans) for c in range(chans)]))
    return jnp.stack(got)


def lines(depth):
    return [[z * PAIR + y for z in range(depth)] for y in range(PAIR)]


def line_step(along, step, depth):
    up = [(z * PAIR + y, (z + 1) * PAIR + y) for z in range(step - 1, depth - 1) for y in range(PAIR)]
    down = [(z * PAIR + y, (z - 1) * PAIR + y) for z in range(1, depth - step + 1) for y in range(PAIR)]
    along = dict(along)
    along[-step] = lax.ppermute(along[1 - step], "filt", up)
    along[step] = lax.ppermute(along[step - 1], "filt", down)
    if step == 1 and depth > 2:
        ends = (0, depth - 1)
        across = [(z * PAIR + y, (depth - 1 - z) * PAIR + y) for z in ends for y in range(PAIR)]
        along[depth - 1] = along[1 - depth] = lax.ppermute(along[0], "filt", across)
    return along


def core_swap(value, chans):
    return lax.ppermute(value, "chan", [(c, c ^ 1) for c in range(chans)])


def pair_swap(value, depth):
    pairs = [(z * PAIR + y, z * PAIR + 1 - y) for z in range(depth) for y in range(PAIR)]
    return lax.ppermute(value, "filt", pairs)


def body(inputs, weights, cotangent):
    chans, filts = lax.axis_size("chan"), lax.axis_size("filt")
    depth = filts // PAIR
    chan, filt = lax.axis_index("chan"), lax.axis_index("filt")
    line, side = filt // PAIR, filt % PAIR
    far, core = chan // 2, chan % 2
    spots = jnp.asarray([[z] + [z + way for way in arrivals(depth, z)] for z in range(depth)], jnp.int32)
    at = jnp.concatenate([jnp.stack([line, side, far, core]).astype(jnp.int32), spots[line]])
    own_rows, width, chans_in = inputs.shape[1:]
    block, filters = cotangent.shape[1], cotangent.shape[2]
    height = own_rows * filts
    scale = 1.0 / math.sqrt(inputs.shape[0] * height * width)

    part = filters // chans
    line_rows = own_rows * PAIR

    def all_rows(same):
        cross = core_swap(same, chans)
        padded = jnp.zeros((height + 2, filters, width), BF16)
        for step in range(chans // 2):
            at_far = lax.rem(far - step + chans // 2, chans // 2) * 2
            padded = lax.dynamic_update_slice(padded, same[step], (1 + (at_far + core) * block, 0, 0))
            padded = lax.dynamic_update_slice(padded, cross[step], (1 + (at_far + 1 - core) * block, 0, 0))
        return padded

    def line_pieces(padded):
        own_part = lax.dynamic_slice_in_dim(padded, chan * part, part, axis=1)
        return jnp.stack([own_part[z * line_rows : (z + 1) * line_rows + 2] for z in range(depth)])

    def exchange(pieces):
        return lax.all_to_all(pieces, "filt", 0, 0, axis_index_groups=lines(depth), tiled=True)

    halves = jnp.split(weights, PAIR if chans_in % (PAIR * 128) == 0 else 1, axis=3)
    halves = [half.reshape((9,) + half.shape[2:]) for half in halves]
    if part % 16:
        order = jnp.stack([(far - c // 2 + chans // 2) % (chans // 2) * 2 + (core + c) % 2 for c in range(chans)])
        halves = [jnp.take(half.reshape((9, chans, part, -1)), order, axis=1).reshape(half.shape) for half in halves]
    kernels = lax.all_gather(halves[0], "filt", axis=0, axis_index_groups=lines(depth))
    later = {}

    mine, theirs = [inputs[0]], [pair_swap(inputs[0], depth)]
    same = fars_gather(cotangent[0], chans)
    along = line_step({0: inputs[0]}, 1, depth)
    fresh = theirs + [same, halves[-1]]
    stages = max(2, depth - 1)
    for stage in range(2, stages + 1):
        ways = list(along)
        ready = lax.optimization_barrier([along[way] for way in ways] + fresh)
        along = dict(zip(ways, ready))
        if stage == 2:
            padded = all_rows(ready[-2])
            pieces = line_pieces(padded)
        elif stage == 3:
            pieces = exchange(ready[-2])
        if stage == stages and len(halves) > 1:
            later = line_step({0: ready[-1]}, 1, depth)
        fresh = []
        if stage < stages:
            along = line_step(along, stage, depth)
        while len(theirs) < min(depth, stage + 1):
            mine.append(arrival(along, depth, line, len(theirs) - 1))
            theirs.append(pair_swap(mine[-1], depth))
            fresh.append(theirs[-1])
        fresh += [pieces, halves[-1]]
    if stages < 3:
        pieces = exchange(pieces)
    same = fars_gather(pieces, chans)
    sources = turned(same, core_swap(same, chans))

    outputs, input_grad, at_next = None, [], after(at, kernels, pieces, *later.values())
    for step in range(2, depth - 1):
        later = line_step(later, step, depth) if later else later
    shards = {id(value): value for value in later.values()}
    ways = [tuple(way for way in later if later[way] is value) for value in shards.values()]

    for which in [*range(1, chans // 2), 0]:
        keep, send = forward_partial(depth, chans, which, at_next, weights, mine, theirs)
        at_next = after(at, send)
        moving = keep + core_swap(send, chans)
        if which:
            if not input_grad:
                kept, sent = input_partial(chans, at_next, sources, [kernels])
                input_grad.append((kept + pair_swap(sent, depth)).astype(BF16))
                at_next = after(at, sent)
            at_next = after(at_next, moving)
            moving = lax.ppermute(moving, "chan", [(c, (c + 2 * which) % chans) for c in range(chans)])
            if later and len(input_grad) < 2:
                kept, sent = input_partial(chans, at_next, sources, list(shards.values()), tuple(ways))
                input_grad.append((kept + pair_swap(sent, depth)).astype(BF16))
                at_next = after(at, sent)
        outputs = moving if outputs is None else outputs + moving
    outputs = outputs.astype(BF16)[None]
    input_grad = jnp.concatenate(input_grad, axis=2)[None]

    weight_grad = weight_gradient(depth, at_next, scale, padded, mine, theirs)
    weight_grad = weight_grad.reshape((3, 3, filters, chans_in))
    return (outputs, input_grad, weight_grad)


def solution(mesh):
    return jax.shard_map(
        body,
        mesh=mesh,
        in_specs=(
            P(None, "filt", None, "chan"),
            P(None, None, "filt", "chan"),
            P(None, "chan", "filt", None),
        ),
        out_specs=(
            P(None, "chan", "filt", None),
            P(None, "filt", None, "chan"),
            P(None, None, "filt", "chan"),
        ),
        check_vma=False,
    )
```

```python
import functools
import math

import jax
import jax.numpy as jnp
from jax import lax
from jax.experimental import pallas as pl
from jax.experimental.pallas import tpu as pltpu
from jax.sharding import PartitionSpec as P

F32 = jnp.float32
BF16 = jnp.bfloat16
NT = (((1,), (1,)), ((), ()))
HBM = pl.BlockSpec(memory_space=pltpu.HBM)
VMEM = pl.BlockSpec(memory_space=pltpu.VMEM)
SMEM = pl.BlockSpec(memory_space=pltpu.SMEM)
PAIR = 2


def params(mib):
    return pltpu.CompilerParams(vmem_limit_bytes=mib << 20)


def cost(flops, moved):
    return pl.CostEstimate(flops=int(flops), bytes_accessed=int(moved), transcendentals=0)


def lane_shift(value, by):
    size = value.shape[1]
    lane = lax.broadcasted_iota(jnp.int32, value.shape, 1)
    keep = lane >= by if by > 0 else lane < size + by
    return jnp.where(keep, pltpu.roll(value, by % size, 1), 0.0)


def after(value, *others):
    return lax.optimization_barrier((value,) + others)[0]


def arrivals(depth, line):
    ways = sorted((way for way in range(-line, depth - line) if way), key=abs)
    if abs(ways[-1]) == depth - 1:
        ways.insert(1, ways.pop())
    return ways


def arrival(along, depth, line, place):
    picked = None
    for z in range(depth):
        value = along[arrivals(depth, z)[place]]
        picked = value if picked is None or value is picked else jnp.where(line == z, value, picked)
    return picked


def load_rows(at, parts, rows, sems, first, last):
    height = parts[0][0].shape[0]

    def place(spot):
        return rows.at[pl.ds(1 + spot * height, height)]

    for half in range(PAIR):
        of_side = lax.rem(at[1] + half, PAIR)
        for index, part in enumerate(parts[half]):
            spot = at[4 + index] * PAIR + of_side

            @pl.when(jnp.logical_and(spot >= first, spot <= last))
            def _():
                pltpu.make_async_copy(part, place(spot), sems.at[spot]).start()

    rows[0] = jnp.zeros(rows.shape[1:], rows.dtype)
    rows[rows.shape[0] - 1] = jnp.zeros(rows.shape[1:], rows.dtype)
    return lambda spot: pltpu.make_async_copy(parts[0][0], place(spot), sems.at[spot]).wait()


def forward_kernel(depth, chans, which, at, weights, *refs):
    count = (len(refs) - 8) // 2
    parts = (refs[:count], refs[count : 2 * count])
    keep, send, rows, taps, made, sems, tap_sems, out_sems = refs[2 * count :]
    filters, chans_in = weights.shape[2], weights.shape[3]
    width = rows.shape[1]
    block = keep.shape[0]
    height = parts[0][0].shape[0]
    far, core = at[2], at[3]
    top = lax.rem(far + which, chans // 2) * 2 * block
    first, spots = top // height, max(1, 2 * block // height)
    wait = load_rows(at, parts, rows, sems, first - 1, first + spots)
    fetches = [
        pltpu.make_async_copy(
            weights.at[tap_row, tap_col],
            taps.at[pl.ds(tap_col * filters, filters), pl.ds(tap_row * chans_in, chans_in)],
            tap_sems.at[tap_row, tap_col],
        )
        for tap_row in range(3)
        for tap_col in range(3)
    ]
    for fetch in fetches:
        fetch.start()
    for fetch in fetches:
        fetch.wait()
    for spot in range(-1, spots + 1):

        @pl.when(jnp.logical_and(first + spot >= 0, first + spot < depth * PAIR))
        def _():
            wait(first + spot)

    group = min(4, block)

    def result(step, place):
        chosen = pl.ds(step * group, group)
        return pltpu.make_async_copy(made.at[place, chosen], (send, keep)[place].at[chosen], out_sems.at[place, step])

    @pl.loop(0, block // group)
    def _(step):
        for place, of_core in enumerate((1 - core, core)):
            start = top + of_core * block + step * group
            window = jnp.concatenate(
                [rows[pl.ds(start + i, group)].reshape(group * width, chans_in) for i in range(3)], axis=1
            )
            product = lax.dot_general(taps[...], window, NT, preferred_element_type=F32)
            for row in range(group):
                part = [
                    product[j * filters : (j + 1) * filters, row * width : (row + 1) * width] for j in range(3)
                ]
                made[place, step * group + row] = part[1] + lane_shift(part[0], 1) + lane_shift(part[2], -1)
            result(step, place).start()

    for step in range(block // group):
        for place in range(2):
            result(step, place).wait()


def forward_partial(depth, chans, which, at, weights, own, other):
    height, width, chans_in = own[0].shape
    filters = weights.shape[2]
    rows = height * depth * PAIR
    half = jax.ShapeDtypeStruct((rows // chans, filters, width), F32)
    return pl.pallas_call(
        functools.partial(forward_kernel, depth, chans, which),
        out_shape=(half, half),
        in_specs=[SMEM, HBM] + [HBM] * (len(own) + len(other)),
        out_specs=(HBM, HBM),
        scratch_shapes=[
            pltpu.VMEM((rows + 2, width, chans_in), BF16),
            pltpu.VMEM((3 * filters, 3 * chans_in), BF16),
            pltpu.VMEM((2, rows // chans, filters, width), F32),
            pltpu.SemaphoreType.DMA((depth * PAIR,)),
            pltpu.SemaphoreType.DMA((3, 3)),
            pltpu.SemaphoreType.DMA((2, rows // chans // min(4, rows // chans))),
        ],
        compiler_params=params(58),
        cost_estimate=cost(
            36 * rows // chans * width * chans_in * filters, 8 * rows // chans * width * (filters + chans_in)
        ),
        name="forward",
    )(at, weights, *own, *other)


def weight_kernel(depth, scale, at, cot, *refs):
    count = (len(refs) - 7) // 2
    parts = (refs[:count], refs[count : 2 * count])
    out, rows, cots, moved, total, sems, cot_sems = refs[2 * count :]
    wait = load_rows(at, parts, rows, sems, 0, depth * PAIR - 1)
    filters, width = cot.shape[1], cot.shape[2]
    chans_in = rows.shape[2]
    height = parts[0][0].shape[0]
    steps, chunk = cots.shape[0], cots.shape[1]

    def fetch(step):
        return pltpu.make_async_copy(cot.at[pl.ds(1 + step * chunk, chunk)], cots.at[step], cot_sems.at[step])

    for step in range(steps):
        fetch(step).start()
    total[...] = jnp.zeros(total.shape, F32)
    wait(0)

    @pl.loop(0, steps)
    def _(step):
        first = step * chunk
        fetch(step).wait()
        for spot in range(max(1, chunk // height)):
            after_it = first // height + spot + 1

            @pl.when(after_it < depth * PAIR)
            def _():
                wait(after_it)

        for row in range(chunk):
            value = cots[step, row]
            wide = value.astype(F32)
            lanes = pl.ds(row * width, width)
            moved[0:filters, lanes] = lane_shift(wide, -1).astype(BF16)
            moved[filters : 2 * filters, lanes] = value
            moved[2 * filters :, lanes] = lane_shift(wide, 1).astype(BF16)
        for tap_row in range(3):
            window = rows[pl.ds(first + tap_row, chunk)].reshape(chunk * width, chans_in)
            total[tap_row] += jnp.dot(moved[...], window, preferred_element_type=F32)

    stores = []
    for tap_row in range(3):
        total[tap_row] = total[tap_row] * scale
        for tap_col in range(3):
            chosen = (tap_row, pl.ds(tap_col * filters, filters))
            stores.append(pltpu.make_async_copy(total.at[chosen], out.at[chosen], cot_sems.at[steps + 3 * tap_row + tap_col]))
            stores[-1].start()
    for store in stores:
        store.wait()


def weight_gradient(depth, at, scale, cot, own, other):
    height, width, chans_in = own[0].shape
    rows, filters = cot.shape[0] - 2, cot.shape[1]
    chunk = max(height, min(8, rows))
    return pl.pallas_call(
        functools.partial(weight_kernel, depth, scale),
        out_shape=jax.ShapeDtypeStruct((3, 3 * filters, chans_in), F32),
        in_specs=[SMEM, HBM] + [HBM] * (len(own) + len(other)),
        out_specs=HBM,
        scratch_shapes=[
            pltpu.VMEM((rows + 2, width, chans_in), BF16),
            pltpu.VMEM((rows // chunk, chunk, filters, width), BF16),
            pltpu.VMEM((3 * filters, chunk * width), BF16),
            pltpu.VMEM((3, 3 * filters, chans_in), F32),
            pltpu.SemaphoreType.DMA((depth * PAIR,)),
            pltpu.SemaphoreType.DMA((rows // chunk + 9,)),
        ],
        compiler_params=params(58),
        cost_estimate=cost(18 * rows * width * chans_in * filters, 2 * rows * width * (filters + chans_in)),
        name="weight_gradient",
    )(at, cot, *own, *other)


def turn_kernel(same, cross, out):
    fars, _, rows = same.shape[:3]
    unroll = max(n for n in (1, 2, 3, 6) if rows % n == 0)

    @pl.loop(0, rows // unroll)
    def _(step):
        for n in range(unroll):
            row = step * unroll + n
            out[0, row] = jnp.concatenate([part[far, 0, row] for far in range(fars) for part in (same, cross)], axis=0).T


def turned(same, cross):
    fars, depth, rows, part, width = same.shape
    filters = 2 * fars * part
    spec = pl.BlockSpec((fars, 1, rows, part, width), lambda d: (0, d, 0, 0, 0))
    return pl.pallas_call(
        turn_kernel,
        grid=(depth,),
        out_shape=jax.ShapeDtypeStruct((depth, rows, width, filters), BF16),
        in_specs=[spec, spec],
        out_specs=pl.BlockSpec((1, rows, width, filters), lambda d: (d, 0, 0, 0)),
        compiler_params=params(58),
        cost_estimate=cost(0, 4 * depth * rows * width * filters),
        name="turned",
    )(same, cross)


def input_kernel(chans, at, cot, kernels, keep, send, source, taps, stacked, made, sems, out_sems):
    side, far, core = at[1], at[2], at[3]
    depth, rows, width, filters = source.shape
    rows = rows - 2
    chans_in = taps.shape[3]
    copies = []
    for n in range(depth):
        copies.append(
            (
                pltpu.make_async_copy(kernels.at[n], taps.at[n], sems.at[n, 0]),
                [
                    pltpu.make_async_copy(
                        cot.at[n, pl.ds(first, (rows + 2) // 2)],
                        source.at[n, pl.ds(first, (rows + 2) // 2)],
                        sems.at[n, 1 + (first > 0)],
                    )
                    for first in (0, (rows + 2) // 2)
                ],
            )
        )
        copies[n][0].start()
    for n in range(depth):
        for copy in copies[n][1]:
            copy.start()
    part = filters // chans
    places = chans if part % 16 == 0 else 1
    size = filters // places
    for n in range(depth):
        copies[n][0].wait()
        for place in range(places):
            chan = lax.rem(far - place // 2 + chans // 2, chans // 2) * 2 + lax.rem(core + place, 2)
            of_chan = pl.ds(0 if places == 1 else pl.multiple_of(chan * size, size), size)
            for i in range(3):
                for j in range(3):
                    stacked[
                        pl.ds((n * 3 + i) * filters + place * size, size), pl.ds(j * chans_in, chans_in)
                    ] = taps[n, 3 * i + j, of_chan]
    for n in range(depth):
        for copy in copies[n][1]:
            copy.wait()
    half = rows // PAIR
    chunk = min(4, half)
    lanes = lax.broadcasted_iota(jnp.int32, (width, chans_in), 0)

    def result(place, step):
        chosen = pl.ds(step * chunk, chunk)
        return pltpu.make_async_copy(made.at[place, chosen], (send, keep)[place].at[chosen], out_sems.at[place, step])

    for place, of_side in enumerate((1 - side, side)):
        for step in range(half // chunk):
            first = of_side * half + step * chunk
            window = [
                source[n, pl.ds(first + 2 - i, chunk)].reshape(chunk * width, filters)
                for n in range(depth)
                for i in range(3)
            ]
            if filters % 128 == 0:
                product = jnp.dot(jnp.concatenate(window, axis=1), stacked[...], preferred_element_type=F32)
            else:
                product = sum(
                    jnp.dot(value, stacked[n * filters : (n + 1) * filters], preferred_element_type=F32)
                    for n, value in enumerate(window)
                )
            for row in range(chunk):
                here = [
                    product[row * width : (row + 1) * width, j * chans_in : (j + 1) * chans_in] for j in range(3)
                ]
                before_it = jnp.where(lanes < width - 1, pltpu.roll(here[0], width - 1, 0), 0.0)
                behind_it = jnp.where(lanes >= 1, pltpu.roll(here[2], 1, 0), 0.0)
                made[place, step * chunk + row] = here[1] + before_it + behind_it
            result(place, step).start()

    for place in range(2):
        for step in range(half // chunk):
            result(place, step).wait()


def input_partial(chans, at, cot, kernels):
    depth, rows, width, filters = cot.shape
    rows = rows - 2
    chans_in = kernels.shape[3]
    half = jax.ShapeDtypeStruct((rows // PAIR, width, chans_in), F32)
    return pl.pallas_call(
        functools.partial(input_kernel, chans),
        out_shape=(half, half),
        in_specs=[SMEM, HBM, HBM],
        out_specs=(HBM, HBM),
        scratch_shapes=[
            pltpu.VMEM(cot.shape, BF16),
            pltpu.VMEM(kernels.shape, BF16),
            pltpu.VMEM((depth * 3 * filters, 3 * chans_in), BF16),
            pltpu.VMEM((PAIR, rows // PAIR, width, chans_in), F32),
            pltpu.SemaphoreType.DMA((depth, 3)),
            pltpu.SemaphoreType.DMA((PAIR, rows // PAIR // min(4, rows // PAIR))),
        ],
        compiler_params=params(58),
        cost_estimate=cost(
            18 * rows * width * chans_in * filters * depth, 2 * depth * filters * ((rows + 2) * width + 9 * chans_in)
        ),
        name="input_gradient",
    )(at, cot, kernels)


def fars_gather(value, chans):
    got = [value]
    for step in range(1, chans // 2):
        got.append(lax.ppermute(value, "chan", [(c, (c + 2 * step) % chans) for c in range(chans)]))
    return jnp.stack(got)


def lines(depth):
    return [[z * PAIR + y for z in range(depth)] for y in range(PAIR)]


def line_step(along, step, depth):
    up = [(z * PAIR + y, (z + 1) * PAIR + y) for z in range(step - 1, depth - 1) for y in range(PAIR)]
    down = [(z * PAIR + y, (z - 1) * PAIR + y) for z in range(1, depth - step + 1) for y in range(PAIR)]
    along = dict(along)
    along[-step] = lax.ppermute(along[1 - step], "filt", up)
    along[step] = lax.ppermute(along[step - 1], "filt", down)
    if step == 1 and depth > 2:
        ends = (0, depth - 1)
        across = [(z * PAIR + y, (depth - 1 - z) * PAIR + y) for z in ends for y in range(PAIR)]
        along[depth - 1] = along[1 - depth] = lax.ppermute(along[0], "filt", across)
    return along


def core_swap(value, chans):
    return lax.ppermute(value, "chan", [(c, c ^ 1) for c in range(chans)])


def pair_swap(value, depth):
    pairs = [(z * PAIR + y, z * PAIR + 1 - y) for z in range(depth) for y in range(PAIR)]
    return lax.ppermute(value, "filt", pairs)


def body(inputs, weights, cotangent):
    chans, filts = lax.axis_size("chan"), lax.axis_size("filt")
    depth = filts // PAIR
    chan, filt = lax.axis_index("chan"), lax.axis_index("filt")
    line, side = filt // PAIR, filt % PAIR
    far, core = chan // 2, chan % 2
    spots = jnp.asarray([[z] + [z + way for way in arrivals(depth, z)] for z in range(depth)], jnp.int32)
    at = jnp.concatenate([jnp.stack([line, side, far, core]).astype(jnp.int32), spots[line]])
    own_rows, width, chans_in = inputs.shape[1:]
    block, filters = cotangent.shape[1], cotangent.shape[2]
    height = own_rows * filts
    scale = 1.0 / math.sqrt(inputs.shape[0] * height * width)

    part = filters // chans
    line_rows = own_rows * PAIR

    def all_rows(same):
        cross = core_swap(same, chans)
        padded = jnp.zeros((height + 2, filters, width), BF16)
        for step in range(chans // 2):
            at_far = lax.rem(far - step + chans // 2, chans // 2) * 2
            padded = lax.dynamic_update_slice(padded, same[step], (1 + (at_far + core) * block, 0, 0))
            padded = lax.dynamic_update_slice(padded, cross[step], (1 + (at_far + 1 - core) * block, 0, 0))
        return padded

    def line_pieces(padded):
        own_part = lax.dynamic_slice_in_dim(padded, chan * part, part, axis=1)
        return jnp.stack([own_part[z * line_rows : (z + 1) * line_rows + 2] for z in range(depth)])

    def exchange(pieces):
        return lax.all_to_all(pieces, "filt", 0, 0, axis_index_groups=lines(depth), tiled=True)

    halves = PAIR if chans_in % (PAIR * 128) == 0 else 1
    kernels = []
    for half in jnp.split(weights, halves, axis=3):
        half = half.reshape((9,) + half.shape[2:])
        kernels.append(lax.all_gather(half, "filt", axis=0, axis_index_groups=lines(depth)))

    mine, theirs = [inputs[0]], [pair_swap(inputs[0], depth)]
    same = fars_gather(cotangent[0], chans)
    along = line_step({0: inputs[0]}, 1, depth)
    fresh = theirs + [same]
    stages = max(2, depth - 1)
    for stage in range(2, stages + 1):
        ways = list(along)
        ready = lax.optimization_barrier([along[way] for way in ways] + fresh)
        along = dict(zip(ways, ready))
        if stage == 2:
            padded = all_rows(ready[-1])
            pieces = line_pieces(padded)
        elif stage == 3:
            pieces = exchange(ready[-1])
        fresh = []
        if stage < stages:
            along = line_step(along, stage, depth)
        while len(theirs) < min(depth, stage + 1):
            mine.append(arrival(along, depth, line, len(theirs) - 1))
            theirs.append(pair_swap(mine[-1], depth))
            fresh.append(theirs[-1])
        fresh.append(pieces)
    if stages < 3:
        pieces = exchange(pieces)
    whiches = [*range(1, chans // 2), 0]
    made = forward_partial(depth, chans, whiches[0], after(at, kernels[0]), weights, mine, theirs)
    same = fars_gather(pieces, chans)
    sources = turned(same, core_swap(after(same, made[1]), chans))

    if part % 16:
        order = [(far - c // 2 + chans // 2) % (chans // 2) * 2 + (core + c) % 2 for c in range(chans)]
        split = [half.reshape((depth, 9, chans, part, -1)) for half in kernels]
        kernels = [jnp.take(half, jnp.stack(order), axis=2).reshape(kernels[0].shape) for half in split]

    outputs, came, at_next = None, [], at
    for which in whiches:
        if made is None:
            made = forward_partial(depth, chans, which, at_next, weights, mine, theirs)
        (keep, send), made = made, None
        at_next = after(at, send)
        moving = keep + core_swap(send, chans)
        if which:
            at_next = after(at_next, moving)
            moving = lax.ppermute(moving, "chan", [(c, (c + 2 * which) % chans) for c in range(chans)])
            came.append(moving)
        outputs = moving if outputs is None else outputs + moving
    outputs = outputs.astype(BF16)[None]

    input_grad = []
    for half in kernels:
        kept, sent = input_partial(chans, at_next, sources, half)
        at_next = after(at_next, sent, *came)
        input_grad.append((kept + pair_swap(sent, depth)).astype(BF16))
    at_next = after(at_next, *input_grad[:-1])
    input_grad = jnp.concatenate(input_grad, axis=2)[None]
    weight_grad = weight_gradient(depth, at_next, scale, padded, mine, theirs)
    weight_grad = weight_grad.reshape((3, 3, filters, chans_in))
    return (outputs, input_grad, weight_grad)


def solution(mesh):
    return jax.shard_map(
        body,
        mesh=mesh,
        in_specs=(
            P(None, "filt", None, "chan"),
            P(None, None, "filt", "chan"),
            P(None, "chan", "filt", None),
        ),
        out_specs=(
            P(None, "chan", "filt", None),
            P(None, "filt", None, "chan"),
            P(None, None, "filt", "chan"),
        ),
        check_vma=False,
    )
```

```python
import functools
import math

import jax
import jax.numpy as jnp
from jax import lax
from jax.experimental import pallas as pl
from jax.experimental.pallas import tpu as pltpu
from jax.sharding import PartitionSpec as P

F32 = jnp.float32
BF16 = jnp.bfloat16
NT = (((1,), (1,)), ((), ()))
HBM = pl.BlockSpec(memory_space=pltpu.HBM)
VMEM = pl.BlockSpec(memory_space=pltpu.VMEM)
SMEM = pl.BlockSpec(memory_space=pltpu.SMEM)
PAIR = 2


def params(mib):
    return pltpu.CompilerParams(vmem_limit_bytes=mib << 20)


def cost(flops, moved):
    return pl.CostEstimate(flops=int(flops), bytes_accessed=int(moved), transcendentals=0)


def lane_shift(value, by):
    size = value.shape[1]
    lane = lax.broadcasted_iota(jnp.int32, value.shape, 1)
    keep = lane >= by if by > 0 else lane < size + by
    return jnp.where(keep, pltpu.roll(value, by % size, 1), 0.0)


def after(value, *others):
    return lax.optimization_barrier((value,) + others)[0]


def arrivals(depth, line):
    ways = sorted((way for way in range(-line, depth - line) if way), key=abs)
    if abs(ways[-1]) == depth - 1:
        ways.insert(1, ways.pop())
    return ways


def arrival(along, depth, line, place):
    picked = None
    for z in range(depth):
        value = along[arrivals(depth, z)[place]]
        picked = value if picked is None or value is picked else jnp.where(line == z, value, picked)
    return picked


def load_rows(at, parts, rows, sems, first, last):
    height = parts[0][0].shape[0]

    def place(spot):
        return rows.at[pl.ds(1 + spot * height, height)]

    for half in range(PAIR):
        of_side = lax.rem(at[1] + half, PAIR)
        for index, part in enumerate(parts[half]):
            spot = at[4 + index] * PAIR + of_side

            @pl.when(jnp.logical_and(spot >= first, spot <= last))
            def _():
                pltpu.make_async_copy(part, place(spot), sems.at[spot]).start()

    rows[0] = jnp.zeros(rows.shape[1:], rows.dtype)
    rows[rows.shape[0] - 1] = jnp.zeros(rows.shape[1:], rows.dtype)
    return lambda spot: pltpu.make_async_copy(parts[0][0], place(spot), sems.at[spot]).wait()


def forward_kernel(depth, chans, which, at, weights, *refs):
    count = (len(refs) - 8) // 2
    parts = (refs[:count], refs[count : 2 * count])
    keep, send, rows, taps, made, sems, tap_sems, out_sems = refs[2 * count :]
    filters, chans_in = weights.shape[2], weights.shape[3]
    width = rows.shape[1]
    block = keep.shape[0]
    height = parts[0][0].shape[0]
    far, core = at[2], at[3]
    top = lax.rem(far + which, chans // 2) * 2 * block
    first, spots = top // height, max(1, 2 * block // height)
    wait = load_rows(at, parts, rows, sems, first - 1, first + spots)
    fetches = [
        pltpu.make_async_copy(
            weights.at[tap_row, tap_col],
            taps.at[pl.ds(tap_col * filters, filters), pl.ds(tap_row * chans_in, chans_in)],
            tap_sems.at[tap_row, tap_col],
        )
        for tap_row in range(3)
        for tap_col in range(3)
    ]
    for fetch in fetches:
        fetch.start()
    for fetch in fetches:
        fetch.wait()
    for spot in range(-1, spots + 1):

        @pl.when(jnp.logical_and(first + spot >= 0, first + spot < depth * PAIR))
        def _():
            wait(first + spot)

    group = min(4, block)

    def result(step, place):
        chosen = pl.ds(step * group, group)
        return pltpu.make_async_copy(made.at[place, chosen], (send, keep)[place].at[chosen], out_sems.at[place, step])

    @pl.loop(0, block // group)
    def _(step):
        for place, of_core in enumerate((1 - core, core)):
            start = top + of_core * block + step * group
            window = jnp.concatenate(
                [rows[pl.ds(start + i, group)].reshape(group * width, chans_in) for i in range(3)], axis=1
            )
            product = lax.dot_general(taps[...], window, NT, preferred_element_type=F32)
            for row in range(group):
                part = [
                    product[j * filters : (j + 1) * filters, row * width : (row + 1) * width] for j in range(3)
                ]
                made[place, step * group + row] = part[1] + lane_shift(part[0], 1) + lane_shift(part[2], -1)
            result(step, place).start()

    for step in range(block // group):
        for place in range(2):
            result(step, place).wait()


def forward_partial(depth, chans, which, at, weights, own, other):
    height, width, chans_in = own[0].shape
    filters = weights.shape[2]
    rows = height * depth * PAIR
    half = jax.ShapeDtypeStruct((rows // chans, filters, width), F32)
    return pl.pallas_call(
        functools.partial(forward_kernel, depth, chans, which),
        out_shape=(half, half),
        in_specs=[SMEM, HBM] + [HBM] * (len(own) + len(other)),
        out_specs=(HBM, HBM),
        scratch_shapes=[
            pltpu.VMEM((rows + 2, width, chans_in), BF16),
            pltpu.VMEM((3 * filters, 3 * chans_in), BF16),
            pltpu.VMEM((2, rows // chans, filters, width), F32),
            pltpu.SemaphoreType.DMA((depth * PAIR,)),
            pltpu.SemaphoreType.DMA((3, 3)),
            pltpu.SemaphoreType.DMA((2, rows // chans // min(4, rows // chans))),
        ],
        compiler_params=params(58),
        cost_estimate=cost(
            36 * rows // chans * width * chans_in * filters, 8 * rows // chans * width * (filters + chans_in)
        ),
        name="forward",
    )(at, weights, *own, *other)


def weight_kernel(depth, scale, at, cot, *refs):
    count = (len(refs) - 7) // 2
    parts = (refs[:count], refs[count : 2 * count])
    out, rows, cots, moved, total, sems, cot_sems = refs[2 * count :]
    wait = load_rows(at, parts, rows, sems, 0, depth * PAIR - 1)
    filters, width = cot.shape[1], cot.shape[2]
    chans_in = rows.shape[2]
    height = parts[0][0].shape[0]
    steps, chunk = cots.shape[0], cots.shape[1]

    def fetch(step):
        return pltpu.make_async_copy(cot.at[pl.ds(1 + step * chunk, chunk)], cots.at[step], cot_sems.at[step])

    for step in range(steps):
        fetch(step).start()
    total[...] = jnp.zeros(total.shape, F32)
    wait(0)

    @pl.loop(0, steps)
    def _(step):
        first = step * chunk
        fetch(step).wait()
        for spot in range(max(1, chunk // height)):
            after_it = first // height + spot + 1

            @pl.when(after_it < depth * PAIR)
            def _():
                wait(after_it)

        for row in range(chunk):
            value = cots[step, row]
            wide = value.astype(F32)
            lanes = pl.ds(row * width, width)
            moved[0:filters, lanes] = lane_shift(wide, -1).astype(BF16)
            moved[filters : 2 * filters, lanes] = value
            moved[2 * filters :, lanes] = lane_shift(wide, 1).astype(BF16)
        for tap_row in range(3):
            window = rows[pl.ds(first + tap_row, chunk)].reshape(chunk * width, chans_in)
            total[tap_row] += jnp.dot(moved[...], window, preferred_element_type=F32)

    stores = []
    for tap_row in range(3):
        total[tap_row] = total[tap_row] * scale
        for tap_col in range(3):
            chosen = (tap_row, pl.ds(tap_col * filters, filters))
            stores.append(pltpu.make_async_copy(total.at[chosen], out.at[chosen], cot_sems.at[steps + 3 * tap_row + tap_col]))
            stores[-1].start()
    for store in stores:
        store.wait()


def weight_gradient(depth, at, scale, cot, own, other):
    height, width, chans_in = own[0].shape
    rows, filters = cot.shape[0] - 2, cot.shape[1]
    chunk = max(height, min(8, rows))
    return pl.pallas_call(
        functools.partial(weight_kernel, depth, scale),
        out_shape=jax.ShapeDtypeStruct((3, 3 * filters, chans_in), F32),
        in_specs=[SMEM, HBM] + [HBM] * (len(own) + len(other)),
        out_specs=HBM,
        scratch_shapes=[
            pltpu.VMEM((rows + 2, width, chans_in), BF16),
            pltpu.VMEM((rows // chunk, chunk, filters, width), BF16),
            pltpu.VMEM((3 * filters, chunk * width), BF16),
            pltpu.VMEM((3, 3 * filters, chans_in), F32),
            pltpu.SemaphoreType.DMA((depth * PAIR,)),
            pltpu.SemaphoreType.DMA((rows // chunk + 9,)),
        ],
        compiler_params=params(58),
        cost_estimate=cost(18 * rows * width * chans_in * filters, 2 * rows * width * (filters + chans_in)),
        name="weight_gradient",
    )(at, cot, *own, *other)


def turn_kernel(same, cross, out):
    fars, _, rows = same.shape[:3]
    unroll = max(n for n in (1, 2, 3, 6) if rows % n == 0)

    @pl.loop(0, rows // unroll)
    def _(step):
        for n in range(unroll):
            row = step * unroll + n
            out[0, row] = jnp.concatenate([part[far, 0, row] for far in range(fars) for part in (same, cross)], axis=0).T


def turned(same, cross):
    fars, depth, rows, part, width = same.shape
    filters = 2 * fars * part
    spec = pl.BlockSpec((fars, 1, rows, part, width), lambda d: (0, d, 0, 0, 0))
    return pl.pallas_call(
        turn_kernel,
        grid=(depth,),
        out_shape=jax.ShapeDtypeStruct((depth, rows, width, filters), BF16),
        in_specs=[spec, spec],
        out_specs=pl.BlockSpec((1, rows, width, filters), lambda d: (d, 0, 0, 0)),
        compiler_params=params(58),
        cost_estimate=cost(0, 4 * depth * rows * width * filters),
        name="turned",
    )(same, cross)


def input_kernel(chans, at, cot, kernels, keep, send, source, taps, stacked, made, sems, out_sems):
    side, far, core = at[1], at[2], at[3]
    depth, rows, width, filters = source.shape
    rows = rows - 2
    chans_in = taps.shape[3]
    copies = []
    for n in range(depth):
        copies.append(
            (
                pltpu.make_async_copy(kernels.at[n], taps.at[n], sems.at[n, 0]),
                [
                    pltpu.make_async_copy(
                        cot.at[n, pl.ds(first, (rows + 2) // 2)],
                        source.at[n, pl.ds(first, (rows + 2) // 2)],
                        sems.at[n, 1 + (first > 0)],
                    )
                    for first in (0, (rows + 2) // 2)
                ],
            )
        )
        copies[n][0].start()
    for n in range(depth):
        for copy in copies[n][1]:
            copy.start()
    part = filters // chans
    places = chans if part % 16 == 0 else 1
    size = filters // places
    for n in range(depth):
        copies[n][0].wait()
        for place in range(places):
            chan = lax.rem(far - place // 2 + chans // 2, chans // 2) * 2 + lax.rem(core + place, 2)
            of_chan = pl.ds(0 if places == 1 else pl.multiple_of(chan * size, size), size)
            for i in range(3):
                for j in range(3):
                    stacked[
                        pl.ds((n * 3 + i) * filters + place * size, size), pl.ds(j * chans_in, chans_in)
                    ] = taps[n, 3 * i + j, of_chan]
    for n in range(depth):
        for copy in copies[n][1]:
            copy.wait()
    half = rows // PAIR
    chunk = min(4, half)
    lanes = lax.broadcasted_iota(jnp.int32, (width, chans_in), 0)

    def result(place, step):
        chosen = pl.ds(step * chunk, chunk)
        return pltpu.make_async_copy(made.at[place, chosen], (send, keep)[place].at[chosen], out_sems.at[place, step])

    for place, of_side in enumerate((1 - side, side)):
        for step in range(half // chunk):
            first = of_side * half + step * chunk
            window = [
                source[n, pl.ds(first + 2 - i, chunk)].reshape(chunk * width, filters)
                for n in range(depth)
                for i in range(3)
            ]
            if filters % 128 == 0:
                product = jnp.dot(jnp.concatenate(window, axis=1), stacked[...], preferred_element_type=F32)
            else:
                product = sum(
                    jnp.dot(value, stacked[n * filters : (n + 1) * filters], preferred_element_type=F32)
                    for n, value in enumerate(window)
                )
            for row in range(chunk):
                here = [
                    product[row * width : (row + 1) * width, j * chans_in : (j + 1) * chans_in] for j in range(3)
                ]
                before_it = jnp.where(lanes < width - 1, pltpu.roll(here[0], width - 1, 0), 0.0)
                behind_it = jnp.where(lanes >= 1, pltpu.roll(here[2], 1, 0), 0.0)
                made[place, step * chunk + row] = here[1] + before_it + behind_it
            result(place, step).start()

    for place in range(2):
        for step in range(half // chunk):
            result(place, step).wait()


def input_partial(chans, at, cot, kernels):
    depth, rows, width, filters = cot.shape
    rows = rows - 2
    chans_in = kernels.shape[3]
    half = jax.ShapeDtypeStruct((rows // PAIR, width, chans_in), F32)
    return pl.pallas_call(
        functools.partial(input_kernel, chans),
        out_shape=(half, half),
        in_specs=[SMEM, HBM, HBM],
        out_specs=(HBM, HBM),
        scratch_shapes=[
            pltpu.VMEM(cot.shape, BF16),
            pltpu.VMEM(kernels.shape, BF16),
            pltpu.VMEM((depth * 3 * filters, 3 * chans_in), BF16),
            pltpu.VMEM((PAIR, rows // PAIR, width, chans_in), F32),
            pltpu.SemaphoreType.DMA((depth, 3)),
            pltpu.SemaphoreType.DMA((PAIR, rows // PAIR // min(4, rows // PAIR))),
        ],
        compiler_params=params(58),
        cost_estimate=cost(
            18 * rows * width * chans_in * filters * depth, 2 * depth * filters * ((rows + 2) * width + 9 * chans_in)
        ),
        name="input_gradient",
    )(at, cot, kernels)


def fars_gather(value, chans):
    got = [value]
    for step in range(1, chans // 2):
        got.append(lax.ppermute(value, "chan", [(c, (c + 2 * step) % chans) for c in range(chans)]))
    return jnp.stack(got)


def lines(depth):
    return [[z * PAIR + y for z in range(depth)] for y in range(PAIR)]


def line_step(along, step, depth):
    up = [(z * PAIR + y, (z + 1) * PAIR + y) for z in range(step - 1, depth - 1) for y in range(PAIR)]
    down = [(z * PAIR + y, (z - 1) * PAIR + y) for z in range(1, depth - step + 1) for y in range(PAIR)]
    along = dict(along)
    along[-step] = lax.ppermute(along[1 - step], "filt", up)
    along[step] = lax.ppermute(along[step - 1], "filt", down)
    if step == 1 and depth > 2:
        ends = (0, depth - 1)
        across = [(z * PAIR + y, (depth - 1 - z) * PAIR + y) for z in ends for y in range(PAIR)]
        along[depth - 1] = along[1 - depth] = lax.ppermute(along[0], "filt", across)
    return along


def core_swap(value, chans):
    return lax.ppermute(value, "chan", [(c, c ^ 1) for c in range(chans)])


def pair_swap(value, depth):
    pairs = [(z * PAIR + y, z * PAIR + 1 - y) for z in range(depth) for y in range(PAIR)]
    return lax.ppermute(value, "filt", pairs)


def body(inputs, weights, cotangent):
    chans, filts = lax.axis_size("chan"), lax.axis_size("filt")
    depth = filts // PAIR
    chan, filt = lax.axis_index("chan"), lax.axis_index("filt")
    line, side = filt // PAIR, filt % PAIR
    far, core = chan // 2, chan % 2
    spots = jnp.asarray([[z] + [z + way for way in arrivals(depth, z)] for z in range(depth)], jnp.int32)
    at = jnp.concatenate([jnp.stack([line, side, far, core]).astype(jnp.int32), spots[line]])
    own_rows, width, chans_in = inputs.shape[1:]
    block, filters = cotangent.shape[1], cotangent.shape[2]
    height = own_rows * filts
    scale = 1.0 / math.sqrt(inputs.shape[0] * height * width)

    part = filters // chans
    line_rows = own_rows * PAIR

    def all_rows(same):
        cross = core_swap(same, chans)
        padded = jnp.zeros((height + 2, filters, width), BF16)
        for step in range(chans // 2):
            at_far = lax.rem(far - step + chans // 2, chans // 2) * 2
            padded = lax.dynamic_update_slice(padded, same[step], (1 + (at_far + core) * block, 0, 0))
            padded = lax.dynamic_update_slice(padded, cross[step], (1 + (at_far + 1 - core) * block, 0, 0))
        return padded

    def line_pieces(padded):
        own_part = lax.dynamic_slice_in_dim(padded, chan * part, part, axis=1)
        return jnp.stack([own_part[z * line_rows : (z + 1) * line_rows + 2] for z in range(depth)])

    def exchange(pieces):
        return lax.all_to_all(pieces, "filt", 0, 0, axis_index_groups=lines(depth), tiled=True)

    halves = PAIR if chans_in % (PAIR * 128) == 0 else 1
    kernels = []
    for half in jnp.split(weights, halves, axis=3):
        half = half.reshape((9,) + half.shape[2:])
        kernels.append(lax.all_gather(half, "filt", axis=0, axis_index_groups=lines(depth)))

    mine, theirs = [inputs[0]], [pair_swap(inputs[0], depth)]
    same = fars_gather(cotangent[0], chans)
    along = line_step({0: inputs[0]}, 1, depth)
    fresh = theirs + [same]
    stages = max(2, depth - 1)
    for stage in range(2, stages + 1):
        ways = list(along)
        ready = lax.optimization_barrier([along[way] for way in ways] + fresh)
        along = dict(zip(ways, ready))
        if stage == 2:
            padded = all_rows(ready[-1])
            pieces = line_pieces(padded)
        fresh = []
        if stage < stages:
            along = line_step(along, stage, depth)
        while len(theirs) < min(depth, stage + 1):
            mine.append(arrival(along, depth, line, len(theirs) - 1))
            theirs.append(pair_swap(mine[-1], depth))
            fresh.append(theirs[-1])
        fresh.append(pieces)
    pieces = exchange(pieces)
    same = fars_gather(pieces, chans)
    sources = turned(same, core_swap(same, chans))

    if part % 16:
        order = [(far - c // 2 + chans // 2) % (chans // 2) * 2 + (core + c) % 2 for c in range(chans)]
        split = [half.reshape((depth, 9, chans, part, -1)) for half in kernels]
        kernels = [jnp.take(half, jnp.stack(order), axis=2).reshape(kernels[0].shape) for half in split]

    outputs, came, at_next = None, [], after(at, kernels[0], pieces)
    for which in [*range(1, chans // 2), 0]:
        keep, send = forward_partial(depth, chans, which, at_next, weights, mine, theirs)
        at_next = after(at, send)
        moving = keep + core_swap(send, chans)
        if which:
            at_next = after(at_next, moving)
            moving = lax.ppermute(moving, "chan", [(c, (c + 2 * which) % chans) for c in range(chans)])
            came.append(moving)
        outputs = moving if outputs is None else outputs + moving
    outputs = outputs.astype(BF16)[None]

    input_grad = []
    for half in kernels:
        kept, sent = input_partial(chans, at_next, sources, half)
        at_next = after(at_next, sent, *came)
        input_grad.append((kept + pair_swap(sent, depth)).astype(BF16))
    at_next = after(at_next, *input_grad[:-1])
    input_grad = jnp.concatenate(input_grad, axis=2)[None]
    weight_grad = weight_gradient(depth, at_next, scale, padded, mine, theirs)
    weight_grad = weight_grad.reshape((3, 3, filters, chans_in))
    return (outputs, input_grad, weight_grad)


def solution(mesh):
    return jax.shard_map(
        body,
        mesh=mesh,
        in_specs=(
            P(None, "filt", None, "chan"),
            P(None, None, "filt", "chan"),
            P(None, "chan", "filt", None),
        ),
        out_specs=(
            P(None, "chan", "filt", None),
            P(None, "filt", None, "chan"),
            P(None, None, "filt", "chan"),
        ),
        check_vma=False,
    )
```

```python
import functools
import math

import jax
import jax.numpy as jnp
from jax import lax
from jax.experimental import pallas as pl
from jax.experimental.pallas import tpu as pltpu
from jax.sharding import PartitionSpec as P

F32 = jnp.float32
BF16 = jnp.bfloat16
NT = (((1,), (1,)), ((), ()))
HBM = pl.BlockSpec(memory_space=pltpu.HBM)
VMEM = pl.BlockSpec(memory_space=pltpu.VMEM)
SMEM = pl.BlockSpec(memory_space=pltpu.SMEM)
PAIR = 2


def params(mib):
    return pltpu.CompilerParams(vmem_limit_bytes=mib << 20)


def cost(flops, moved):
    return pl.CostEstimate(flops=int(flops), bytes_accessed=int(moved), transcendentals=0)


def lane_shift(value, by):
    size = value.shape[1]
    lane = lax.broadcasted_iota(jnp.int32, value.shape, 1)
    keep = lane >= by if by > 0 else lane < size + by
    return jnp.where(keep, pltpu.roll(value, by % size, 1), 0.0)


def after(value, *others):
    return lax.optimization_barrier((value,) + others)[0]


def arrivals(depth, line):
    ways = sorted((way for way in range(-line, depth - line) if way), key=abs)
    if abs(ways[-1]) == depth - 1:
        ways.insert(1, ways.pop())
    return ways


def arrival(along, depth, line, place):
    picked = None
    for z in range(depth):
        value = along[arrivals(depth, z)[place]]
        picked = value if picked is None or value is picked else jnp.where(line == z, value, picked)
    return picked


def load_rows(at, parts, rows, sems, first, last):
    height = parts[0][0].shape[0]

    def place(spot):
        return rows.at[pl.ds(1 + spot * height, height)]

    for half in range(PAIR):
        of_side = lax.rem(at[1] + half, PAIR)
        for index, part in enumerate(parts[half]):
            spot = at[4 + index] * PAIR + of_side

            @pl.when(jnp.logical_and(spot >= first, spot <= last))
            def _():
                pltpu.make_async_copy(part, place(spot), sems.at[spot]).start()

    rows[0] = jnp.zeros(rows.shape[1:], rows.dtype)
    rows[rows.shape[0] - 1] = jnp.zeros(rows.shape[1:], rows.dtype)
    return lambda spot: pltpu.make_async_copy(parts[0][0], place(spot), sems.at[spot]).wait()


def forward_kernel(depth, chans, which, at, weights, *refs):
    count = (len(refs) - 8) // 2
    parts = (refs[:count], refs[count : 2 * count])
    keep, send, rows, taps, made, sems, tap_sems, out_sems = refs[2 * count :]
    filters, chans_in = weights.shape[2], weights.shape[3]
    width = rows.shape[1]
    block = keep.shape[0]
    height = parts[0][0].shape[0]
    far, core = at[2], at[3]
    top = lax.rem(far + which, chans // 2) * 2 * block
    first, spots = top // height, max(1, 2 * block // height)
    wait = load_rows(at, parts, rows, sems, first - 1, first + spots)
    fetches = [
        pltpu.make_async_copy(
            weights.at[tap_row, tap_col],
            taps.at[pl.ds(tap_col * filters, filters), pl.ds(tap_row * chans_in, chans_in)],
            tap_sems.at[tap_row, tap_col],
        )
        for tap_row in range(3)
        for tap_col in range(3)
    ]
    for fetch in fetches:
        fetch.start()
    for fetch in fetches:
        fetch.wait()
    for spot in range(-1, spots + 1):

        @pl.when(jnp.logical_and(first + spot >= 0, first + spot < depth * PAIR))
        def _():
            wait(first + spot)

    group = min(8, block)

    def result(step, place):
        chosen = pl.ds(step * group, group)
        return pltpu.make_async_copy(made.at[place, chosen], (send, keep)[place].at[chosen], out_sems.at[place, step])

    @pl.loop(0, block // group)
    def _(step):
        for place, of_core in enumerate((1 - core, core)):
            start = top + of_core * block + step * group
            window = jnp.concatenate(
                [rows[pl.ds(start + i, group)].reshape(group * width, chans_in) for i in range(3)], axis=1
            )
            product = lax.dot_general(taps[...], window, NT, preferred_element_type=F32)
            for row in range(group):
                part = [
                    product[j * filters : (j + 1) * filters, row * width : (row + 1) * width] for j in range(3)
                ]
                made[place, step * group + row] = part[1] + lane_shift(part[0], 1) + lane_shift(part[2], -1)
            result(step, place).start()

    for step in range(block // group):
        for place in range(2):
            result(step, place).wait()


def forward_partial(depth, chans, which, at, weights, own, other):
    height, width, chans_in = own[0].shape
    filters = weights.shape[2]
    rows = height * depth * PAIR
    half = jax.ShapeDtypeStruct((rows // chans, filters, width), F32)
    return pl.pallas_call(
        functools.partial(forward_kernel, depth, chans, which),
        out_shape=(half, half),
        in_specs=[SMEM, HBM] + [HBM] * (len(own) + len(other)),
        out_specs=(HBM, HBM),
        scratch_shapes=[
            pltpu.VMEM((rows + 2, width, chans_in), BF16),
            pltpu.VMEM((3 * filters, 3 * chans_in), BF16),
            pltpu.VMEM((2, rows // chans, filters, width), F32),
            pltpu.SemaphoreType.DMA((depth * PAIR,)),
            pltpu.SemaphoreType.DMA((3, 3)),
            pltpu.SemaphoreType.DMA((2, rows // chans // min(8, rows // chans))),
        ],
        compiler_params=params(58),
        cost_estimate=cost(
            36 * rows // chans * width * chans_in * filters, 8 * rows // chans * width * (filters + chans_in)
        ),
        name="forward",
    )(at, weights, *own, *other)


def weight_kernel(depth, scale, at, cot, *refs):
    count = (len(refs) - 7) // 2
    parts = (refs[:count], refs[count : 2 * count])
    out, rows, cots, moved, total, sems, cot_sems = refs[2 * count :]
    wait = load_rows(at, parts, rows, sems, 0, depth * PAIR - 1)
    filters, width = cot.shape[1], cot.shape[2]
    chans_in = rows.shape[2]
    height = parts[0][0].shape[0]
    steps, chunk = cots.shape[0], cots.shape[1]

    def fetch(step):
        return pltpu.make_async_copy(cot.at[pl.ds(1 + step * chunk, chunk)], cots.at[step], cot_sems.at[step])

    for step in range(steps):
        fetch(step).start()
    total[...] = jnp.zeros(total.shape, F32)
    wait(0)

    @pl.loop(0, steps)
    def _(step):
        first = step * chunk
        fetch(step).wait()
        for spot in range(max(1, chunk // height)):
            after_it = first // height + spot + 1

            @pl.when(after_it < depth * PAIR)
            def _():
                wait(after_it)

        for row in range(chunk):
            value = cots[step, row]
            wide = value.astype(F32)
            lanes = pl.ds(row * width, width)
            moved[0:filters, lanes] = lane_shift(wide, -1).astype(BF16)
            moved[filters : 2 * filters, lanes] = value
            moved[2 * filters :, lanes] = lane_shift(wide, 1).astype(BF16)
        for tap_row in range(3):
            window = rows[pl.ds(first + tap_row, chunk)].reshape(chunk * width, chans_in)
            total[tap_row] += jnp.dot(moved[...], window, preferred_element_type=F32)

    stores = []
    for tap_row in range(3):
        total[tap_row] = total[tap_row] * scale
        for tap_col in range(3):
            chosen = (tap_row, pl.ds(tap_col * filters, filters))
            stores.append(pltpu.make_async_copy(total.at[chosen], out.at[chosen], cot_sems.at[steps + 3 * tap_row + tap_col]))
            stores[-1].start()
    for store in stores:
        store.wait()


def weight_gradient(depth, at, scale, cot, own, other):
    height, width, chans_in = own[0].shape
    rows, filters = cot.shape[0] - 2, cot.shape[1]
    chunk = max(height, min(8, rows))
    return pl.pallas_call(
        functools.partial(weight_kernel, depth, scale),
        out_shape=jax.ShapeDtypeStruct((3, 3 * filters, chans_in), F32),
        in_specs=[SMEM, HBM] + [HBM] * (len(own) + len(other)),
        out_specs=HBM,
        scratch_shapes=[
            pltpu.VMEM((rows + 2, width, chans_in), BF16),
            pltpu.VMEM((rows // chunk, chunk, filters, width), BF16),
            pltpu.VMEM((3 * filters, chunk * width), BF16),
            pltpu.VMEM((3, 3 * filters, chans_in), F32),
            pltpu.SemaphoreType.DMA((depth * PAIR,)),
            pltpu.SemaphoreType.DMA((rows // chunk + 9,)),
        ],
        compiler_params=params(58),
        cost_estimate=cost(18 * rows * width * chans_in * filters, 2 * rows * width * (filters + chans_in)),
        name="weight_gradient",
    )(at, cot, *own, *other)


def turn_kernel(same, cross, out):
    fars, _, rows = same.shape[:3]
    unroll = max(n for n in (1, 2, 3, 6) if rows % n == 0)

    @pl.loop(0, rows // unroll)
    def _(step):
        for n in range(unroll):
            row = step * unroll + n
            out[0, row] = jnp.concatenate([part[far, 0, row] for far in range(fars) for part in (same, cross)], axis=0).T


def turned(same, cross):
    fars, depth, rows, part, width = same.shape
    filters = 2 * fars * part
    spec = pl.BlockSpec((fars, 1, rows, part, width), lambda d: (0, d, 0, 0, 0))
    return pl.pallas_call(
        turn_kernel,
        grid=(depth,),
        out_shape=jax.ShapeDtypeStruct((depth, rows, width, filters), BF16),
        in_specs=[spec, spec],
        out_specs=pl.BlockSpec((1, rows, width, filters), lambda d: (d, 0, 0, 0)),
        compiler_params=params(58),
        cost_estimate=cost(0, 4 * depth * rows * width * filters),
        name="turned",
    )(same, cross)


def input_kernel(chans, at, cot, kernels, keep, send, source, taps, stacked, made, sems, out_sems):
    side, far, core = at[1], at[2], at[3]
    depth, rows, width, filters = source.shape
    rows = rows - 2
    chans_in = taps.shape[3]
    copies = []
    for n in range(depth):
        copies.append(
            (
                pltpu.make_async_copy(kernels.at[n], taps.at[n], sems.at[n, 0]),
                [
                    pltpu.make_async_copy(
                        cot.at[n, pl.ds(first, (rows + 2) // 2)],
                        source.at[n, pl.ds(first, (rows + 2) // 2)],
                        sems.at[n, 1 + (first > 0)],
                    )
                    for first in (0, (rows + 2) // 2)
                ],
            )
        )
        copies[n][0].start()
    for n in range(depth):
        for copy in copies[n][1]:
            copy.start()
    part = filters // chans
    places = chans if part % 16 == 0 else 1
    size = filters // places
    for n in range(depth):
        copies[n][0].wait()
        for place in range(places):
            chan = lax.rem(far - place // 2 + chans // 2, chans // 2) * 2 + lax.rem(core + place, 2)
            of_chan = pl.ds(0 if places == 1 else pl.multiple_of(chan * size, size), size)
            for i in range(3):
                for j in range(3):
                    stacked[
                        pl.ds((n * 3 + i) * filters + place * size, size), pl.ds(j * chans_in, chans_in)
                    ] = taps[n, 3 * i + j, of_chan]
    for n in range(depth):
        for copy in copies[n][1]:
            copy.wait()
    half = rows // PAIR
    chunk = min(8, half)
    lanes = lax.broadcasted_iota(jnp.int32, (width, chans_in), 0)

    def result(place, step):
        chosen = pl.ds(step * chunk, chunk)
        return pltpu.make_async_copy(made.at[place, chosen], (send, keep)[place].at[chosen], out_sems.at[place, step])

    for place, of_side in enumerate((1 - side, side)):
        for step in range(half // chunk):
            first = of_side * half + step * chunk
            window = [
                source[n, pl.ds(first + 2 - i, chunk)].reshape(chunk * width, filters)
                for n in range(depth)
                for i in range(3)
            ]
            if filters % 128 == 0:
                product = jnp.dot(jnp.concatenate(window, axis=1), stacked[...], preferred_element_type=F32)
            else:
                product = sum(
                    jnp.dot(value, stacked[n * filters : (n + 1) * filters], preferred_element_type=F32)
                    for n, value in enumerate(window)
                )
            for row in range(chunk):
                here = [
                    product[row * width : (row + 1) * width, j * chans_in : (j + 1) * chans_in] for j in range(3)
                ]
                before_it = jnp.where(lanes < width - 1, pltpu.roll(here[0], width - 1, 0), 0.0)
                behind_it = jnp.where(lanes >= 1, pltpu.roll(here[2], 1, 0), 0.0)
                made[place, step * chunk + row] = here[1] + before_it + behind_it
            result(place, step).start()

    for place in range(2):
        for step in range(half // chunk):
            result(place, step).wait()


def input_partial(chans, at, cot, kernels):
    depth, rows, width, filters = cot.shape
    rows = rows - 2
    chans_in = kernels.shape[3]
    half = jax.ShapeDtypeStruct((rows // PAIR, width, chans_in), F32)
    return pl.pallas_call(
        functools.partial(input_kernel, chans),
        out_shape=(half, half),
        in_specs=[SMEM, HBM, HBM],
        out_specs=(HBM, HBM),
        scratch_shapes=[
            pltpu.VMEM(cot.shape, BF16),
            pltpu.VMEM(kernels.shape, BF16),
            pltpu.VMEM((depth * 3 * filters, 3 * chans_in), BF16),
            pltpu.VMEM((PAIR, rows // PAIR, width, chans_in), F32),
            pltpu.SemaphoreType.DMA((depth, 3)),
            pltpu.SemaphoreType.DMA((PAIR, rows // PAIR // min(8, rows // PAIR))),
        ],
        compiler_params=params(58),
        cost_estimate=cost(
            18 * rows * width * chans_in * filters * depth, 2 * depth * filters * ((rows + 2) * width + 9 * chans_in)
        ),
        name="input_gradient",
    )(at, cot, kernels)


def fars_gather(value, chans):
    got = [value]
    for step in range(1, chans // 2):
        got.append(lax.ppermute(value, "chan", [(c, (c + 2 * step) % chans) for c in range(chans)]))
    return jnp.stack(got)


def lines(depth):
    return [[z * PAIR + y for z in range(depth)] for y in range(PAIR)]


def line_step(along, step, depth):
    up = [(z * PAIR + y, (z + 1) * PAIR + y) for z in range(step - 1, depth - 1) for y in range(PAIR)]
    down = [(z * PAIR + y, (z - 1) * PAIR + y) for z in range(1, depth - step + 1) for y in range(PAIR)]
    along = dict(along)
    along[-step] = lax.ppermute(along[1 - step], "filt", up)
    along[step] = lax.ppermute(along[step - 1], "filt", down)
    if step == 1 and depth > 2:
        ends = (0, depth - 1)
        across = [(z * PAIR + y, (depth - 1 - z) * PAIR + y) for z in ends for y in range(PAIR)]
        along[depth - 1] = along[1 - depth] = lax.ppermute(along[0], "filt", across)
    return along


def core_swap(value, chans):
    return lax.ppermute(value, "chan", [(c, c ^ 1) for c in range(chans)])


def pair_swap(value, depth):
    pairs = [(z * PAIR + y, z * PAIR + 1 - y) for z in range(depth) for y in range(PAIR)]
    return lax.ppermute(value, "filt", pairs)


def body(inputs, weights, cotangent):
    chans, filts = lax.axis_size("chan"), lax.axis_size("filt")
    depth = filts // PAIR
    chan, filt = lax.axis_index("chan"), lax.axis_index("filt")
    line, side = filt // PAIR, filt % PAIR
    far, core = chan // 2, chan % 2
    spots = jnp.asarray([[z] + [z + way for way in arrivals(depth, z)] for z in range(depth)], jnp.int32)
    at = jnp.concatenate([jnp.stack([line, side, far, core]).astype(jnp.int32), spots[line]])
    own_rows, width, chans_in = inputs.shape[1:]
    block, filters = cotangent.shape[1], cotangent.shape[2]
    height = own_rows * filts
    scale = 1.0 / math.sqrt(inputs.shape[0] * height * width)

    part = filters // chans
    line_rows = own_rows * PAIR

    def all_rows(same):
        cross = core_swap(same, chans)
        padded = jnp.zeros((height + 2, filters, width), BF16)
        for step in range(chans // 2):
            at_far = lax.rem(far - step + chans // 2, chans // 2) * 2
            padded = lax.dynamic_update_slice(padded, same[step], (1 + (at_far + core) * block, 0, 0))
            padded = lax.dynamic_update_slice(padded, cross[step], (1 + (at_far + 1 - core) * block, 0, 0))
        return padded

    def line_pieces(padded):
        own_part = lax.dynamic_slice_in_dim(padded, chan * part, part, axis=1)
        return jnp.stack([own_part[z * line_rows : (z + 1) * line_rows + 2] for z in range(depth)])

    def exchange(pieces):
        return lax.all_to_all(pieces, "filt", 0, 0, axis_index_groups=lines(depth), tiled=True)

    halves = PAIR if chans_in % (PAIR * 128) == 0 else 1
    kernels = []
    for half in jnp.split(weights, halves, axis=3):
        half = half.reshape((9,) + half.shape[2:])
        kernels.append(lax.all_gather(half, "filt", axis=0, axis_index_groups=lines(depth)))

    mine, theirs = [inputs[0]], [pair_swap(inputs[0], depth)]
    same = fars_gather(cotangent[0], chans)
    along = line_step({0: inputs[0]}, 1, depth)
    fresh = theirs + [same]
    stages = max(2, depth - 1)
    for stage in range(2, stages + 1):
        ways = list(along)
        ready = lax.optimization_barrier([along[way] for way in ways] + fresh)
        along = dict(zip(ways, ready))
        if stage == 2:
            padded = all_rows(ready[-1])
            pieces = line_pieces(padded)
        fresh = []
        if stage < stages:
            along = line_step(along, stage, depth)
        while len(theirs) < min(depth, stage + 1):
            mine.append(arrival(along, depth, line, len(theirs) - 1))
            theirs.append(pair_swap(mine[-1], depth))
            fresh.append(theirs[-1])
        fresh.append(pieces)
    pieces = exchange(pieces)
    same = fars_gather(pieces, chans)
    sources = turned(same, core_swap(same, chans))

    if part % 16:
        order = [(far - c // 2 + chans // 2) % (chans // 2) * 2 + (core + c) % 2 for c in range(chans)]
        split = [half.reshape((depth, 9, chans, part, -1)) for half in kernels]
        kernels = [jnp.take(half, jnp.stack(order), axis=2).reshape(kernels[0].shape) for half in split]

    outputs, came, at_next = None, [], after(at, kernels[0], pieces)
    for which in [*range(1, chans // 2), 0]:
        keep, send = forward_partial(depth, chans, which, at_next, weights, mine, theirs)
        at_next = after(at, send)
        moving = keep + core_swap(send, chans)
        if which:
            at_next = after(at_next, moving)
            moving = lax.ppermute(moving, "chan", [(c, (c + 2 * which) % chans) for c in range(chans)])
            came.append(moving)
        outputs = moving if outputs is None else outputs + moving
    outputs = outputs.astype(BF16)[None]

    input_grad = []
    for half in kernels:
        kept, sent = input_partial(chans, at_next, sources, half)
        at_next = after(at_next, sent, *came)
        input_grad.append((kept + pair_swap(sent, depth)).astype(BF16))
    at_next = after(at_next, *input_grad[:-1])
    input_grad = jnp.concatenate(input_grad, axis=2)[None]
    weight_grad = weight_gradient(depth, at_next, scale, padded, mine, theirs)
    weight_grad = weight_grad.reshape((3, 3, filters, chans_in))
    return (outputs, input_grad, weight_grad)


def solution(mesh):
    return jax.shard_map(
        body,
        mesh=mesh,
        in_specs=(
            P(None, "filt", None, "chan"),
            P(None, None, "filt", "chan"),
            P(None, "chan", "filt", None),
        ),
        out_specs=(
            P(None, "chan", "filt", None),
            P(None, "filt", None, "chan"),
            P(None, None, "filt", "chan"),
        ),
        check_vma=False,
    )
```

```python
import functools
import math

import jax
import jax.numpy as jnp
from jax import lax
from jax.experimental import pallas as pl
from jax.experimental.pallas import tpu as pltpu
from jax.sharding import PartitionSpec as P

F32 = jnp.float32
BF16 = jnp.bfloat16
NT = (((1,), (1,)), ((), ()))
HBM = pl.BlockSpec(memory_space=pltpu.HBM)
VMEM = pl.BlockSpec(memory_space=pltpu.VMEM)
SMEM = pl.BlockSpec(memory_space=pltpu.SMEM)
PAIR = 2


def params(mib):
    return pltpu.CompilerParams(vmem_limit_bytes=mib << 20)


def cost(flops, moved):
    return pl.CostEstimate(flops=int(flops), bytes_accessed=int(moved), transcendentals=0)


def lane_shift(value, by):
    size = value.shape[1]
    lane = lax.broadcasted_iota(jnp.int32, value.shape, 1)
    keep = lane >= by if by > 0 else lane < size + by
    return jnp.where(keep, pltpu.roll(value, by % size, 1), 0.0)


def after(value, *others):
    return lax.optimization_barrier((value,) + others)[0]


def arrivals(depth, line):
    ways = sorted((way for way in range(-line, depth - line) if way), key=abs)
    if abs(ways[-1]) == depth - 1:
        ways.insert(1, ways.pop())
    return ways


def arrival(along, depth, line, place):
    picked = None
    for z in range(depth):
        value = along[arrivals(depth, z)[place]]
        picked = value if picked is None or value is picked else jnp.where(line == z, value, picked)
    return picked


def load_rows(at, parts, rows, sems, first, last):
    height = parts[0][0].shape[0]

    def place(spot):
        return rows.at[pl.ds(1 + spot * height, height)]

    for half in range(PAIR):
        of_side = lax.rem(at[1] + half, PAIR)
        for index, part in enumerate(parts[half]):
            spot = at[4 + index] * PAIR + of_side

            @pl.when(jnp.logical_and(spot >= first, spot <= last))
            def _():
                pltpu.make_async_copy(part, place(spot), sems.at[spot]).start()

    rows[0] = jnp.zeros(rows.shape[1:], rows.dtype)
    rows[rows.shape[0] - 1] = jnp.zeros(rows.shape[1:], rows.dtype)
    return lambda spot: pltpu.make_async_copy(parts[0][0], place(spot), sems.at[spot]).wait()


def forward_kernel(depth, chans, which, at, weights, *refs):
    count = (len(refs) - 8) // 2
    parts = (refs[:count], refs[count : 2 * count])
    keep, send, rows, taps, made, sems, tap_sems, out_sems = refs[2 * count :]
    filters, chans_in = weights.shape[2], weights.shape[3]
    width = rows.shape[1]
    block = keep.shape[0]
    height = parts[0][0].shape[0]
    far, core = at[2], at[3]
    top = lax.rem(far + which, chans // 2) * 2 * block
    first, spots = top // height, max(1, 2 * block // height)
    wait = load_rows(at, parts, rows, sems, first - 1, first + spots)
    fetches = [
        pltpu.make_async_copy(
            weights.at[tap_row, tap_col],
            taps.at[pl.ds(tap_col * filters, filters), pl.ds(tap_row * chans_in, chans_in)],
            tap_sems.at[tap_row, tap_col],
        )
        for tap_row in range(3)
        for tap_col in range(3)
    ]
    for fetch in fetches:
        fetch.start()
    for fetch in fetches:
        fetch.wait()
    for spot in range(-1, spots + 1):

        @pl.when(jnp.logical_and(first + spot >= 0, first + spot < depth * PAIR))
        def _():
            wait(first + spot)

    group = min(4, block)

    def result(step, place):
        chosen = pl.ds(step * group, group)
        return pltpu.make_async_copy(made.at[place, chosen], (send, keep)[place].at[chosen], out_sems.at[place, step])

    @pl.loop(0, block // group)
    def _(step):
        for place, of_core in enumerate((1 - core, core)):
            start = top + of_core * block + step * group
            window = jnp.concatenate(
                [rows[pl.ds(start + i, group)].reshape(group * width, chans_in) for i in range(3)], axis=1
            )
            product = lax.dot_general(taps[...], window, NT, preferred_element_type=F32)
            for row in range(group):
                part = [
                    product[j * filters : (j + 1) * filters, row * width : (row + 1) * width] for j in range(3)
                ]
                made[place, step * group + row] = part[1] + lane_shift(part[0], 1) + lane_shift(part[2], -1)
            result(step, place).start()

    for step in range(block // group):
        for place in range(2):
            result(step, place).wait()


def forward_partial(depth, chans, which, at, weights, own, other):
    height, width, chans_in = own[0].shape
    filters = weights.shape[2]
    rows = height * depth * PAIR
    half = jax.ShapeDtypeStruct((rows // chans, filters, width), F32)
    return pl.pallas_call(
        functools.partial(forward_kernel, depth, chans, which),
        out_shape=(half, half),
        in_specs=[SMEM, HBM] + [HBM] * (len(own) + len(other)),
        out_specs=(HBM, HBM),
        scratch_shapes=[
            pltpu.VMEM((rows + 2, width, chans_in), BF16),
            pltpu.VMEM((3 * filters, 3 * chans_in), BF16),
            pltpu.VMEM((2, rows // chans, filters, width), F32),
            pltpu.SemaphoreType.DMA((depth * PAIR,)),
            pltpu.SemaphoreType.DMA((3, 3)),
            pltpu.SemaphoreType.DMA((2, rows // chans // min(4, rows // chans))),
        ],
        compiler_params=params(58),
        cost_estimate=cost(
            36 * rows // chans * width * chans_in * filters, 8 * rows // chans * width * (filters + chans_in)
        ),
        name="forward",
    )(at, weights, *own, *other)


def weight_kernel(depth, scale, at, cot, *refs):
    count = (len(refs) - 7) // 2
    parts = (refs[:count], refs[count : 2 * count])
    out, rows, cots, moved, total, sems, cot_sems = refs[2 * count :]
    wait = load_rows(at, parts, rows, sems, 0, depth * PAIR - 1)
    filters, width = cot.shape[1], cot.shape[2]
    chans_in = rows.shape[2]
    height = parts[0][0].shape[0]
    steps, chunk = cots.shape[0], cots.shape[1]

    def fetch(step):
        return pltpu.make_async_copy(cot.at[pl.ds(1 + step * chunk, chunk)], cots.at[step], cot_sems.at[step])

    for step in range(steps):
        fetch(step).start()
    total[...] = jnp.zeros(total.shape, F32)
    wait(0)

    @pl.loop(0, steps)
    def _(step):
        first = step * chunk
        fetch(step).wait()
        for spot in range(max(1, chunk // height)):
            after_it = first // height + spot + 1

            @pl.when(after_it < depth * PAIR)
            def _():
                wait(after_it)

        for row in range(chunk):
            value = cots[step, row]
            wide = value.astype(F32)
            lanes = pl.ds(row * width, width)
            moved[0:filters, lanes] = lane_shift(wide, -1).astype(BF16)
            moved[filters : 2 * filters, lanes] = value
            moved[2 * filters :, lanes] = lane_shift(wide, 1).astype(BF16)
        for tap_row in range(3):
            window = rows[pl.ds(first + tap_row, chunk)].reshape(chunk * width, chans_in)
            total[tap_row] += jnp.dot(moved[...], window, preferred_element_type=F32)

    stores = []
    for tap_row in range(3):
        total[tap_row] = total[tap_row] * scale
        for tap_col in range(3):
            chosen = (tap_row, pl.ds(tap_col * filters, filters))
            stores.append(pltpu.make_async_copy(total.at[chosen], out.at[chosen], cot_sems.at[steps + 3 * tap_row + tap_col]))
            stores[-1].start()
    for store in stores:
        store.wait()


def weight_gradient(depth, at, scale, cot, own, other):
    height, width, chans_in = own[0].shape
    rows, filters = cot.shape[0] - 2, cot.shape[1]
    chunk = max(height, min(8, rows))
    return pl.pallas_call(
        functools.partial(weight_kernel, depth, scale),
        out_shape=jax.ShapeDtypeStruct((3, 3 * filters, chans_in), F32),
        in_specs=[SMEM, HBM] + [HBM] * (len(own) + len(other)),
        out_specs=HBM,
        scratch_shapes=[
            pltpu.VMEM((rows + 2, width, chans_in), BF16),
            pltpu.VMEM((rows // chunk, chunk, filters, width), BF16),
            pltpu.VMEM((3 * filters, chunk * width), BF16),
            pltpu.VMEM((3, 3 * filters, chans_in), F32),
            pltpu.SemaphoreType.DMA((depth * PAIR,)),
            pltpu.SemaphoreType.DMA((rows // chunk + 9,)),
        ],
        compiler_params=params(58),
        cost_estimate=cost(18 * rows * width * chans_in * filters, 2 * rows * width * (filters + chans_in)),
        name="weight_gradient",
    )(at, cot, *own, *other)


def turn_kernel(same, cross, out):
    fars, _, rows = same.shape[:3]
    unroll = max(n for n in (1, 2, 3, 6) if rows % n == 0)

    @pl.loop(0, rows // unroll)
    def _(step):
        for n in range(unroll):
            row = step * unroll + n
            out[0, row] = jnp.concatenate([part[far, 0, row] for far in range(fars) for part in (same, cross)], axis=0).T


def turned(same, cross):
    fars, depth, rows, part, width = same.shape
    filters = 2 * fars * part
    spec = pl.BlockSpec((fars, 1, rows, part, width), lambda d: (0, d, 0, 0, 0))
    return pl.pallas_call(
        turn_kernel,
        grid=(depth,),
        out_shape=jax.ShapeDtypeStruct((depth, rows, width, filters), BF16),
        in_specs=[spec, spec],
        out_specs=pl.BlockSpec((1, rows, width, filters), lambda d: (d, 0, 0, 0)),
        compiler_params=params(58),
        cost_estimate=cost(0, 4 * depth * rows * width * filters),
        name="turned",
    )(same, cross)


def input_kernel(chans, at, cot, kernels, keep, send, source, taps, stacked, made, sems, out_sems):
    side, far, core = at[1], at[2], at[3]
    depth, rows, width, filters = source.shape
    rows = rows - 2
    chans_in = taps.shape[3]
    copies = []
    for n in range(depth):
        copies.append(
            (
                pltpu.make_async_copy(kernels.at[n], taps.at[n], sems.at[n, 0]),
                [
                    pltpu.make_async_copy(
                        cot.at[n, pl.ds(first, (rows + 2) // 2)],
                        source.at[n, pl.ds(first, (rows + 2) // 2)],
                        sems.at[n, 1 + (first > 0)],
                    )
                    for first in (0, (rows + 2) // 2)
                ],
            )
        )
        copies[n][0].start()
    for n in range(depth):
        for copy in copies[n][1]:
            copy.start()
    part = filters // chans
    places = chans if part % 16 == 0 else 1
    size = filters // places
    for n in range(depth):
        copies[n][0].wait()
        for place in range(places):
            chan = lax.rem(far - place // 2 + chans // 2, chans // 2) * 2 + lax.rem(core + place, 2)
            of_chan = pl.ds(0 if places == 1 else pl.multiple_of(chan * size, size), size)
            for i in range(3):
                for j in range(3):
                    stacked[
                        pl.ds((n * 3 + i) * filters + place * size, size), pl.ds(j * chans_in, chans_in)
                    ] = taps[n, 3 * i + j, of_chan]
    for n in range(depth):
        for copy in copies[n][1]:
            copy.wait()
    half = rows // PAIR
    chunk = min(4, half)
    lanes = lax.broadcasted_iota(jnp.int32, (width, chans_in), 0)

    def result(place, step):
        chosen = pl.ds(step * chunk, chunk)
        return pltpu.make_async_copy(made.at[place, chosen], (send, keep)[place].at[chosen], out_sems.at[place, step])

    for place, of_side in enumerate((1 - side, side)):
        for step in range(half // chunk):
            first = of_side * half + step * chunk
            window = [
                source[n, pl.ds(first + 2 - i, chunk)].reshape(chunk * width, filters)
                for n in range(depth)
                for i in range(3)
            ]
            if filters % 128 == 0:
                product = jnp.dot(jnp.concatenate(window, axis=1), stacked[...], preferred_element_type=F32)
            else:
                product = sum(
                    jnp.dot(value, stacked[n * filters : (n + 1) * filters], preferred_element_type=F32)
                    for n, value in enumerate(window)
                )
            for row in range(chunk):
                here = [
                    product[row * width : (row + 1) * width, j * chans_in : (j + 1) * chans_in] for j in range(3)
                ]
                before_it = jnp.where(lanes < width - 1, pltpu.roll(here[0], width - 1, 0), 0.0)
                behind_it = jnp.where(lanes >= 1, pltpu.roll(here[2], 1, 0), 0.0)
                made[place, step * chunk + row] = here[1] + before_it + behind_it
            result(place, step).start()

    for place in range(2):
        for step in range(half // chunk):
            result(place, step).wait()


def input_partial(chans, at, cot, kernels):
    depth, rows, width, filters = cot.shape
    rows = rows - 2
    chans_in = kernels.shape[3]
    half = jax.ShapeDtypeStruct((rows // PAIR, width, chans_in), F32)
    return pl.pallas_call(
        functools.partial(input_kernel, chans),
        out_shape=(half, half),
        in_specs=[SMEM, HBM, HBM],
        out_specs=(HBM, HBM),
        scratch_shapes=[
            pltpu.VMEM(cot.shape, BF16),
            pltpu.VMEM(kernels.shape, BF16),
            pltpu.VMEM((depth * 3 * filters, 3 * chans_in), BF16),
            pltpu.VMEM((PAIR, rows // PAIR, width, chans_in), F32),
            pltpu.SemaphoreType.DMA((depth, 3)),
            pltpu.SemaphoreType.DMA((PAIR, rows // PAIR // min(4, rows // PAIR))),
        ],
        compiler_params=params(58),
        cost_estimate=cost(
            18 * rows * width * chans_in * filters * depth, 2 * depth * filters * ((rows + 2) * width + 9 * chans_in)
        ),
        name="input_gradient",
    )(at, cot, kernels)


def fars_gather(value, chans):
    got = [value]
    for step in range(1, chans // 2):
        got.append(lax.ppermute(value, "chan", [(c, (c + 2 * step) % chans) for c in range(chans)]))
    return jnp.stack(got)


def lines(depth):
    return [[z * PAIR + y for z in range(depth)] for y in range(PAIR)]


def line_step(along, step, depth):
    up = [(z * PAIR + y, (z + 1) * PAIR + y) for z in range(step - 1, depth - 1) for y in range(PAIR)]
    down = [(z * PAIR + y, (z - 1) * PAIR + y) for z in range(1, depth - step + 1) for y in range(PAIR)]
    along = dict(along)
    along[-step] = lax.ppermute(along[1 - step], "filt", up)
    along[step] = lax.ppermute(along[step - 1], "filt", down)
    if step == 1 and depth > 2:
        ends = (0, depth - 1)
        across = [(z * PAIR + y, (depth - 1 - z) * PAIR + y) for z in ends for y in range(PAIR)]
        along[depth - 1] = along[1 - depth] = lax.ppermute(along[0], "filt", across)
    return along


def core_swap(value, chans):
    return lax.ppermute(value, "chan", [(c, c ^ 1) for c in range(chans)])


def pair_swap(value, depth):
    pairs = [(z * PAIR + y, z * PAIR + 1 - y) for z in range(depth) for y in range(PAIR)]
    return lax.ppermute(value, "filt", pairs)


def body(inputs, weights, cotangent):
    chans, filts = lax.axis_size("chan"), lax.axis_size("filt")
    depth = filts // PAIR
    chan, filt = lax.axis_index("chan"), lax.axis_index("filt")
    line, side = filt // PAIR, filt % PAIR
    far, core = chan // 2, chan % 2
    spots = jnp.asarray([[z] + [z + way for way in arrivals(depth, z)] for z in range(depth)], jnp.int32)
    at = jnp.concatenate([jnp.stack([line, side, far, core]).astype(jnp.int32), spots[line]])
    own_rows, width, chans_in = inputs.shape[1:]
    block, filters = cotangent.shape[1], cotangent.shape[2]
    height = own_rows * filts
    scale = 1.0 / math.sqrt(inputs.shape[0] * height * width)

    part = filters // chans
    line_rows = own_rows * PAIR

    def all_rows(same):
        cross = core_swap(same, chans)
        padded = jnp.zeros((height + 2, filters, width), BF16)
        for step in range(chans // 2):
            at_far = lax.rem(far - step + chans // 2, chans // 2) * 2
            padded = lax.dynamic_update_slice(padded, same[step], (1 + (at_far + core) * block, 0, 0))
            padded = lax.dynamic_update_slice(padded, cross[step], (1 + (at_far + 1 - core) * block, 0, 0))
        return padded

    def line_pieces(padded):
        own_part = lax.dynamic_slice_in_dim(padded, chan * part, part, axis=1)
        return jnp.stack([own_part[z * line_rows : (z + 1) * line_rows + 2] for z in range(depth)])

    def exchange(pieces):
        return lax.all_to_all(pieces, "filt", 0, 0, axis_index_groups=lines(depth), tiled=True)

    halves = PAIR if chans_in % (PAIR * 128) == 0 else 1
    kernels = []
    for half in jnp.split(weights, halves, axis=3):
        half = half.reshape((9,) + half.shape[2:])
        kernels.append(lax.all_gather(half, "filt", axis=0, axis_index_groups=lines(depth)))

    mine, theirs = [inputs[0]], [pair_swap(inputs[0], depth)]
    same = fars_gather(cotangent[0], chans)
    along = line_step({0: inputs[0]}, 1, depth)
    fresh = theirs + [same]
    stages = max(2, depth - 1)
    for stage in range(2, stages + 1):
        late = {way: along.pop(way) for way in list(along) if stage == 2 < depth - 1 == abs(way)}
        ways = list(along)
        ready = lax.optimization_barrier([along[way] for way in ways] + fresh)
        along = dict(zip(ways, ready))
        if stage == 2:
            padded = all_rows(ready[-1])
            pieces = line_pieces(padded)
        fresh, near = [], dict(along)
        if stage < stages:
            along = line_step(along, stage, depth)
        while len(theirs) < min(depth, stage + 1):
            mine.append(arrival(near, depth, line, len(theirs) - 1))
            theirs.append(pair_swap(mine[-1], depth))
            fresh.append(theirs[-1])
            if late:
                near.update(late)
                near = dict(zip(near, lax.optimization_barrier(list(near.values()))))
                along.update(late)
                late = {}
        fresh.append(pieces)
    pieces = exchange(pieces)
    same = fars_gather(pieces, chans)
    sources = turned(same, core_swap(same, chans))

    if part % 16:
        order = [(far - c // 2 + chans // 2) % (chans // 2) * 2 + (core + c) % 2 for c in range(chans)]
        split = [half.reshape((depth, 9, chans, part, -1)) for half in kernels]
        kernels = [jnp.take(half, jnp.stack(order), axis=2).reshape(kernels[0].shape) for half in split]

    outputs, came, at_next = None, [], after(at, kernels[0], pieces)
    for which in [*range(1, chans // 2), 0]:
        keep, send = forward_partial(depth, chans, which, at_next, weights, mine, theirs)
        at_next = after(at, send)
        moving = keep + core_swap(send, chans)
        if which:
            at_next = after(at_next, moving)
            moving = lax.ppermute(moving, "chan", [(c, (c + 2 * which) % chans) for c in range(chans)])
            came.append(moving)
        outputs = moving if outputs is None else outputs + moving
    outputs = outputs.astype(BF16)[None]

    input_grad = []
    for half in kernels:
        kept, sent = input_partial(chans, at_next, sources, half)
        at_next = after(at_next, sent, *came)
        input_grad.append((kept + pair_swap(sent, depth)).astype(BF16))
    at_next = after(at_next, *input_grad[:-1])
    input_grad = jnp.concatenate(input_grad, axis=2)[None]
    weight_grad = weight_gradient(depth, at_next, scale, padded, mine, theirs)
    weight_grad = weight_grad.reshape((3, 3, filters, chans_in))
    return (outputs, input_grad, weight_grad)


def solution(mesh):
    return jax.shard_map(
        body,
        mesh=mesh,
        in_specs=(
            P(None, "filt", None, "chan"),
            P(None, None, "filt", "chan"),
            P(None, "chan", "filt", None),
        ),
        out_specs=(
            P(None, "chan", "filt", None),
            P(None, "filt", None, "chan"),
            P(None, None, "filt", "chan"),
        ),
        check_vma=False,
    )
```

```python
import functools
import math

import jax
import jax.numpy as jnp
from jax import lax
from jax.experimental import pallas as pl
from jax.experimental.pallas import tpu as pltpu
from jax.sharding import PartitionSpec as P

F32 = jnp.float32
BF16 = jnp.bfloat16
NT = (((1,), (1,)), ((), ()))
HBM = pl.BlockSpec(memory_space=pltpu.HBM)
VMEM = pl.BlockSpec(memory_space=pltpu.VMEM)
SMEM = pl.BlockSpec(memory_space=pltpu.SMEM)
PAIR = 2


def params(mib):
    return pltpu.CompilerParams(vmem_limit_bytes=mib << 20)


def cost(flops, moved):
    return pl.CostEstimate(flops=int(flops), bytes_accessed=int(moved), transcendentals=0)


def lane_shift(value, by):
    size = value.shape[1]
    lane = lax.broadcasted_iota(jnp.int32, value.shape, 1)
    keep = lane >= by if by > 0 else lane < size + by
    return jnp.where(keep, pltpu.roll(value, by % size, 1), 0.0)


def after(value, *others):
    return lax.optimization_barrier((value,) + others)[0]


def arrivals(depth, line):
    ways = sorted((way for way in range(-line, depth - line) if way), key=abs)
    if abs(ways[-1]) == depth - 1:
        ways.insert(1, ways.pop())
    return ways


def arrival(along, depth, line, place):
    picked = None
    for z in range(depth):
        value = along[arrivals(depth, z)[place]]
        picked = value if picked is None or value is picked else jnp.where(line == z, value, picked)
    return picked


def load_rows(at, parts, rows, sems, first, last):
    height = parts[0][0].shape[0]

    def place(spot):
        return rows.at[pl.ds(1 + spot * height, height)]

    for half in range(PAIR):
        of_side = lax.rem(at[1] + half, PAIR)
        for index, part in enumerate(parts[half]):
            spot = at[4 + index] * PAIR + of_side

            @pl.when(jnp.logical_and(spot >= first, spot <= last))
            def _():
                pltpu.make_async_copy(part, place(spot), sems.at[spot]).start()

    rows[0] = jnp.zeros(rows.shape[1:], rows.dtype)
    rows[rows.shape[0] - 1] = jnp.zeros(rows.shape[1:], rows.dtype)
    return lambda spot: pltpu.make_async_copy(parts[0][0], place(spot), sems.at[spot]).wait()


def forward_kernel(depth, chans, which, at, weights, *refs):
    count = (len(refs) - 8) // 2
    parts = (refs[:count], refs[count : 2 * count])
    keep, send, rows, taps, made, sems, tap_sems, out_sems = refs[2 * count :]
    filters, chans_in = weights.shape[2], weights.shape[3]
    width = rows.shape[1]
    block = keep.shape[0]
    height = parts[0][0].shape[0]
    far, core = at[2], at[3]
    top = lax.rem(far + which, chans // 2) * 2 * block
    first, spots = top // height, max(1, 2 * block // height)
    wait = load_rows(at, parts, rows, sems, first - 1, first + spots)
    fetches = [
        pltpu.make_async_copy(
            weights.at[tap_row, tap_col],
            taps.at[pl.ds(tap_col * filters, filters), pl.ds(tap_row * chans_in, chans_in)],
            tap_sems.at[tap_row, tap_col],
        )
        for tap_row in range(3)
        for tap_col in range(3)
    ]
    for fetch in fetches:
        fetch.start()
    for fetch in fetches:
        fetch.wait()
    for spot in range(-1, spots + 1):

        @pl.when(jnp.logical_and(first + spot >= 0, first + spot < depth * PAIR))
        def _():
            wait(first + spot)

    group = min(8, block)

    def result(step, place):
        chosen = pl.ds(step * group, group)
        return pltpu.make_async_copy(made.at[place, chosen], (send, keep)[place].at[chosen], out_sems.at[place, step])

    @pl.loop(0, block // group)
    def _(step):
        for place, of_core in enumerate((1 - core, core)):
            start = top + of_core * block + step * group
            window = jnp.concatenate(
                [rows[pl.ds(start + i, group)].reshape(group * width, chans_in) for i in range(3)], axis=1
            )
            product = lax.dot_general(taps[...], window, NT, preferred_element_type=F32)
            for row in range(group):
                part = [
                    product[j * filters : (j + 1) * filters, row * width : (row + 1) * width] for j in range(3)
                ]
                made[place, step * group + row] = part[1] + lane_shift(part[0], 1) + lane_shift(part[2], -1)
            result(step, place).start()

    for step in range(block // group):
        for place in range(2):
            result(step, place).wait()


def forward_partial(depth, chans, which, at, weights, own, other):
    height, width, chans_in = own[0].shape
    filters = weights.shape[2]
    rows = height * depth * PAIR
    half = jax.ShapeDtypeStruct((rows // chans, filters, width), F32)
    return pl.pallas_call(
        functools.partial(forward_kernel, depth, chans, which),
        out_shape=(half, half),
        in_specs=[SMEM, HBM] + [HBM] * (len(own) + len(other)),
        out_specs=(HBM, HBM),
        scratch_shapes=[
            pltpu.VMEM((rows + 2, width, chans_in), BF16),
            pltpu.VMEM((3 * filters, 3 * chans_in), BF16),
            pltpu.VMEM((2, rows // chans, filters, width), F32),
            pltpu.SemaphoreType.DMA((depth * PAIR,)),
            pltpu.SemaphoreType.DMA((3, 3)),
            pltpu.SemaphoreType.DMA((2, rows // chans // min(8, rows // chans))),
        ],
        compiler_params=params(58),
        cost_estimate=cost(
            36 * rows // chans * width * chans_in * filters, 8 * rows // chans * width * (filters + chans_in)
        ),
        name="forward",
    )(at, weights, *own, *other)


def weight_kernel(depth, scale, at, cot, *refs):
    count = (len(refs) - 7) // 2
    parts = (refs[:count], refs[count : 2 * count])
    out, rows, cots, moved, total, sems, cot_sems = refs[2 * count :]
    wait = load_rows(at, parts, rows, sems, 0, depth * PAIR - 1)
    filters, width = cot.shape[1], cot.shape[2]
    chans_in = rows.shape[2]
    height = parts[0][0].shape[0]
    steps, chunk = cots.shape[0], cots.shape[1]

    def fetch(step):
        return pltpu.make_async_copy(cot.at[pl.ds(1 + step * chunk, chunk)], cots.at[step], cot_sems.at[step])

    for step in range(steps):
        fetch(step).start()
    total[...] = jnp.zeros(total.shape, F32)
    wait(0)

    @pl.loop(0, steps)
    def _(step):
        first = step * chunk
        fetch(step).wait()
        for spot in range(max(1, chunk // height)):
            after_it = first // height + spot + 1

            @pl.when(after_it < depth * PAIR)
            def _():
                wait(after_it)

        for row in range(chunk):
            value = cots[step, row]
            wide = value.astype(F32)
            lanes = pl.ds(row * width, width)
            moved[0:filters, lanes] = lane_shift(wide, -1).astype(BF16)
            moved[filters : 2 * filters, lanes] = value
            moved[2 * filters :, lanes] = lane_shift(wide, 1).astype(BF16)
        for tap_row in range(3):
            window = rows[pl.ds(first + tap_row, chunk)].reshape(chunk * width, chans_in)
            total[tap_row] += jnp.dot(moved[...], window, preferred_element_type=F32)

    stores = []
    for tap_row in range(3):
        total[tap_row] = total[tap_row] * scale
        for tap_col in range(3):
            chosen = (tap_row, pl.ds(tap_col * filters, filters))
            stores.append(pltpu.make_async_copy(total.at[chosen], out.at[chosen], cot_sems.at[steps + 3 * tap_row + tap_col]))
            stores[-1].start()
    for store in stores:
        store.wait()


def weight_gradient(depth, at, scale, cot, own, other):
    height, width, chans_in = own[0].shape
    rows, filters = cot.shape[0] - 2, cot.shape[1]
    chunk = max(height, min(8, rows))
    return pl.pallas_call(
        functools.partial(weight_kernel, depth, scale),
        out_shape=jax.ShapeDtypeStruct((3, 3 * filters, chans_in), F32),
        in_specs=[SMEM, HBM] + [HBM] * (len(own) + len(other)),
        out_specs=HBM,
        scratch_shapes=[
            pltpu.VMEM((rows + 2, width, chans_in), BF16),
            pltpu.VMEM((rows // chunk, chunk, filters, width), BF16),
            pltpu.VMEM((3 * filters, chunk * width), BF16),
            pltpu.VMEM((3, 3 * filters, chans_in), F32),
            pltpu.SemaphoreType.DMA((depth * PAIR,)),
            pltpu.SemaphoreType.DMA((rows // chunk + 9,)),
        ],
        compiler_params=params(58),
        cost_estimate=cost(18 * rows * width * chans_in * filters, 2 * rows * width * (filters + chans_in)),
        name="weight_gradient",
    )(at, cot, *own, *other)


def turn_kernel(same, cross, out):
    fars, _, rows = same.shape[:3]
    unroll = max(n for n in (1, 2, 3, 6) if rows % n == 0)

    @pl.loop(0, rows // unroll)
    def _(step):
        for n in range(unroll):
            row = step * unroll + n
            out[0, row] = jnp.concatenate([part[far, 0, row] for far in range(fars) for part in (same, cross)], axis=0).T


def turned(same, cross):
    fars, depth, rows, part, width = same.shape
    filters = 2 * fars * part
    spec = pl.BlockSpec((fars, 1, rows, part, width), lambda d: (0, d, 0, 0, 0))
    return pl.pallas_call(
        turn_kernel,
        grid=(depth,),
        out_shape=jax.ShapeDtypeStruct((depth, rows, width, filters), BF16),
        in_specs=[spec, spec],
        out_specs=pl.BlockSpec((1, rows, width, filters), lambda d: (d, 0, 0, 0)),
        compiler_params=params(58),
        cost_estimate=cost(0, 4 * depth * rows * width * filters),
        name="turned",
    )(same, cross)


def input_kernel(chans, at, cot, kernels, keep, send, source, taps, stacked, made, sems, out_sems):
    side, far, core = at[1], at[2], at[3]
    depth, rows, width, filters = source.shape
    rows = rows - 2
    chans_in = taps.shape[3]
    copies = []
    for n in range(depth):
        copies.append(
            (
                pltpu.make_async_copy(kernels.at[n], taps.at[n], sems.at[n, 0]),
                [
                    pltpu.make_async_copy(
                        cot.at[n, pl.ds(first, (rows + 2) // 2)],
                        source.at[n, pl.ds(first, (rows + 2) // 2)],
                        sems.at[n, 1 + (first > 0)],
                    )
                    for first in (0, (rows + 2) // 2)
                ],
            )
        )
        copies[n][0].start()
    for n in range(depth):
        for copy in copies[n][1]:
            copy.start()
    part = filters // chans
    places = chans if part % 16 == 0 else 1
    size = filters // places
    for n in range(depth):
        copies[n][0].wait()
        for place in range(places):
            chan = lax.rem(far - place // 2 + chans // 2, chans // 2) * 2 + lax.rem(core + place, 2)
            of_chan = pl.ds(0 if places == 1 else pl.multiple_of(chan * size, size), size)
            for i in range(3):
                for j in range(3):
                    stacked[
                        pl.ds((n * 3 + i) * filters + place * size, size), pl.ds(j * chans_in, chans_in)
                    ] = taps[n, 3 * i + j, of_chan]
    for n in range(depth):
        for copy in copies[n][1]:
            copy.wait()
    half = rows // PAIR
    chunk = min(8, half)
    lanes = lax.broadcasted_iota(jnp.int32, (width, chans_in), 0)

    def result(place, step):
        chosen = pl.ds(step * chunk, chunk)
        return pltpu.make_async_copy(made.at[place, chosen], (send, keep)[place].at[chosen], out_sems.at[place, step])

    for place, of_side in enumerate((1 - side, side)):
        for step in range(half // chunk):
            first = of_side * half + step * chunk
            window = [
                source[n, pl.ds(first + 2 - i, chunk)].reshape(chunk * width, filters)
                for n in range(depth)
                for i in range(3)
            ]
            if filters % 128 == 0:
                product = jnp.dot(jnp.concatenate(window, axis=1), stacked[...], preferred_element_type=F32)
            else:
                product = sum(
                    jnp.dot(value, stacked[n * filters : (n + 1) * filters], preferred_element_type=F32)
                    for n, value in enumerate(window)
                )
            for row in range(chunk):
                here = [
                    product[row * width : (row + 1) * width, j * chans_in : (j + 1) * chans_in] for j in range(3)
                ]
                before_it = jnp.where(lanes < width - 1, pltpu.roll(here[0], width - 1, 0), 0.0)
                behind_it = jnp.where(lanes >= 1, pltpu.roll(here[2], 1, 0), 0.0)
                made[place, step * chunk + row] = here[1] + before_it + behind_it
            result(place, step).start()

    for place in range(2):
        for step in range(half // chunk):
            result(place, step).wait()


def input_partial(chans, at, cot, kernels):
    depth, rows, width, filters = cot.shape
    rows = rows - 2
    chans_in = kernels.shape[3]
    half = jax.ShapeDtypeStruct((rows // PAIR, width, chans_in), F32)
    return pl.pallas_call(
        functools.partial(input_kernel, chans),
        out_shape=(half, half),
        in_specs=[SMEM, HBM, HBM],
        out_specs=(HBM, HBM),
        scratch_shapes=[
            pltpu.VMEM(cot.shape, BF16),
            pltpu.VMEM(kernels.shape, BF16),
            pltpu.VMEM((depth * 3 * filters, 3 * chans_in), BF16),
            pltpu.VMEM((PAIR, rows // PAIR, width, chans_in), F32),
            pltpu.SemaphoreType.DMA((depth, 3)),
            pltpu.SemaphoreType.DMA((PAIR, rows // PAIR // min(8, rows // PAIR))),
        ],
        compiler_params=params(58),
        cost_estimate=cost(
            18 * rows * width * chans_in * filters * depth, 2 * depth * filters * ((rows + 2) * width + 9 * chans_in)
        ),
        name="input_gradient",
    )(at, cot, kernels)


def fars_gather(value, chans):
    got = [value]
    for step in range(1, chans // 2):
        got.append(lax.ppermute(value, "chan", [(c, (c + 2 * step) % chans) for c in range(chans)]))
    return jnp.stack(got)


def lines(depth):
    return [[z * PAIR + y for z in range(depth)] for y in range(PAIR)]


def line_step(along, step, depth):
    up = [(z * PAIR + y, (z + 1) * PAIR + y) for z in range(step - 1, depth - 1) for y in range(PAIR)]
    down = [(z * PAIR + y, (z - 1) * PAIR + y) for z in range(1, depth - step + 1) for y in range(PAIR)]
    along = dict(along)
    along[-step] = lax.ppermute(along[1 - step], "filt", up)
    along[step] = lax.ppermute(along[step - 1], "filt", down)
    if step == 1 and depth > 2:
        ends = (0, depth - 1)
        across = [(z * PAIR + y, (depth - 1 - z) * PAIR + y) for z in ends for y in range(PAIR)]
        along[depth - 1] = along[1 - depth] = lax.ppermute(along[0], "filt", across)
    return along


def core_swap(value, chans):
    return lax.ppermute(value, "chan", [(c, c ^ 1) for c in range(chans)])


def pair_swap(value, depth):
    pairs = [(z * PAIR + y, z * PAIR + 1 - y) for z in range(depth) for y in range(PAIR)]
    return lax.ppermute(value, "filt", pairs)


def body(inputs, weights, cotangent):
    chans, filts = lax.axis_size("chan"), lax.axis_size("filt")
    depth = filts // PAIR
    chan, filt = lax.axis_index("chan"), lax.axis_index("filt")
    line, side = filt // PAIR, filt % PAIR
    far, core = chan // 2, chan % 2
    spots = jnp.asarray([[z] + [z + way for way in arrivals(depth, z)] for z in range(depth)], jnp.int32)
    at = jnp.concatenate([jnp.stack([line, side, far, core]).astype(jnp.int32), spots[line]])
    own_rows, width, chans_in = inputs.shape[1:]
    block, filters = cotangent.shape[1], cotangent.shape[2]
    height = own_rows * filts
    scale = 1.0 / math.sqrt(inputs.shape[0] * height * width)

    part = filters // chans
    line_rows = own_rows * PAIR

    def all_rows(same):
        cross = core_swap(same, chans)
        padded = jnp.zeros((height + 2, filters, width), BF16)
        for step in range(chans // 2):
            at_far = lax.rem(far - step + chans // 2, chans // 2) * 2
            padded = lax.dynamic_update_slice(padded, same[step], (1 + (at_far + core) * block, 0, 0))
            padded = lax.dynamic_update_slice(padded, cross[step], (1 + (at_far + 1 - core) * block, 0, 0))
        return padded

    def line_pieces(padded):
        own_part = lax.dynamic_slice_in_dim(padded, chan * part, part, axis=1)
        return jnp.stack([own_part[z * line_rows : (z + 1) * line_rows + 2] for z in range(depth)])

    def exchange(pieces):
        return lax.all_to_all(pieces, "filt", 0, 0, axis_index_groups=lines(depth), tiled=True)

    halves = PAIR if chans_in % (PAIR * 128) == 0 else 1
    kernels = []
    for half in jnp.split(weights, halves, axis=3):
        half = half.reshape((9,) + half.shape[2:])
        kernels.append(lax.all_gather(half, "filt", axis=0, axis_index_groups=lines(depth)))

    mine, theirs = [inputs[0]], [pair_swap(inputs[0], depth)]
    same = fars_gather(cotangent[0], chans)
    along = line_step({0: inputs[0]}, 1, depth)
    fresh = theirs + [same]
    stages = max(2, depth - 1)
    for stage in range(2, stages + 1):
        ways = list(along)
        ready = lax.optimization_barrier([along[way] for way in ways] + fresh)
        along = dict(zip(ways, ready))
        if stage == 2:
            padded = all_rows(ready[-1])
            pieces = line_pieces(padded)
        fresh = []
        if stage < stages:
            along = line_step(along, stage, depth)
        while len(theirs) < min(depth, stage + 1):
            mine.append(arrival(along, depth, line, len(theirs) - 1))
            theirs.append(pair_swap(mine[-1], depth))
            fresh.append(theirs[-1])
        fresh.append(pieces)
    pieces = exchange(pieces)
    same = fars_gather(pieces, chans)
    sources = turned(same, core_swap(same, chans))

    if part % 16:
        order = [(far - c // 2 + chans // 2) % (chans // 2) * 2 + (core + c) % 2 for c in range(chans)]
        split = [half.reshape((depth, 9, chans, part, -1)) for half in kernels]
        kernels = [jnp.take(half, jnp.stack(order), axis=2).reshape(kernels[0].shape) for half in split]

    outputs, came, at_next = None, [], after(at, kernels[0], pieces)
    for which in [*range(1, chans // 2), 0]:
        keep, send = forward_partial(depth, chans, which, at_next, weights, mine, theirs)
        at_next = after(at, send)
        moving = keep + core_swap(after(send, same), chans)
        if which:
            at_next = after(at_next, moving)
            moving = lax.ppermute(moving, "chan", [(c, (c + 2 * which) % chans) for c in range(chans)])
            came.append(moving)
        outputs = moving if outputs is None else outputs + moving
    outputs = outputs.astype(BF16)[None]

    input_grad = []
    for half in kernels:
        kept, sent = input_partial(chans, at_next, sources, half)
        at_next = after(at_next, sent, *came)
        input_grad.append((kept + pair_swap(sent, depth)).astype(BF16))
    at_next = after(at_next, *input_grad[:-1])
    input_grad = jnp.concatenate(input_grad, axis=2)[None]
    weight_grad = weight_gradient(depth, at_next, scale, padded, mine, theirs)
    weight_grad = weight_grad.reshape((3, 3, filters, chans_in))
    return (outputs, input_grad, weight_grad)


def solution(mesh):
    return jax.shard_map(
        body,
        mesh=mesh,
        in_specs=(
            P(None, "filt", None, "chan"),
            P(None, None, "filt", "chan"),
            P(None, "chan", "filt", None),
        ),
        out_specs=(
            P(None, "chan", "filt", None),
            P(None, "filt", None, "chan"),
            P(None, None, "filt", "chan"),
        ),
        check_vma=False,
    )
```
